128 devices in a mesh: ctx: 64 (over y, x, z_lo, core), head: 2 (over z_hi).
Axes of the slice: x: 4, y: 4, z: 4 (z_hi: 2, z_lo: 2; z = z_hi * 2 + z_lo), core: 2. Of those that a mesh axis runs over, the one named last changes fastest.
Arguments:
- queries: bfloat16 [16384, 4096], P(('ctx', 'head')), may hold values from -80 to 80
- input_key_rows: bfloat16 [16384, 1024], P(('ctx', 'head')), may hold values from -4 to 4
- input_value_rows: bfloat16 [16384, 1024], P(('ctx', 'head')), may hold values from -6 to 6
- attention_output_gradient: bfloat16 [16384, 4096], P(('ctx', 'head')), may hold values from -6 to 6
- level_offsets: int32 [5, 8], P(None, 'head'), may hold values from 0 to 15, as said below
Outputs:
- attended: bfloat16 [16384, 4096], P(('ctx', 'head'))
- grad_queries: bfloat16 [16384, 4096], P(('ctx', 'head'))
- grad_keys: bfloat16 [16384, 1024], P(('ctx', 'head'))
- grad_values: bfloat16 [16384, 1024], P(('ctx', 'head'))
The draws below stay inside these ranges and needn't reach their ends.
Inputs may be any that keep to these rules, and one draw needn't show every extreme that they name: level_offsets[k, g] lies in 0 .. 2^k - 1.
All inputs are finite; a program needn't handle non-finite values.
Results may differ from the reference program's by a relative error of at most 0.018.
Values may be sent and summed in bfloat16 or wider, within the bound.
No kernel may reach another device: no remote copies, remote signals or barrier semaphores. Data moves between devices by JAX's collectives and lax.ppermute only.
A program may use at most 128 MiB of HBM per device.

```python
import jax
import jax.numpy as jnp
from jax import lax

QUERY_HEADS = 32
KEY_VALUE_HEADS = 8
HEAD_DIMENSION = 128
DILATION_LEVELS = 5
TOKENS_PER_SHARD = 256
SEQUENCE_TOKENS = 16384
N_CTX = 64


def drawn_rows(key):
    primary_baseline = jnp.clip(jax.random.normal(jax.random.fold_in(key, 21), (SEQUENCE_TOKENS, KEY_VALUE_HEADS, HEAD_DIMENSION), jnp.float32), -4.0, 4.0)
    return primary_baseline


def draw_input_key_rows(key, part):
    primary_baseline = drawn_rows(key)
    return primary_baseline.reshape(SEQUENCE_TOKENS, KEY_VALUE_HEADS * HEAD_DIMENSION).astype(jnp.bfloat16)


def draw_queries(key, part):
    key = jax.random.fold_in(key, 7)
    newly_drawn = jnp.clip(2.0 * jax.random.normal(key, (SEQUENCE_TOKENS, KEY_VALUE_HEADS, QUERY_HEADS // KEY_VALUE_HEADS, HEAD_DIMENSION), jnp.float32), -8.0, 8.0)
    return newly_drawn.reshape(SEQUENCE_TOKENS, QUERY_HEADS * HEAD_DIMENSION).astype(jnp.bfloat16)


def draw_level_offsets(key, part):
    key = jax.random.fold_in(key, 3)
    spans = 2 ** jnp.arange(DILATION_LEVELS, dtype=jnp.int32)
    unscaled_values = jax.random.randint(key, (DILATION_LEVELS, KEY_VALUE_HEADS), 0, 1 << 30)
    offsets_drawn = unscaled_values % spans[:, None]
    highest_head = jax.random.randint(jax.random.fold_in(key, 1), (), 0, KEY_VALUE_HEADS)
    required_rows = (jnp.arange(DILATION_LEVELS)[:, None] == DILATION_LEVELS - 1) & (jnp.arange(KEY_VALUE_HEADS)[None, :] == highest_head)
    return jnp.where(required_rows, spans[DILATION_LEVELS - 1] - 1, offsets_drawn).astype(jnp.int32)


def level_of(own_key, extent, cuts, least, top_value):
    loudness, own = 1.0, jax.random.fold_in(own_key, 6)
    for axis_at, shards_of in cuts:
        steps = jnp.exp(jax.random.uniform(jax.random.fold_in(own, axis_at), (shards_of,), jnp.float32, least / len(cuts), top_value / len(cuts)))
        loudness = loudness * jnp.repeat(steps, extent[axis_at] // shards_of).reshape([-1 if axis == axis_at else 1 for axis in range(len(extent))])
    return loudness


def scatter_about(own_key, extent, deviation, most, split=(), kind=jnp.bfloat16):
    values = deviation * jax.random.normal(own_key, extent, jnp.float32)
    if split:
        values = values * level_of(own_key, extent, split, -0.22, 0.18)
    return jnp.clip(values, -most, most).astype(kind)


def setup_inputs(seed: int = 0) -> dict:
    key_list = jax.random.split(jax.random.key(seed), 6)
    queries = draw_queries(jax.random.fold_in(key_list[5], 71), 0)
    input_key_rows = draw_input_key_rows(jax.random.fold_in(key_list[5], 71), 0)
    input_value_rows = scatter_about(key_list[2], (SEQUENCE_TOKENS, KEY_VALUE_HEADS * HEAD_DIMENSION), 1.0, 6.0, ((0, 128),))
    attention_output_gradient = scatter_about(key_list[3], (SEQUENCE_TOKENS, QUERY_HEADS * HEAD_DIMENSION), 1.0, 6.0, ((0, 128),))
    level_offsets = draw_level_offsets(jax.random.fold_in(key_list[5], 71), 0)
    return {"queries": queries, "input_key_rows": input_key_rows, "input_value_rows": input_value_rows, "attention_output_gradient": attention_output_gradient, "level_offsets": level_offsets}


def to_bfloat(source):
    return lax.optimization_barrier(source.astype(jnp.bfloat16)).astype(jnp.float32)


def select_rows(source, selected_rows_set, dilation_step):
    kept_count = source.shape[0] // dilation_step
    shaped = source.reshape((kept_count, dilation_step) + source.shape[1:])
    take_index = selected_rows_set.astype(jnp.int32).reshape((1, 1, -1) + (1,) * (source.ndim - 2))
    take_index = jnp.broadcast_to(take_index, (kept_count, 1) + source.shape[1:])
    return jnp.take_along_axis(shaped, take_index, axis=1)[:, 0]


def scatter_rows(source, selected_rows_set, dilation_step):
    member = jnp.arange(dilation_step, dtype=jnp.int32)[:, None] == selected_rows_set.astype(jnp.int32)[None, :]
    member = member.reshape((1, dilation_step, source.shape[1]) + (1,) * (source.ndim - 2))
    placed = jnp.where(member, source[:, None], jnp.zeros((), source.dtype))
    return placed.reshape((source.shape[0] * dilation_step,) + source.shape[1:])


def merge_levels(complete_logsumexp, group_members):
    peak = complete_logsumexp[0]
    for lse_one, member in zip(complete_logsumexp[1:], group_members[1:]):
        peak = jnp.maximum(peak, jnp.where(member, lse_one, complete_logsumexp[0]))
    row_total = jnp.zeros_like(peak)
    for lse_one, member in zip(complete_logsumexp, group_members):
        row_total = row_total + jnp.where(member, jnp.exp(lse_one - peak), 0.0)
    return peak + jnp.log(row_total)


def segment_forward(segment_data):
    segment_query_rows, segment_key_rows, segment_value_rows = segment_data
    scores = jnp.einsum("rghd,kgd->ghrk", segment_query_rows.astype(jnp.float32), segment_key_rows.astype(jnp.float32)) * HEAD_DIMENSION ** -0.5
    row_peak = jnp.max(scores, -1, keepdims=True)
    raised = jnp.exp(scores - row_peak)
    row_total = jnp.sum(raised, -1, keepdims=True)
    weights = to_bfloat(raised / row_total)
    level_output = jnp.einsum("ghrk,kgd->rghd", weights, segment_value_rows.astype(jnp.float32))
    level_logsumexp = jnp.transpose((row_peak + jnp.log(row_total))[..., 0], (2, 0, 1))
    return level_output, level_logsumexp


def segment_backward(segment_data):
    segment_query_rows, segment_gradients, segment_logsumexp, segment_correction, segment_key_rows, segment_value_rows = segment_data
    query_full = segment_query_rows.astype(jnp.float32)
    key_full = segment_key_rows.astype(jnp.float32)
    grad_full = segment_gradients.astype(jnp.float32)
    scores = jnp.einsum("rghd,kgd->ghrk", query_full, key_full) * HEAD_DIMENSION ** -0.5
    probs = jnp.exp(scores - jnp.transpose(segment_logsumexp, (1, 2, 0))[..., None])
    grad_values = jnp.einsum("ghrk,rghd->kgd", to_bfloat(probs), grad_full)
    grad_weights = jnp.einsum("rghd,kgd->ghrk", grad_full, segment_value_rows.astype(jnp.float32))
    grad_scores = to_bfloat(probs * (grad_weights - jnp.transpose(segment_correction, (1, 2, 0))[..., None]))
    grad_queries = HEAD_DIMENSION ** -0.5 * jnp.einsum("ghrk,kgd->rghd", grad_scores, key_full)
    grad_keys = HEAD_DIMENSION ** -0.5 * jnp.einsum("ghrk,rghd->kgd", grad_scores, query_full)
    return grad_queries, grad_keys, grad_values


def reference(queries, input_key_rows, input_value_rows, attention_output_gradient, level_offsets):
    token_positions = queries.shape[0]
    heads_per_group = QUERY_HEADS // KEY_VALUE_HEADS
    query_tensor = queries.reshape(token_positions, KEY_VALUE_HEADS, heads_per_group, HEAD_DIMENSION)
    key_tensor = input_key_rows.reshape(token_positions, KEY_VALUE_HEADS, HEAD_DIMENSION)
    value_tensor = input_value_rows.reshape(token_positions, KEY_VALUE_HEADS, HEAD_DIMENSION)
    gradient_tensor = attention_output_gradient.reshape(token_positions, KEY_VALUE_HEADS, heads_per_group, HEAD_DIMENSION)
    group_members = []
    complete_logsumexp = []
    level_outputs = []
    for level_k in range(DILATION_LEVELS):
        dilation_step = 2 ** level_k
        segment_list = N_CTX // dilation_step
        selected_rows_set = level_offsets[level_k]
        segment_query_rows = select_rows(query_tensor, selected_rows_set, dilation_step).reshape(segment_list, TOKENS_PER_SHARD, KEY_VALUE_HEADS, heads_per_group, HEAD_DIMENSION)
        segment_key_rows = select_rows(key_tensor, selected_rows_set, dilation_step).reshape(segment_list, TOKENS_PER_SHARD, KEY_VALUE_HEADS, HEAD_DIMENSION)
        segment_value_rows = select_rows(value_tensor, selected_rows_set, dilation_step).reshape(segment_list, TOKENS_PER_SHARD, KEY_VALUE_HEADS, HEAD_DIMENSION)
        level_output, level_logsumexp = lax.map(segment_forward, (segment_query_rows, segment_key_rows, segment_value_rows))
        level_outputs.append(level_output.reshape(token_positions // dilation_step, KEY_VALUE_HEADS, heads_per_group, HEAD_DIMENSION))
        complete_logsumexp.append(scatter_rows(level_logsumexp.reshape(token_positions // dilation_step, KEY_VALUE_HEADS, heads_per_group), selected_rows_set, dilation_step))
        group_members.append(scatter_rows(jnp.ones((token_positions // dilation_step, KEY_VALUE_HEADS, 1), jnp.float32), selected_rows_set, dilation_step) > 0.5)
    combined_logsumexp = merge_levels(complete_logsumexp, group_members)
    attended = jnp.zeros((token_positions, KEY_VALUE_HEADS, heads_per_group, HEAD_DIMENSION), jnp.float32)
    for level_k in range(DILATION_LEVELS):
        share = jnp.where(group_members[level_k], jnp.exp(complete_logsumexp[level_k] - combined_logsumexp), 0.0)
        attended = attended + share[..., None] * scatter_rows(level_outputs[level_k], level_offsets[level_k], 2 ** level_k)
    attended_low = attended.astype(jnp.bfloat16)
    row_correction = jnp.sum(gradient_tensor.astype(jnp.float32) * attended_low.astype(jnp.float32), -1)
    query_gradient = jnp.zeros((token_positions, KEY_VALUE_HEADS, heads_per_group, HEAD_DIMENSION), jnp.float32)
    key_gradient = jnp.zeros((token_positions, KEY_VALUE_HEADS, HEAD_DIMENSION), jnp.float32)
    value_gradient = jnp.zeros((token_positions, KEY_VALUE_HEADS, HEAD_DIMENSION), jnp.float32)
    for level_k in range(DILATION_LEVELS):
        dilation_step = 2 ** level_k
        segment_list = N_CTX // dilation_step
        selected_rows_set = level_offsets[level_k]
        segment_query_rows = select_rows(query_tensor, selected_rows_set, dilation_step).reshape(segment_list, TOKENS_PER_SHARD, KEY_VALUE_HEADS, heads_per_group, HEAD_DIMENSION)
        segment_gradients = select_rows(gradient_tensor, selected_rows_set, dilation_step).reshape(segment_list, TOKENS_PER_SHARD, KEY_VALUE_HEADS, heads_per_group, HEAD_DIMENSION)
        segment_logsumexp = select_rows(combined_logsumexp, selected_rows_set, dilation_step).reshape(segment_list, TOKENS_PER_SHARD, KEY_VALUE_HEADS, heads_per_group)
        segment_correction = select_rows(row_correction, selected_rows_set, dilation_step).reshape(segment_list, TOKENS_PER_SHARD, KEY_VALUE_HEADS, heads_per_group)
        segment_key_rows = select_rows(key_tensor, selected_rows_set, dilation_step).reshape(segment_list, TOKENS_PER_SHARD, KEY_VALUE_HEADS, HEAD_DIMENSION)
        segment_value_rows = select_rows(value_tensor, selected_rows_set, dilation_step).reshape(segment_list, TOKENS_PER_SHARD, KEY_VALUE_HEADS, HEAD_DIMENSION)
        partial_queries, partial_keys, partial_values = lax.map(segment_backward, (segment_query_rows, segment_gradients, segment_logsumexp, segment_correction, segment_key_rows, segment_value_rows))
        query_gradient = query_gradient + scatter_rows(partial_queries.reshape(token_positions // dilation_step, KEY_VALUE_HEADS, heads_per_group, HEAD_DIMENSION), selected_rows_set, dilation_step)
        key_gradient = key_gradient + scatter_rows(partial_keys.reshape(token_positions // dilation_step, KEY_VALUE_HEADS, HEAD_DIMENSION), selected_rows_set, dilation_step)
        value_gradient = value_gradient + scatter_rows(partial_values.reshape(token_positions // dilation_step, KEY_VALUE_HEADS, HEAD_DIMENSION), selected_rows_set, dilation_step)
    return (attended_low.reshape(token_positions, QUERY_HEADS * HEAD_DIMENSION),
            query_gradient.astype(jnp.bfloat16).reshape(token_positions, QUERY_HEADS * HEAD_DIMENSION),
            key_gradient.astype(jnp.bfloat16).reshape(token_positions, KEY_VALUE_HEADS * HEAD_DIMENSION),
            value_gradient.astype(jnp.bfloat16).reshape(token_positions, KEY_VALUE_HEADS * HEAD_DIMENSION))
```

```python
import functools

import jax
import jax.numpy as jnp
from jax import lax
from jax.experimental import pallas as pl
from jax.experimental.pallas import tpu as pltpu
from jax.sharding import PartitionSpec as P

D = 128
GROUPS = 8
HEADS = 4
TOKENS = 128
WIDE = HEADS * D
SCALE = D ** (-0.5)
LOG2E = 1.4426950408889634
AXES = ("ctx", "head")
BF = jnp.bfloat16
F32 = jnp.float32
ANY_ROWS = ((0, 64, 1), (64, 96, 2), (96, 112, 3), (112, 120, 4))
VMEM_LIMIT = 56 * 1024 * 1024


def dot(a, b):
    return lax.dot_general(a, b, (((1,), (0,)), ((), ())), preferred_element_type=F32)


def dot_nt(a, b):
    return lax.dot_general(a, b, (((1,), (1,)), ((), ())), preferred_element_type=F32)


def one_hot(mask):
    return jnp.where(mask, 1.0, 0.0).astype(BF)


def selected_token(row, offs, group):
    token = jnp.full(row.shape, -1, jnp.int32)
    for start, stop, level in ANY_ROWS:
        inside = (row >= start) & (row < stop)
        token = jnp.where(inside, (row - start) * 2**level + offs[level, group], token)
    return token


def selector(offs, group):
    shape = (128, TOKENS)
    row = lax.broadcasted_iota(jnp.int32, shape, 0)
    return one_hot(selected_token(row, offs, group) == lax.broadcasted_iota(jnp.int32, shape, 1))


def placer(offs, group):
    shape = (TOKENS, 128)
    row = lax.broadcasted_iota(jnp.int32, shape, 1)
    return one_hot(selected_token(row, offs, group) == lax.broadcasted_iota(jnp.int32, shape, 0))


def group_rows(keys_ref, values_ref, group):
    lanes = slice(group * D, (group + 1) * D)
    return jnp.concatenate([keys_ref[:, lanes], values_ref[:, lanes]], 1)


def select_kernel(offs, keys, values, first, middle, tail, last):
    for g in range(GROUPS):
        rows = dot(selector(offs, g), group_rows(keys, values, g))
        first[g] = rows[0:64].astype(BF)
        middle[g] = rows[64:128].astype(BF)
        tail[g] = rows[96:128].astype(BF)
        last[g] = rows[112:128].astype(BF)


def compact_kernel(one, two, three, packed):
    for g in range(GROUPS):
        a, b, c = one[g].astype(F32), two[g].astype(F32), three[g].astype(F32)
        packed[g] = jnp.concatenate([a[:24], b[:8], c[:8], jnp.zeros((8, 2 * D), F32)], 0).astype(BF)


def assemble_kernel(
    offs, first, mid_own, x_own, keys, values, x_far, mid_up, x_up, mid_down, x_down, held
):
    for g in range(GROUPS):
        far = dot(selector(offs, g), group_rows(keys, values, g))
        mids = [mid_own[g].astype(F32), far[64:128], mid_up[g].astype(F32), mid_down[g].astype(F32)]
        extras = [ref[g].astype(F32) for ref in (x_own, x_far, x_up, x_down)]
        rows = [first[g].astype(F32), far[0:64]]
        rows += [m[0:32] for m in mids]
        for m, x in zip(mids, extras):
            rows += [m[32:48], x[0:16]]
        for m, x in zip(mids, extras):
            rows += [m[48:56], x[16:40]]
        held[g] = jnp.concatenate(rows, 0).astype(BF)


def by_level(rows):
    parts = []
    for start, stop in ((0, 64), (64, 96), (96, 112), (112, 120), (120, 128)):
        parts += [rows[start:stop, h * D : (h + 1) * D] for h in range(HEADS)]
    return jnp.concatenate(parts, 0)


def by_selection(rows):
    heads = []
    for h in range(HEADS):
        parts = []
        base = 0
        for count in (64, 32, 16, 8, 8):
            parts.append(rows[base + h * count : base + (h + 1) * count])
            base += HEADS * count
        heads.append(jnp.concatenate(parts, 0))
    return jnp.concatenate(heads, 1)


def split3(x):
    high = x.astype(BF)
    rest = x - high.astype(F32)
    mid = rest.astype(BF)
    low = (rest - mid.astype(F32)).astype(BF)
    return [high.astype(F32), mid.astype(F32), low.astype(F32)]


def attention_kernel(
    offs, q_ref, g_ref, k_ref, v_ref, kp_ref, vp_ref, own_ref, other_ref,
    att_ref, dq_ref, d0_ref, down_ref, dother_ref,
):
    group = pl.program_id(0)
    eye = one_hot(
        lax.broadcasted_iota(jnp.int32, (D, D), 0) == lax.broadcasted_iota(jnp.int32, (D, D), 1)
    )
    pick = selector(offs, group)
    place = placer(offs, group)
    q_rows = q_ref[...]
    g_rows = g_ref[...]
    q0 = jnp.concatenate([q_rows[:, h * D : (h + 1) * D] for h in range(HEADS)], 0)
    g0 = jnp.concatenate([g_rows[:, h * D : (h + 1) * D] for h in range(HEADS)], 0)
    qs = by_level(dot(pick, q_rows)).astype(BF)
    gs = by_level(dot(pick, g_rows)).astype(BF)

    shape = (512, WIDE)
    row = lax.broadcasted_iota(jnp.int32, shape, 0)
    target = jnp.full(shape, -1, jnp.int32)
    base = 0
    for count, level in ((64, 1), (32, 2), (16, 3), (8, 4)):
        r = row - base
        shift = count.bit_length() - 1
        value = (r >> shift) * TOKENS + (r & (count - 1)) * 2**level + offs[level, group]
        target = jnp.where((r >= 0) & (r < HEADS * count), value, target)
        base += HEADS * count
    spread = one_hot(target == lax.broadcasted_iota(jnp.int32, shape, 1))

    own = own_ref[0]
    other = other_ref[0]

    def both(start, lanes):
        return [own[start : start + 128, lanes], other[start : start + 128, lanes]]

    k_lanes, v_lanes = slice(0, D), slice(D, 2 * D)
    keys = [
        jnp.concatenate([k_ref[...], kp_ref[...]], 0),
        jnp.concatenate(both(0, k_lanes), 0),
        jnp.concatenate(both(128, k_lanes), 0),
        jnp.concatenate(both(256, k_lanes) + both(384, k_lanes), 0),
    ]
    values = [
        jnp.concatenate([v_ref[...], vp_ref[...]], 0),
        jnp.concatenate(both(0, v_lanes), 0),
        jnp.concatenate(both(128, v_lanes), 0),
        jnp.concatenate(both(256, v_lanes) + both(384, v_lanes), 0),
    ]
    queries = [q0, qs[0:256], qs[256:384], qs[384:512]]
    grads = [g0, gs[0:256], gs[256:384], gs[384:512]]

    raised, peaks, lses, outs = [], [], [], []
    for i in range(4):
        scores = dot_nt(keys[i], queries[i]) * (SCALE * LOG2E)
        if i == 3:
            shape = (512, 128)
            third = lax.broadcasted_iota(jnp.int32, shape, 0) < 256
            column = lax.broadcasted_iota(jnp.int32, shape, 1) < 64
            scores = jnp.where(third == column, scores, -jnp.inf)
        peak = jnp.max(scores, 0, keepdims=True)
        power = jnp.exp2(scores - peak)
        total = jnp.sum(power, 0, keepdims=True)
        raised.append(power)
        peaks.append(peak)
        lses.append(peak + jnp.log2(total))
        flipped = dot_nt(eye, values[i]).astype(BF)
        outs.append(dot(flipped, power.astype(BF)))

    lse_first = lses[0]
    lse_rest = jnp.concatenate(lses[1:], 1)
    lane = lax.broadcasted_iota(jnp.int32, (1, 512), 1)
    rows = []
    for start, stop in ((0, 256), (256, 384), (384, 448), (448, 480)):
        inside = (lane >= start) & (lane < stop)
        rows += [jnp.where(inside, part, 0.0) for part in split3(lse_rest)]
        rows.append(jnp.where(inside, 1.0, 0.0))
    placed = dot(jnp.concatenate(rows, 0).astype(BF), spread)
    merged_peak = lse_first
    level_lse = []
    for k in range(4):
        part = placed[4 * k : 4 * k + 1] + placed[4 * k + 1 : 4 * k + 2] + placed[4 * k + 2 : 4 * k + 3]
        member = placed[4 * k + 3 : 4 * k + 4] > 0.5
        level_lse.append((part, member))
        merged_peak = jnp.maximum(merged_peak, jnp.where(member, part, lse_first))
    row_total = jnp.exp2(lse_first - merged_peak)
    for part, member in level_lse:
        row_total = row_total + jnp.where(member, jnp.exp2(part - merged_peak), 0.0)
    merged = merged_peak + jnp.log2(row_total)

    def at_selection(x):
        parts = split3(x) + [jnp.zeros((13, WIDE), F32)]
        got = dot_nt(jnp.concatenate(parts, 0).astype(BF), spread)
        return got[0:1] + got[1:2] + got[2:3]

    merged_sel = at_selection(merged)
    bounds = ((0, 256), (256, 384), (384, 512))
    factors = [jnp.exp2(peaks[0] - merged)]
    factors += [jnp.exp2(peaks[i + 1] - merged_sel[:, a:b]) for i, (a, b) in enumerate(bounds)]

    def to_rows(flat):
        flat = flat.astype(BF)
        return [dot_nt(eye, flat[:, c : c + 128]) for c in range(0, flat.shape[1], 128)]

    def gather_levels(first, rest):
        level0 = jnp.concatenate(to_rows(first), 1)
        rows = jnp.concatenate(sum([to_rows(part) for part in rest], []), 0)
        return level0 + dot(place, by_selection(rows).astype(BF))

    scaled = [outs[i] * factors[i] for i in range(4)]
    attended = gather_levels(scaled[0], scaled[1:]).astype(BF)
    att_ref[...] = attended

    product = g_rows.astype(F32) * attended.astype(F32)
    high = product.astype(BF)
    low = (product - high.astype(F32)).astype(BF)
    ones = jnp.ones((16, D), BF)
    delta = jnp.concatenate(
        [
            (dot_nt(ones, high[:, h * D : (h + 1) * D]) + dot_nt(ones, low[:, h * D : (h + 1) * D]))[0:1]
            for h in range(HEADS)
        ],
        1,
    )
    delta_sel = at_selection(delta)
    deltas = [delta] + [delta_sel[:, a:b] for a, b in bounds]

    dqs = []
    for i in range(4):
        probs = raised[i] * factors[i]
        grad_weights = dot_nt(values[i], grads[i])
        grad_scores = (probs * (grad_weights - deltas[i])).astype(BF)
        grad_values = dot(probs.astype(BF), grads[i])
        grad_keys = dot(grad_scores, queries[i]) * SCALE
        flipped = dot_nt(eye, keys[i]).astype(BF)
        dqs.append(dot(flipped, grad_scores) * SCALE)
        pair = jnp.concatenate([grad_keys, grad_values], 1).astype(BF)
        if i == 0:
            d0_ref[0] = pair
        else:
            start = 128 * (i - 1)
            for part in range(pair.shape[0] // 256):
                at = start + 128 * part
                down_ref[0, at : at + 128] = pair[256 * part : 256 * part + 128]
                dother_ref[0, at : at + 128] = pair[256 * part + 128 : 256 * part + 256]
    dq_ref[...] = gather_levels(dqs[0], dqs[1:]).astype(BF)


def reduce_kernel(offs, d0, mine, theirs, kept, far, up, down, x_far, x_kept):
    for g in range(GROUPS):
        total = mine[g].astype(F32) + theirs[g].astype(F32)
        place = placer(offs, g)
        zero = jnp.zeros((8, 2 * D), F32)
        for z in range(4):
            middle = [
                total[128 + 32 * z : 160 + 32 * z],
                total[256 + 32 * z : 272 + 32 * z],
                total[384 + 32 * z : 392 + 32 * z],
                zero,
            ]
            extra = [total[272 + 32 * z : 288 + 32 * z], total[392 + 32 * z : 416 + 32 * z], zero]
            if z < 2:
                rows = jnp.concatenate([total[64 * z : 64 * z + 64]] + middle, 0).astype(BF)
                whole = d0[g, 128 * z : 128 * z + 128].astype(F32) + dot(place, rows)
                if z == 0:
                    kept[g] = whole
                    x_kept[g] = jnp.concatenate(extra, 0)
                else:
                    far[g] = whole.astype(BF)
                    x_far[g] = jnp.concatenate(extra, 0).astype(BF)
            else:
                ref = up if z == 2 else down
                ref[g] = jnp.concatenate(middle + extra, 0).astype(BF)


def cross_kernel(kept, far, up, down, one, two, three):
    for g in range(GROUPS):
        total = kept[g] + far[g].astype(F32) + up[g, 64:112].astype(F32) + down[g, 64:112].astype(F32)
        zero = jnp.zeros((8, 2 * D), F32)
        one[g] = jnp.concatenate([total[0:24], zero], 0).astype(BF)
        two[g] = jnp.concatenate([total[24:32], zero], 0).astype(BF)
        three[g] = jnp.concatenate([total[32:40], zero], 0).astype(BF)


def finish_kernel(offs, kept, far, up, down, one, two, three, dk_ref, dv_ref):
    for g in range(GROUPS):
        middle = up[g, 0:64].astype(F32) + down[g, 0:64].astype(F32)
        a, b, c = one[g].astype(F32), two[g].astype(F32), three[g].astype(F32)
        rows = jnp.concatenate(
            [
                jnp.zeros((64, 2 * D), F32),
                middle[0:32],
                middle[32:48] + a[0:16],
                middle[48:56] + a[16:24] + b[0:8] + c[0:8],
                jnp.zeros((8, 2 * D), F32),
            ],
            0,
        ).astype(BF)
        whole = kept[g] + far[g].astype(F32) + dot(placer(offs, g), rows)
        dk_ref[:, g * D : (g + 1) * D] = whole[:, :D].astype(BF)
        dv_ref[:, g * D : (g + 1) * D] = whole[:, D:].astype(BF)


def whole_call(body, name, outs, offs, *arrays):
    specs = [pl.BlockSpec(memory_space=pltpu.VMEM)] * len(arrays)
    if offs is not None:
        specs = [pl.BlockSpec(memory_space=pltpu.SMEM)] + specs
        arrays = (offs,) + arrays
    shapes = [jax.ShapeDtypeStruct(shape, dtype) for shape, dtype in outs]
    return pl.pallas_call(
        body,
        name=name,
        out_shape=shapes,
        in_specs=specs,
        out_specs=[pl.BlockSpec(memory_space=pltpu.VMEM)] * len(shapes),
        compiler_params=pltpu.CompilerParams(vmem_limit_bytes=VMEM_LIMIT),
    )(*arrays)


def attention(offs, q, g, k, v, kp, vp, own, other):
    lanes = lambda width: pl.BlockSpec((TOKENS, width), lambda i: (0, i))
    block = lambda rows: pl.BlockSpec((1, rows, 2 * D), lambda i: (i, 0, 0))
    return pl.pallas_call(
        attention_kernel,
        name="attention",
        grid=(GROUPS,),
        in_specs=[pl.BlockSpec(memory_space=pltpu.SMEM)]
        + [lanes(WIDE), lanes(WIDE), lanes(D), lanes(D), lanes(D), lanes(D), block(512), block(512)],
        out_specs=[lanes(WIDE), lanes(WIDE), block(256), block(512), block(512)],
        out_shape=[
            jax.ShapeDtypeStruct((TOKENS, GROUPS * WIDE), BF),
            jax.ShapeDtypeStruct((TOKENS, GROUPS * WIDE), BF),
            jax.ShapeDtypeStruct((GROUPS, 256, 2 * D), BF),
            jax.ShapeDtypeStruct((GROUPS, 512, 2 * D), BF),
            jax.ShapeDtypeStruct((GROUPS, 512, 2 * D), BF),
        ],
        compiler_params=pltpu.CompilerParams(vmem_limit_bytes=VMEM_LIMIT),
    )(offs, q, g, k, v, kp, vp, own, other)


def routes(count):
    def along_z(i, step):
        z = ((i & 1) * 2 + (i >> 2 & 1) + step) % 4
        return (i & ~5) | (z & 1) << 2 | z >> 1

    table = {
        "head": lambda i: i ^ 1,
        "core": lambda i: i ^ 2,
        "up": lambda i: along_z(i, 1),
        "down": lambda i: along_z(i, -1),
        "x1": lambda i: i ^ 8,
        "x2": lambda i: i ^ 16,
        "x3": lambda i: i ^ 24,
    }
    return {name: [(i, to(i)) for i in range(count)] for name, to in table.items()}


def shards(count, queries, key_rows, value_rows, gradient, level_offsets):
    route = routes(count)

    def send(x, name):
        return lax.ppermute(x, AXES, route[name])

    other_offsets = send(level_offsets, "head")
    low = lax.axis_index("head") == 0
    offs = jnp.where(
        low,
        jnp.concatenate([level_offsets, other_offsets], 1),
        jnp.concatenate([other_offsets, level_offsets], 1),
    )
    far_keys = send(key_rows, "head")
    far_values = send(value_rows, "head")

    rows = lambda n, dtype=BF: ((GROUPS, n, 2 * D), dtype)
    first, middle, tail, last = whole_call(
        select_kernel, "select", [rows(64), rows(64), rows(32), rows(16)], offs, key_rows, value_rows
    )
    middle_down = send(middle, "up")
    middle_up = send(middle, "down")
    (extra,) = whole_call(
        compact_kernel, "compact", [rows(48)], None, send(tail, "x1"), send(last, "x2"), send(last, "x3")
    )
    extra_down = send(extra, "up")
    extra_up = send(extra, "down")
    extra_far = send(extra, "head")
    (own,) = whole_call(
        assemble_kernel, "assemble", [rows(512)], offs, first, middle, extra, far_keys, far_values,
        extra_far, middle_up, extra_up, middle_down, extra_down,
    )
    other = send(own, "core")
    attended, grad_queries, d0, down_own, down_other = attention(
        offs, queries, gradient, key_rows, value_rows, far_keys, far_values, own, other
    )
    theirs = send(down_other, "core")
    kept, far, up, down, x_far, x_kept = whole_call(
        reduce_kernel, "reduce", [rows(128, F32), rows(128), rows(112), rows(112), rows(48), rows(48, F32)],
        offs, d0, down_own, theirs,
    )
    from_down = send(up, "up")
    from_up = send(down, "down")
    x_far = send(x_far, "head")
    far = send(far, "head")
    one, two, three = whole_call(
        cross_kernel, "cross", [rows(32), rows(16), rows(16)], None, x_kept, x_far, from_up, from_down
    )
    one, two, three = send(one, "x1"), send(two, "x2"), send(three, "x3")
    out = ((TOKENS, GROUPS * D), BF)
    grad_keys, grad_values = whole_call(
        finish_kernel, "finish", [out, out], offs, kept, far, from_up, from_down, one, two, three
    )
    return (attended, grad_queries, grad_keys, grad_values)


def solution(mesh):
    rows = P(AXES, None)
    return jax.shard_map(
        functools.partial(shards, mesh.size),
        mesh=mesh,
        in_specs=(rows, rows, rows, rows, P(None, "head")),
        out_specs=(rows, rows, rows, rows),
        check_vma=False,
    )
```

```python
import functools

import jax
import jax.numpy as jnp
from jax import lax
from jax.experimental import pallas as pl
from jax.experimental.pallas import tpu as pltpu
from jax.sharding import PartitionSpec as P

D = 128
GROUPS = 8
HEADS = 4
TOKENS = 128
TOGETHER = 1
WIDE = HEADS * D
SCALE = D ** (-0.5)
LOG2E = 1.4426950408889634
AXES = ("ctx", "head")
BF = jnp.bfloat16
F32 = jnp.float32
ANY_ROWS = ((0, 64, 1), (64, 96, 2), (96, 112, 3), (112, 120, 4))
VMEM_LIMIT = 24 * 1024 * 1024


def dot(a, b):
    return lax.dot_general(a, b, (((1,), (0,)), ((), ())), preferred_element_type=F32)


def dot_nt(a, b):
    return lax.dot_general(a, b, (((1,), (1,)), ((), ())), preferred_element_type=F32)


def dot_tn(a, b):
    return lax.dot_general(a, b, (((0,), (0,)), ((), ())), preferred_element_type=F32)


def one_hot(mask):
    return jnp.where(mask, 1.0, 0.0).astype(BF)


def selected_token(row, offs, group):
    token = jnp.full(row.shape, -1, jnp.int32)
    for start, stop, level in ANY_ROWS:
        inside = (row >= start) & (row < stop)
        token = jnp.where(inside, (row - start) * 2**level + offs[level, group], token)
    return token


def selector(offs, group):
    shape = (128, TOKENS)
    row = lax.broadcasted_iota(jnp.int32, shape, 0)
    return one_hot(selected_token(row, offs, group) == lax.broadcasted_iota(jnp.int32, shape, 1))


def placer(offs, group):
    shape = (TOKENS, 128)
    row = lax.broadcasted_iota(jnp.int32, shape, 1)
    return one_hot(selected_token(row, offs, group) == lax.broadcasted_iota(jnp.int32, shape, 0))


def group_rows(keys_ref, values_ref, group):
    lanes = slice(group * D, (group + 1) * D)
    return jnp.concatenate([keys_ref[:, lanes], values_ref[:, lanes]], 1)


def select_kernel(offs, keys, values, first, middle, tail, last):
    for g in range(GROUPS):
        rows = dot(selector(offs, g), group_rows(keys, values, g))
        first[g] = rows[0:64].astype(BF)
        middle[g] = rows[64:128].astype(BF)
        tail[g] = rows[96:128].astype(BF)
        last[g] = rows[112:128].astype(BF)


def compact_kernel(one, two, three, packed):
    for g in range(GROUPS):
        a, b, c = one[g].astype(F32), two[g].astype(F32), three[g].astype(F32)
        packed[g] = jnp.concatenate([a[:24], b[:8], c[:8], jnp.zeros((8, 2 * D), F32)], 0).astype(BF)


def assemble_kernel(
    offs, first, mid_own, x_own, keys, values, x_far, mid_up, x_up, mid_down, x_down, held
):
    for g in range(GROUPS):
        far = dot(selector(offs, g), group_rows(keys, values, g))
        mids = [mid_own[g].astype(F32), far[64:128], mid_up[g].astype(F32), mid_down[g].astype(F32)]
        extras = [ref[g].astype(F32) for ref in (x_own, x_far, x_up, x_down)]
        rows = [first[g].astype(F32), far[0:64]]
        rows += [m[0:32] for m in mids]
        for m, x in zip(mids, extras):
            rows += [m[32:48], x[0:16]]
        for m, x in zip(mids, extras):
            rows += [m[48:56], x[16:40]]
        held[g] = jnp.concatenate(rows, 0).astype(BF)


def by_level(rows):
    parts = []
    for start, stop in ((0, 64), (64, 96), (96, 112), (112, 120), (120, 128)):
        parts += [rows[start:stop, h * D : (h + 1) * D] for h in range(HEADS)]
    return jnp.concatenate(parts, 0)


def by_selection(rows):
    heads = []
    for h in range(HEADS):
        parts = []
        base = 0
        for count in (64, 32, 16, 8, 8):
            parts.append(rows[base + h * count : base + (h + 1) * count])
            base += HEADS * count
        heads.append(jnp.concatenate(parts, 0))
    return jnp.concatenate(heads, 1)


def replicated(column, lanes):
    return jnp.broadcast_to(column, (column.shape[0], lanes))


def heads_to_lanes(column):
    count = column.shape[0] // HEADS
    wide = replicated(column, 128)
    lane = lax.broadcasted_iota(jnp.int32, (count, 128), 1)
    out = wide[(HEADS - 1) * count :]
    for h in range(HEADS - 1):
        out = jnp.where(lane == h, wide[h * count : (h + 1) * count], out)
    return out


def lanes_to_heads(x):
    return jnp.concatenate([x[:, h : h + 1] for h in range(HEADS)], 0)


def attention_kernel(
    offs, q_ref, g_ref, k_ref, v_ref, kp_ref, vp_ref, own_ref, other_ref,
    att_ref, dq_ref, d0_ref, down_ref, dother_ref, level_ref, token_ref, delta_ref,
):
    members = range(TOGETHER)
    first_group = pl.program_id(0) * TOGETHER
    ones = jnp.ones((256, D), BF)
    bounds = ((0, 256), (256, 384), (384, 448), (448, 480))
    starts = [[(offs[k, first_group + j], 128 >> k) for k in range(1, 5)] for j in members]

    def load(j):
        wide, lanes = slice(j * WIDE, (j + 1) * WIDE), slice(j * D, (j + 1) * D)
        pick = selector(offs, first_group + j)
        q_rows, g_rows = q_ref[:, wide], g_ref[:, wide]
        qs = by_level(dot(pick, q_rows)).astype(BF)
        gs = by_level(dot(pick, g_rows)).astype(BF)
        own, other = own_ref[j], other_ref[j]
        queries = [jnp.concatenate([q_rows[:, h * D : (h + 1) * D] for h in range(HEADS)], 0)]
        grads = [jnp.concatenate([g_rows[:, h * D : (h + 1) * D] for h in range(HEADS)], 0)]
        keys = [jnp.concatenate([k_ref[:, lanes], kp_ref[:, lanes]], 0)]
        values = [jnp.concatenate([v_ref[:, lanes], vp_ref[:, lanes]], 0)]
        for k, (a, b) in enumerate(bounds):
            queries.append(qs[a:b])
            grads.append(gs[a:b])
            both = jnp.concatenate([own[128 * k : 128 * k + 128], other[128 * k : 128 * k + 128]], 0)
            keys.append(both[:, :D])
            values.append(both[:, D:])
        return queries, grads, keys, values

    def forward(state):
        queries, _, keys, values = state
        raised, peaks, lses, outs = [], [], [], []
        for k in range(5):
            scores = dot_nt(queries[k], keys[k]) * (SCALE * LOG2E)
            peak = jnp.max(scores, 1, keepdims=True)
            power = jnp.exp2(scores - peak).astype(BF)
            out = dot(power, jnp.concatenate([values[k], ones], 1))
            raised.append(power)
            peaks.append(peak)
            lses.append(peak + jnp.log2(out[:, D : D + 1]))
            outs.append(out[:, :D])
        return raised, peaks, lses, outs

    def for_levels(j, ref, x):
        ref[j] = x
        columns = [lanes_to_heads(x)]
        for k, (start, count) in enumerate(starts[j]):
            columns.append(lanes_to_heads(ref[j, pl.ds(start, count, 2 ** (k + 1)), :]))
        return columns

    def merge(j, lses, peaks):
        for k, (start, count) in enumerate(starts[j]):
            level_ref[j, k, pl.ds(start, count, 2 ** (k + 1)), :] = heads_to_lanes(lses[k + 1])
        first = heads_to_lanes(lses[0])
        merged_peak = first
        for k in range(4):
            merged_peak = jnp.maximum(merged_peak, level_ref[j, k])
        row_total = jnp.exp2(first - merged_peak)
        for k in range(4):
            row_total = row_total + jnp.exp2(level_ref[j, k] - merged_peak)
        merged = merged_peak + jnp.log2(row_total)
        return [jnp.exp2(p - m) for p, m in zip(peaks, for_levels(j, token_ref, merged))]

    def gather_levels(j, parts):
        level0 = jnp.concatenate([parts[0][h * 128 : h * 128 + 128] for h in range(HEADS)], 1)
        rows = jnp.concatenate(parts[1:] + [jnp.zeros((32, D), F32)], 0)
        return level0 + dot(placer(offs, first_group + j), by_selection(rows).astype(BF))

    def attend(j, outs, factors):
        wide = slice(j * WIDE, (j + 1) * WIDE)
        attended = gather_levels(j, [out * factor for out, factor in zip(outs, factors)]).astype(BF)
        att_ref[:, wide] = attended
        product = g_ref[:, wide].astype(F32) * attended.astype(F32)
        delta = jnp.concatenate(
            [jnp.sum(product[:, h * D : (h + 1) * D], 1, keepdims=True) for h in range(HEADS)], 0
        )
        return for_levels(j, delta_ref, heads_to_lanes(delta))

    def backward(j, k, state, raised, factors, deltas):
        queries, grads, keys, values = state
        probs = raised[k].astype(F32) * factors[k]
        grad_weights = dot_nt(grads[k], values[k])
        grad_scores = (probs * (grad_weights - deltas[k])).astype(BF)
        grad_values = dot_tn(probs.astype(BF), grads[k])
        grad_keys = dot_tn(grad_scores, queries[k]) * SCALE
        pair = jnp.concatenate([grad_keys, grad_values], 1).astype(BF)
        if k == 0:
            d0_ref[j] = pair
        else:
            at = 128 * (k - 1)
            down_ref[j, at : at + 128] = pair[:128]
            dother_ref[j, at : at + 128] = pair[128:]
        return dot(grad_scores, keys[k]) * SCALE

    level_ref[...] = jnp.full(level_ref.shape, -1e30, F32)
    states = [load(j) for j in members]
    results = [forward(states[j]) for j in members]
    factors = [merge(j, results[j][2], results[j][1]) for j in members]
    deltas = [attend(j, results[j][3], factors[j]) for j in members]
    for j in members:
        dqs = [backward(j, k, states[j], results[j][0], factors[j], deltas[j]) for k in range(5)]
        dq_ref[:, j * WIDE : (j + 1) * WIDE] = gather_levels(j, dqs).astype(BF)


def middle_and_extra(total, z):
    zero = jnp.zeros((8, 2 * D), F32)
    middle = [
        total[128 + 32 * z : 160 + 32 * z],
        total[256 + 32 * z : 272 + 32 * z],
        total[384 + 32 * z : 392 + 32 * z],
        zero,
    ]
    return middle, [total[272 + 32 * z : 288 + 32 * z], total[392 + 32 * z : 416 + 32 * z], zero]


def reduce_kernel(mine, theirs, rows_kept, rows_far, up, down, x_far, x_kept):
    for g in range(GROUPS):
        total = mine[g].astype(F32) + theirs[g].astype(F32)
        for z, ref in enumerate((rows_kept, rows_far, up, down)):
            middle, extra = middle_and_extra(total, z)
            if z < 2:
                ref[g] = jnp.concatenate([total[64 * z : 64 * z + 64]] + middle, 0).astype(BF)
            else:
                ref[g] = jnp.concatenate(middle + extra, 0).astype(BF)
            if z == 0:
                x_kept[g] = jnp.concatenate(extra, 0)
            if z == 1:
                x_far[g] = jnp.concatenate(extra, 0).astype(BF)


def place_kernel(offs, d0, rows_far, _, far):
    for g in range(GROUPS):
        far[g] = (d0[g, 128:256].astype(F32) + dot(placer(offs, g), rows_far[g])).astype(BF)


def cross_kernel(kept, far, up, down, one, two, three):
    for g in range(GROUPS):
        total = kept[g] + far[g].astype(F32) + up[g, 64:112].astype(F32) + down[g, 64:112].astype(F32)
        zero = jnp.zeros((8, 2 * D), F32)
        one[g] = jnp.concatenate([total[0:24], zero], 0).astype(BF)
        two[g] = jnp.concatenate([total[24:32], zero], 0).astype(BF)
        three[g] = jnp.concatenate([total[32:40], zero], 0).astype(BF)


def finish_kernel(offs, d0, rows_kept, far, up, down, one, two, three, dk_ref, dv_ref):
    for g in range(GROUPS):
        kept = rows_kept[g].astype(F32)
        middle = up[g, 0:64].astype(F32) + down[g, 0:64].astype(F32) + kept[64:128]
        a, b, c = one[g].astype(F32), two[g].astype(F32), three[g].astype(F32)
        rows = jnp.concatenate(
            [
                kept[0:64],
                middle[0:32],
                middle[32:48] + a[0:16],
                middle[48:56] + a[16:24] + b[0:8] + c[0:8],
                jnp.zeros((8, 2 * D), F32),
            ],
            0,
        ).astype(BF)
        whole = d0[g, 0:128].astype(F32) + far[g].astype(F32) + dot(placer(offs, g), rows)
        dk_ref[:, g * D : (g + 1) * D] = whole[:, :D].astype(BF)
        dv_ref[:, g * D : (g + 1) * D] = whole[:, D:].astype(BF)


def whole_call(body, name, outs, offs, *arrays, after=()):
    specs = [pl.BlockSpec(memory_space=pltpu.VMEM)] * len(arrays)
    specs += [pl.BlockSpec(memory_space=pl.ANY)] * len(after)
    arrays = arrays + tuple(after)
    if offs is not None:
        specs = [pl.BlockSpec(memory_space=pltpu.SMEM)] + specs
        arrays = (offs,) + arrays
    shapes = [jax.ShapeDtypeStruct(shape, dtype) for shape, dtype in outs]
    return pl.pallas_call(
        body,
        name=name,
        out_shape=shapes,
        in_specs=specs,
        out_specs=[pl.BlockSpec(memory_space=pltpu.VMEM)] * len(shapes),
        cost_estimate=pl.CostEstimate(flops=0, bytes_accessed=4 * 10**6, transcendentals=0),
        compiler_params=pltpu.CompilerParams(vmem_limit_bytes=VMEM_LIMIT),
    )(*arrays)


def attention(offs, q, g, k, v, kp, vp, own, other):
    lanes = lambda width: pl.BlockSpec((TOKENS, TOGETHER * width), lambda i: (0, i))
    block = lambda rows: pl.BlockSpec((TOGETHER, rows, 2 * D), lambda i: (i, 0, 0))
    return pl.pallas_call(
        attention_kernel,
        name="attention",
        grid=(GROUPS // TOGETHER,),
        in_specs=[pl.BlockSpec(memory_space=pltpu.SMEM)]
        + [lanes(WIDE), lanes(WIDE), lanes(D), lanes(D), lanes(D), lanes(D), block(512), block(512)],
        out_specs=[lanes(WIDE), lanes(WIDE), block(256), block(512), block(512)],
        out_shape=[
            jax.ShapeDtypeStruct((TOKENS, GROUPS * WIDE), BF),
            jax.ShapeDtypeStruct((TOKENS, GROUPS * WIDE), BF),
            jax.ShapeDtypeStruct((GROUPS, 256, 2 * D), BF),
            jax.ShapeDtypeStruct((GROUPS, 512, 2 * D), BF),
            jax.ShapeDtypeStruct((GROUPS, 512, 2 * D), BF),
        ],
        scratch_shapes=[
            pltpu.VMEM((TOGETHER, 4, TOKENS, 128), F32),
            pltpu.VMEM((TOGETHER, TOKENS, 128), F32),
            pltpu.VMEM((TOGETHER, TOKENS, 128), F32),
        ],
        compiler_params=pltpu.CompilerParams(vmem_limit_bytes=62 * 1024 * 1024),
    )(offs, q, g, k, v, kp, vp, own, other)


def routes(count):
    def along_z(i, step):
        z = ((i & 1) * 2 + (i >> 2 & 1) + step) % 4
        return (i & ~5) | (z & 1) << 2 | z >> 1

    table = {
        "head": lambda i: i ^ 1,
        "core": lambda i: i ^ 2,
        "up": lambda i: along_z(i, 1),
        "down": lambda i: along_z(i, -1),
        "x1": lambda i: i ^ 8,
        "x2": lambda i: i ^ 16,
        "x3": lambda i: i ^ 24,
    }
    return {name: [(i, to(i)) for i in range(count)] for name, to in table.items()}


def shards(count, queries, key_rows, value_rows, gradient, level_offsets):
    route = routes(count)

    def send(x, name):
        return lax.ppermute(x, AXES, route[name])

    other_offsets = send(level_offsets, "head")
    low = lax.axis_index("head") == 0
    offs = jnp.where(
        low,
        jnp.concatenate([level_offsets, other_offsets], 1),
        jnp.concatenate([other_offsets, level_offsets], 1),
    )
    key_swap, value_swap, other_offsets = lax.optimization_barrier((key_rows, value_rows, other_offsets))
    far_keys = send(key_swap, "head")
    far_values = send(value_swap, "head")

    rows = lambda n, dtype=BF: ((GROUPS, n, 2 * D), dtype)
    first, middle, tail, last = whole_call(
        select_kernel, "select", [rows(64), rows(64), rows(32), rows(16)], offs, key_rows, value_rows
    )
    middle_down = send(middle, "up")
    middle_up = send(middle, "down")
    (extra,) = whole_call(
        compact_kernel, "compact", [rows(48)], None, send(tail, "x1"), send(last, "x2"), send(last, "x3")
    )
    extra_down = send(extra, "up")
    extra_up = send(extra, "down")
    extra_far = send(extra, "head")
    (own,) = whole_call(
        assemble_kernel, "assemble", [rows(512)], offs, first, middle, extra, far_keys, far_values,
        extra_far, middle_up, extra_up, middle_down, extra_down,
    )
    other = send(own, "core")
    attended, grad_queries, d0, down_own, down_other = attention(
        offs, queries, gradient, key_rows, value_rows, far_keys, far_values, own, other
    )
    theirs = send(down_other, "core")
    rows_kept, rows_far, up, down, x_far, x_kept = whole_call(
        reduce_kernel, "reduce", [rows(128), rows(128), rows(112), rows(112), rows(48), rows(48, F32)],
        None, down_own, theirs,
    )
    from_down = send(up, "up")
    from_up = send(down, "down")
    x_far = send(x_far, "head")
    (far,) = whole_call(place_kernel, "place", [rows(128)], offs, d0, rows_far, after=(x_far,))
    far = send(far, "head")
    one, two, three = whole_call(
        cross_kernel, "cross", [rows(32), rows(16), rows(16)], None, x_kept, x_far, from_up, from_down
    )
    one, two, three = send(one, "x1"), send(two, "x2"), send(three, "x3")
    out = ((TOKENS, GROUPS * D), BF)
    grad_keys, grad_values = whole_call(
        finish_kernel, "finish", [out, out], offs, d0, rows_kept, far, from_up, from_down, one, two, three
    )
    return (attended, grad_queries, grad_keys, grad_values)


def solution(mesh):
    rows = P(AXES, None)
    return jax.shard_map(
        functools.partial(shards, mesh.size),
        mesh=mesh,
        in_specs=(rows, rows, rows, rows, P(None, "head")),
        out_specs=(rows, rows, rows, rows),
        check_vma=False,
    )
```

```python
import functools

import jax
import jax.numpy as jnp
from jax import lax
from jax.experimental import pallas as pl
from jax.experimental.pallas import tpu as pltpu
from jax.sharding import PartitionSpec as P

D = 128
GROUPS = 8
HEADS = 4
TOKENS = 128
PARTS = 2
SHARE = GROUPS // PARTS
WIDE = HEADS * D
SCALE = D ** (-0.5)
LOG2E = 1.4426950408889634
AXES = ("ctx", "head")
BF = jnp.bfloat16
F32 = jnp.float32
ANY_ROWS = ((0, 64, 1), (64, 96, 2), (96, 112, 3), (112, 120, 4))
VMEM_LIMIT = 24 * 1024 * 1024


def dot(a, b):
    return lax.dot_general(a, b, (((1,), (0,)), ((), ())), preferred_element_type=F32)


def dot_nt(a, b):
    return lax.dot_general(a, b, (((1,), (1,)), ((), ())), preferred_element_type=F32)


def dot_tn(a, b):
    return lax.dot_general(a, b, (((0,), (0,)), ((), ())), preferred_element_type=F32)


def one_hot(mask):
    return jnp.where(mask, 1.0, 0.0).astype(BF)


def selected_token(row, offs, group):
    token = jnp.full(row.shape, -1, jnp.int32)
    for start, stop, level in ANY_ROWS:
        inside = (row >= start) & (row < stop)
        token = jnp.where(inside, (row - start) * 2**level + offs[level, group], token)
    return token


def selector(offs, group):
    shape = (128, TOKENS)
    row = lax.broadcasted_iota(jnp.int32, shape, 0)
    return one_hot(selected_token(row, offs, group) == lax.broadcasted_iota(jnp.int32, shape, 1))


def placer(offs, group):
    shape = (TOKENS, 128)
    row = lax.broadcasted_iota(jnp.int32, shape, 1)
    return one_hot(selected_token(row, offs, group) == lax.broadcasted_iota(jnp.int32, shape, 0))


def group_rows(pair_ref, member):
    k, v = member * D, (SHARE + member) * D
    return jnp.concatenate([pair_ref[:, k : k + D], pair_ref[:, v : v + D]], 1)


def select_kernel(base, offs, pair, first, middle, tail, last):
    for g in range(SHARE):
        rows = dot(selector(offs, base + g), group_rows(pair, g))
        first[g] = rows[0:64].astype(BF)
        middle[g] = rows[64:128].astype(BF)
        tail[g] = rows[96:128].astype(BF)
        last[g] = rows[112:128].astype(BF)


def compact_kernel(one, two, three, _, packed):
    for g in range(SHARE):
        a, b, c = one[g].astype(F32), two[g].astype(F32), three[g].astype(F32)
        packed[g] = jnp.concatenate([a[:24], b[:8], c[:8], jnp.zeros((8, 2 * D), F32)], 0).astype(BF)


def assemble_kernel(
    base, offs, first, mid_own, x_own, pair, x_far, mid_up, x_up, mid_down, x_down, *refs
):
    held = refs[-1]
    for g in range(SHARE):
        far = dot(selector(offs, base + g), group_rows(pair, g))
        mids = [mid_own[g].astype(F32), far[64:128], mid_up[g].astype(F32), mid_down[g].astype(F32)]
        extras = [ref[g].astype(F32) for ref in (x_own, x_far, x_up, x_down)]
        rows = [first[g].astype(F32), far[0:64]]
        rows += [m[0:32] for m in mids]
        for m, x in zip(mids, extras):
            rows += [m[32:48], x[0:16]]
        for m, x in zip(mids, extras):
            rows += [m[48:56], x[16:40]]
        held[g] = jnp.concatenate(rows, 0).astype(BF)


def by_level(rows):
    parts = []
    for start, stop in ((0, 64), (64, 96), (96, 112), (112, 120), (120, 128)):
        parts += [rows[start:stop, h * D : (h + 1) * D] for h in range(HEADS)]
    return jnp.concatenate(parts, 0)


def by_selection(rows):
    heads = []
    for h in range(HEADS):
        parts = []
        base = 0
        for count in (64, 32, 16, 8, 8):
            parts.append(rows[base + h * count : base + (h + 1) * count])
            base += HEADS * count
        heads.append(jnp.concatenate(parts, 0))
    return jnp.concatenate(heads, 1)


def heads_to_lanes(x):
    count = x.shape[0] // HEADS
    lane = lax.broadcasted_iota(jnp.int32, (count, 128), 1) & (HEADS - 1)
    out = x[(HEADS - 1) * count :]
    for h in range(HEADS - 1):
        out = jnp.where(lane == h, x[h * count : (h + 1) * count], out)
    return out


def attention_kernel(
    base, offs, q_ref, g_ref, pair_ref, far_ref, own_ref, other_ref, *refs
):
    att_ref, dq_ref, d0_ref, down_ref, dother_ref, level_ref, token_ref, delta_ref = refs[-8:]
    members = range(SHARE)
    ones = jnp.ones((256, D), BF)
    bounds = ((0, 256), (256, 384), (384, 448), (448, 480))
    starts = [[(offs[k, base + j], 128 >> k) for k in range(1, 5)] for j in members]

    def load(j):
        wide = slice(j * WIDE, (j + 1) * WIDE)
        own_pair, far_pair = group_rows(pair_ref, j), group_rows(far_ref, j)
        pick = selector(offs, base + j)
        q_rows, g_rows = q_ref[:, wide], g_ref[:, wide]
        qs = by_level(dot(pick, q_rows)).astype(BF)
        gs = by_level(dot(pick, g_rows)).astype(BF)
        own, other = own_ref[j], other_ref[j]
        queries = [jnp.concatenate([q_rows[:, h * D : (h + 1) * D] for h in range(HEADS)], 0)]
        grads = [jnp.concatenate([g_rows[:, h * D : (h + 1) * D] for h in range(HEADS)], 0)]
        keys = [jnp.concatenate([own_pair[:, :D], far_pair[:, :D]], 0)]
        values = [jnp.concatenate([own_pair[:, D:], far_pair[:, D:]], 0)]
        for k, (a, b) in enumerate(bounds):
            queries.append(qs[a:b])
            grads.append(gs[a:b])
            both = jnp.concatenate([own[128 * k : 128 * k + 128], other[128 * k : 128 * k + 128]], 0)
            keys.append(both[:, :D])
            values.append(both[:, D:])
        return queries, grads, keys, values

    def forward(states):
        results = [([], [], [], []) for _ in states]
        for k in range(5):
            scores = [dot_nt(st[0][k], st[2][k]) * (SCALE * LOG2E) for st in states]
            peaks = [jnp.max(x, 1, keepdims=True) for x in scores]
            powers = [jnp.exp2(x - p).astype(BF) for x, p in zip(scores, peaks)]
            outs = [dot(p, jnp.concatenate([st[3][k], ones], 1)) for p, st in zip(powers, states)]
            for r, power, peak, out in zip(results, powers, peaks, outs):
                peak = heads_to_lanes(jnp.broadcast_to(peak, (peak.shape[0], 128)))
                r[0].append(power)
                r[1].append(peak)
                r[2].append(peak + jnp.log2(heads_to_lanes(out[:, D:])))
                r[3].append(out[:, :D])
        return results

    def for_levels(ref, xs):
        for j, x in enumerate(xs):
            ref[j] = x
        columns = [[x] for x in xs]
        for k in range(4):
            for j in members:
                start, count = starts[j][k]
                columns[j].append(ref[j, pl.ds(start, count, 2 ** (k + 1)), :])
        return columns

    def merge(results):
        for k in range(4):
            for j in members:
                start, count = starts[j][k]
                level_ref[j, k, pl.ds(start, count, 2 ** (k + 1)), :] = results[j][2][k + 1]
        firsts = [r[2][0] for r in results]
        tops = [functools.reduce(jnp.maximum, [level_ref[j, k] for k in range(4)], firsts[j]) for j in members]
        sums = [
            jnp.exp2(firsts[j] - tops[j]) + sum(jnp.exp2(level_ref[j, k] - tops[j]) for k in range(4))
            for j in members
        ]
        columns = for_levels(token_ref, [top + jnp.log2(x) for top, x in zip(tops, sums)])
        return [[jnp.exp2(p - m) for p, m in zip(r[1], c)] for r, c in zip(results, columns)]

    def expand(x):
        return jnp.concatenate([jnp.broadcast_to(x[:, h : h + 1], x.shape) for h in range(HEADS)], 0)

    def beside(x):
        high = x.astype(BF).astype(F32)
        lane = lax.broadcasted_iota(jnp.int32, x.shape, 1)
        both = jnp.where(lane < 64, high, x - high)
        return jnp.concatenate(
            [jnp.where((lane & (HEADS - 1)) == h, both, 0.0) for h in range(HEADS)], 0
        ).astype(BF)

    def gather_levels(parts):
        level0 = [jnp.concatenate([p[0][h * 128 : h * 128 + 128] for h in range(HEADS)], 1) for p in parts]
        rows = [jnp.concatenate(p[1:] + [jnp.zeros((32, D), F32)], 0) for p in parts]
        rows = [by_selection(x).astype(BF) for x in rows]
        return [x + dot(placer(offs, base + j), r) for j, (x, r) in enumerate(zip(level0, rows))]

    def attend(results, spread):
        parts = [[out * f for out, f in zip(r[3], fs)] for r, fs in zip(results, spread)]
        attended = [x.astype(BF) for x in gather_levels(parts)]
        deltas = []
        for j, x in enumerate(attended):
            wide = slice(j * WIDE, (j + 1) * WIDE)
            att_ref[:, wide] = x
            product = g_ref[:, wide].astype(F32) * x.astype(F32)
            sums = [
                jnp.broadcast_to(jnp.sum(product[:, h * D : (h + 1) * D], 1, keepdims=True), (TOKENS, 128))
                for h in range(HEADS)
            ]
            deltas.append(heads_to_lanes(jnp.concatenate(sums, 0)))
        return for_levels(delta_ref, deltas)

    def backward(k, states, results, scaled, deltas):
        probs = [r[0][k] for r in results]
        weights = [
            dot_nt(
                jnp.concatenate([g[k], beside(d[k])], 1),
                jnp.concatenate([st[3][k], minus], 1),
            )
            for g, d, st in zip(scaled, deltas, states)
        ]
        scores = [(p.astype(F32) * w).astype(BF) for p, w in zip(probs, weights)]
        grad_values = [dot_tn(g[k], p).T for g, p in zip(scaled, probs)]
        grad_keys = [dot_tn(st[0][k], x).T * SCALE for x, st in zip(scores, states)]
        for j in members:
            pair = jnp.concatenate([grad_keys[j], grad_values[j]], 1).astype(BF)
            if k == 0:
                d0_ref[j] = pair
            else:
                at = 128 * (k - 1)
                down_ref[j, at : at + 128] = pair[:128]
                dother_ref[j, at : at + 128] = pair[128:]
        return [dot(x, st[2][k]) * SCALE for x, st in zip(scores, states)]

    shape = (2 * D, WIDE)
    row = lax.broadcasted_iota(jnp.int32, shape, 0) & (D - 1)
    widen = one_hot(row == lax.broadcasted_iota(jnp.int32, shape, 1) // D)
    lane = lax.broadcasted_iota(jnp.int32, (2 * D, D), 1)
    minus = jnp.where((lane & 63) < HEADS, -1.0, 0.0).astype(BF)
    level_ref[...] = jnp.full(level_ref.shape, -1e30, F32)
    states = [load(j) for j in members]
    results = forward(states)
    factors = merge(results)
    spread = [[expand(f) for f in fs] for fs in factors]
    deltas = attend(results, spread)
    deltas = [[f * d for f, d in zip(fs, ds)] for fs, ds in zip(factors, deltas)]
    scaled = [
        [(g.astype(F32) * f).astype(BF) for g, f in zip(st[1], fs)] for st, fs in zip(states, spread)
    ]
    dqs = [backward(k, states, results, scaled, deltas) for k in range(5)]
    for j, x in enumerate(gather_levels([[d[j] for d in dqs] for j in members])):
        dq_ref[:, j * WIDE : (j + 1) * WIDE] = x.astype(BF)


def middle_and_extra(total, z):
    zero = jnp.zeros((8, 2 * D), F32)
    middle = [
        total[128 + 32 * z : 160 + 32 * z],
        total[256 + 32 * z : 272 + 32 * z],
        total[384 + 32 * z : 392 + 32 * z],
        zero,
    ]
    return middle, [total[272 + 32 * z : 288 + 32 * z], total[392 + 32 * z : 416 + 32 * z], zero]


def reduce_kernel(mine, theirs, *refs):
    rows_kept, rows_far, up, down, x_far, x_kept = refs[-6:]
    for g in range(SHARE):
        total = mine[g].astype(F32) + theirs[g].astype(F32)
        for z, ref in enumerate((rows_kept, rows_far, up, down)):
            middle, extra = middle_and_extra(total, z)
            if z < 2:
                ref[g] = jnp.concatenate([total[64 * z : 64 * z + 64]] + middle, 0).astype(BF)
            else:
                ref[g] = jnp.concatenate(middle + extra, 0).astype(BF)
            if z == 0:
                x_kept[g] = jnp.concatenate(extra, 0)
            if z == 1:
                x_far[g] = jnp.concatenate(extra, 0).astype(BF)


def place_kernel(base, offs, d0, rows_far, _, far):
    for g in range(SHARE):
        far[g] = (d0[g, 128:256].astype(F32) + dot(placer(offs, base + g), rows_far[g])).astype(BF)


def cross_kernel(kept, far, up, down, one, two, three):
    for g in range(SHARE):
        total = kept[g] + far[g].astype(F32) + up[g, 64:112].astype(F32) + down[g, 64:112].astype(F32)
        zero = jnp.zeros((8, 2 * D), F32)
        one[g] = jnp.concatenate([total[0:24], zero], 0).astype(BF)
        two[g] = jnp.concatenate([total[24:32], zero], 0).astype(BF)
        three[g] = jnp.concatenate([total[32:40], zero], 0).astype(BF)


def finish_kernel(base, offs, d0, rows_kept, far, up, down, one, two, three, *refs):
    dk_ref, dv_ref = refs[-2:]
    if base:
        before_k, before_v = refs[:2]
        dk_ref[:, : base * D] = before_k[...]
        dv_ref[:, : base * D] = before_v[...]
    for g in range(SHARE):
        kept = rows_kept[g].astype(F32)
        middle = up[g, 0:64].astype(F32) + down[g, 0:64].astype(F32) + kept[64:128]
        a, b, c = one[g].astype(F32), two[g].astype(F32), three[g].astype(F32)
        rows = jnp.concatenate(
            [
                kept[0:64],
                middle[0:32],
                middle[32:48] + a[0:16],
                middle[48:56] + a[16:24] + b[0:8] + c[0:8],
                jnp.zeros((8, 2 * D), F32),
            ],
            0,
        ).astype(BF)
        whole = d0[g, 0:128].astype(F32) + far[g].astype(F32) + dot(placer(offs, base + g), rows)
        lanes = slice((base + g) * D, (base + g + 1) * D)
        dk_ref[:, lanes] = whole[:, :D].astype(BF)
        dv_ref[:, lanes] = whole[:, D:].astype(BF)


def whole_call(body, name, outs, offs, *arrays, after=()):
    specs = [pl.BlockSpec(memory_space=pltpu.VMEM)] * len(arrays)
    specs += [pl.BlockSpec(memory_space=pl.ANY)] * len(after)
    arrays = arrays + tuple(after)
    if offs is not None:
        specs = [pl.BlockSpec(memory_space=pltpu.SMEM)] + specs
        arrays = (offs,) + arrays
    shapes = [jax.ShapeDtypeStruct(shape, dtype) for shape, dtype in outs]
    return pl.pallas_call(
        body,
        name=name,
        out_shape=shapes,
        in_specs=specs,
        out_specs=[pl.BlockSpec(memory_space=pltpu.VMEM)] * len(shapes),
        cost_estimate=pl.CostEstimate(flops=0, bytes_accessed=4 * 10**6, transcendentals=0),
        compiler_params=pltpu.CompilerParams(vmem_limit_bytes=VMEM_LIMIT),
    )(*arrays)


def attention(base, offs, q, g, pair, far, own, other, before, after):
    part = base // SHARE
    lanes = pl.BlockSpec((TOKENS, SHARE * WIDE), lambda i: (0, part))
    whole = lambda *shape: pl.BlockSpec(shape, lambda i: (0,) * len(shape))
    pairs = whole(TOKENS, SHARE * 2 * D)
    rows = lambda n: whole(SHARE, n, 2 * D)
    return pl.pallas_call(
        functools.partial(attention_kernel, base),
        name="attention",
        grid=(1,),
        in_specs=[pl.BlockSpec(memory_space=pltpu.SMEM), lanes, lanes, pairs, pairs, rows(512), rows(512)]
        + [pl.BlockSpec(memory_space=pl.ANY)] * (len(before) + len(after)),
        out_specs=[lanes, lanes, rows(256), rows(512), rows(512)],
        out_shape=[
            jax.ShapeDtypeStruct((TOKENS, GROUPS * WIDE), BF),
            jax.ShapeDtypeStruct((TOKENS, GROUPS * WIDE), BF),
            jax.ShapeDtypeStruct((SHARE, 256, 2 * D), BF),
            jax.ShapeDtypeStruct((SHARE, 512, 2 * D), BF),
            jax.ShapeDtypeStruct((SHARE, 512, 2 * D), BF),
        ],
        scratch_shapes=[
            pltpu.VMEM((SHARE, 4, TOKENS, 128), F32),
            pltpu.VMEM((SHARE, TOKENS, 128), F32),
            pltpu.VMEM((SHARE, TOKENS, 128), F32),
        ],
        input_output_aliases={7 + i: i for i in range(len(before))},
        cost_estimate=pl.CostEstimate(flops=16 * 10**9, bytes_accessed=60 * 10**6, transcendentals=4 * 10**6),
        compiler_params=pltpu.CompilerParams(vmem_limit_bytes=48 * 1024 * 1024),
    )(offs, q, g, pair, far, own, other, *before, *after)


def routes(count):
    def along_z(i, step):
        z = ((i & 1) * 2 + (i >> 2 & 1) + step) % 4
        return (i & ~5) | (z & 1) << 2 | z >> 1

    table = {
        "head": lambda i: i ^ 1,
        "core": lambda i: i ^ 2,
        "up": lambda i: along_z(i, 1),
        "down": lambda i: along_z(i, -1),
        "x1": lambda i: i ^ 8,
        "x2": lambda i: i ^ 16,
        "x3": lambda i: i ^ 24,
    }
    return {name: [(i, to(i)) for i in range(count)] for name, to in table.items()}


def shards(count, queries, key_rows, value_rows, gradient, level_offsets):
    route = routes(count)

    def send(x, name):
        return lax.ppermute(x, AXES, route[name])

    other_offsets = send(level_offsets, "head")
    low = lax.axis_index("head") == 0
    offs = jnp.where(
        low,
        jnp.concatenate([level_offsets, other_offsets], 1),
        jnp.concatenate([other_offsets, level_offsets], 1),
    )
    rows = lambda n, dtype=BF: ((SHARE, n, 2 * D), dtype)
    bases = [part * SHARE for part in range(PARTS)]
    span = SHARE * D
    pairs = [
        jnp.concatenate([x[:, part * span : (part + 1) * span] for x in (key_rows, value_rows)], 1)
        for part in range(PARTS)
    ]

    gathered = []
    follow = offs
    for base, pair in zip(bases, pairs):
        pair_sent, _ = lax.optimization_barrier((pair, follow))
        far_pair = send(pair_sent, "head")
        first, middle, tail, last = whole_call(
            functools.partial(select_kernel, base), "select", [rows(64), rows(64), rows(32), rows(16)], offs, pair
        )
        follow = middle
        gathered.append((far_pair, first, middle, send(tail, "x1"), send(last, "x2"), send(last, "x3")))

    packed = []
    last_middle = gathered[-1][2]
    for _, first, middle, one, two, three in gathered:
        middle_down = send(middle, "up")
        middle_up = send(middle, "down")
        (extra,) = whole_call(compact_kernel, "compact", [rows(48)], None, one, two, three, after=(last_middle,))
        received = (send(extra, "head"), middle_up, send(extra, "down"), middle_down, send(extra, "up"))
        packed.append((first, middle, extra, received))

    before, after, turn, first_done = (), (packed[-1][2],), (), ()
    returned = []
    for base, pair, (far_pair, *_), (first, middle, extra, received) in zip(bases, pairs, gathered, packed):
        (own,) = whole_call(
            functools.partial(assemble_kernel, base), "assemble", [rows(512)], offs, first, middle, extra,
            far_pair, *received, after=first_done,
        )
        other = send(own, "core")
        attended, grad_queries, d0, down_own, down_other = attention(
            base, offs, queries, gradient, pair, far_pair, own, other, before, after
        )
        before, first_done = (attended, grad_queries), (d0,)
        down_other, _ = lax.optimization_barrier((down_other, turn))
        theirs = send(down_other, "core")
        rows_kept, rows_far, up, down, x_far, x_kept = whole_call(
            reduce_kernel, "reduce", [rows(128), rows(128), rows(112), rows(112), rows(48), rows(48, F32)],
            None, down_own, theirs,
        )
        from_down = send(up, "up")
        from_up = send(down, "down")
        x_far = send(x_far, "head")
        (far,) = whole_call(
            functools.partial(place_kernel, base), "place", [rows(128)], offs, d0, rows_far, after=(x_far,)
        )
        after = (far,)
        far = send(far, "head")
        turn = (from_down, from_up)
        one, two, three = whole_call(
            cross_kernel, "cross", [rows(32), rows(16), rows(16)], None, x_kept, x_far, from_up, from_down
        )
        one, two, three = send(one, "x1"), send(two, "x2"), send(three, "x3")
        returned.append((d0, rows_kept, far, from_up, from_down, one, two, three))

    grads = ()
    for base, arrays in zip(bases, returned):
        out = ((TOKENS, (base + SHARE) * D), BF)
        grads = whole_call(
            functools.partial(finish_kernel, base), "finish", [out, out], offs, *arrays, *grads
        )
    return (attended, grad_queries, *grads)


def solution(mesh):
    rows = P(AXES, None)
    return jax.shard_map(
        functools.partial(shards, mesh.size),
        mesh=mesh,
        in_specs=(rows, rows, rows, rows, P(None, "head")),
        out_specs=(rows, rows, rows, rows),
        check_vma=False,
    )
```

```python
import functools

import jax
import jax.numpy as jnp
from jax import lax
from jax.experimental import pallas as pl
from jax.experimental.pallas import tpu as pltpu
from jax.sharding import PartitionSpec as P

D = 128
GROUPS = 8
HEADS = 4
TOKENS = 128
TOGETHER = 4
WIDE = HEADS * D
SCALE = D ** (-0.5)
LOG2E = 1.4426950408889634
AXES = ("ctx", "head")
BF = jnp.bfloat16
F32 = jnp.float32
ANY_ROWS = ((0, 64, 1), (64, 96, 2), (96, 112, 3), (112, 120, 4))
VMEM_LIMIT = 24 * 1024 * 1024
GRID_LIMIT = 61 * 1024 * 1024


def dot(a, b):
    return lax.dot_general(a, b, (((1,), (0,)), ((), ())), preferred_element_type=F32)


def dot_nt(a, b):
    return lax.dot_general(a, b, (((1,), (1,)), ((), ())), preferred_element_type=F32)


def dot_tn(a, b):
    return lax.dot_general(a, b, (((0,), (0,)), ((), ())), preferred_element_type=F32)


def one_hot(mask):
    return jnp.where(mask, 1.0, 0.0).astype(BF)


def selected_token(row, offs, group):
    token = jnp.full(row.shape, -1, jnp.int32)
    for start, stop, level in ANY_ROWS:
        inside = (row >= start) & (row < stop)
        token = jnp.where(inside, (row - start) * 2**level + offs[level, group], token)
    return token


def selector(offs, group):
    shape = (128, TOKENS)
    row = lax.broadcasted_iota(jnp.int32, shape, 0)
    return one_hot(selected_token(row, offs, group) == lax.broadcasted_iota(jnp.int32, shape, 1))


def placer(offs, group):
    shape = (TOKENS, 128)
    row = lax.broadcasted_iota(jnp.int32, shape, 1)
    return one_hot(selected_token(row, offs, group) == lax.broadcasted_iota(jnp.int32, shape, 0))


def group_rows(keys_ref, values_ref, group):
    lanes = slice(group * D, (group + 1) * D)
    return jnp.concatenate([keys_ref[:, lanes], values_ref[:, lanes]], 1)


def select_kernel(offs, keys, values, first, middle, tail, last):
    for g in range(GROUPS):
        rows = dot(selector(offs, g), group_rows(keys, values, g))
        first[g] = rows[0:64].astype(BF)
        middle[g] = rows[64:128].astype(BF)
        tail[g] = rows[96:128].astype(BF)
        last[g] = rows[112:128].astype(BF)


def compact_kernel(middle, one, two, three, lift, extra):
    for g in range(GROUPS):
        mine, a, b, c = [ref[g].astype(F32) for ref in (middle, one, two, three)]
        last = [a[16:24], b[:8], c[:8]]
        lift[g] = jnp.concatenate([mine[0:48], a[0:16], mine[48:56]] + last, 0).astype(BF)
        extra[g] = jnp.concatenate([a[0:16]] + last + [jnp.zeros((8, 2 * D), F32)], 0).astype(BF)


def assemble_kernel(offs, first, lift, keys, values, x_far, lift_up, lift_down, _, held):
    for g in range(GROUPS):
        far = dot(selector(offs, g), group_rows(keys, values, g))
        extra = x_far[g].astype(F32)
        across = jnp.concatenate([far[64:112], extra[0:16], far[112:120], extra[16:40]], 0)
        lifts = [lift[g].astype(F32), across, lift_up[g].astype(F32), lift_down[g].astype(F32)]
        rows = [first[g].astype(F32), far[0:64]]
        for a, b in ((0, 32), (32, 64), (64, 96)):
            rows += [x[a:b] for x in lifts]
        held[g] = jnp.concatenate(rows, 0).astype(BF)


def by_level(rows):
    parts = []
    for start, stop in ((0, 64), (64, 96), (96, 112), (112, 120), (120, 128)):
        parts += [rows[start:stop, h * D : (h + 1) * D] for h in range(HEADS)]
    return jnp.concatenate(parts, 0)


def by_selection(rows):
    heads = []
    for h in range(HEADS):
        parts = []
        base = 0
        for count in (64, 32, 16, 8, 8):
            parts.append(rows[base + h * count : base + (h + 1) * count])
            base += HEADS * count
        heads.append(jnp.concatenate(parts, 0))
    return jnp.concatenate(heads, 1)


def heads_to_lanes(x):
    count = x.shape[0] // HEADS
    lane = lax.broadcasted_iota(jnp.int32, (count, 128), 1) & (HEADS - 1)
    out = x[(HEADS - 1) * count :]
    for h in range(HEADS - 1):
        out = jnp.where(lane == h, x[h * count : (h + 1) * count], out)
    return out


def wide_lanes(j):
    return slice(j * WIDE, (j + 1) * WIDE)


def by_head(rows):
    return jnp.concatenate([rows[:, h * D : (h + 1) * D] for h in range(HEADS)], 0)


def by_token(rows):
    count = rows.shape[0] // HEADS
    return jnp.concatenate([rows[h * count : (h + 1) * count] for h in range(HEADS)], 1)


def expand(x):
    return jnp.concatenate([jnp.broadcast_to(x[:, h : h + 1], x.shape) for h in range(HEADS)], 0)


def beside(x):
    high = x.astype(BF).astype(F32)
    lane = lax.broadcasted_iota(jnp.int32, x.shape, 1)
    both = jnp.where(lane < 64, high, x - high)
    return jnp.concatenate(
        [jnp.where((lane & (HEADS - 1)) == h, both, 0.0) for h in range(HEADS)], 0
    ).astype(BF)


def minus_lanes():
    lane = lax.broadcasted_iota(jnp.int32, (2 * D, D), 1)
    return jnp.where((lane & 63) < HEADS, -1.0, 0.0).astype(BF)


def forward(queries, keys, values):
    ones = jnp.ones((2 * D, D), BF)
    scores = [dot_nt(q, k) * (SCALE * LOG2E) for q, k in zip(queries, keys)]
    peaks = [jnp.max(x, 1, keepdims=True) for x in scores]
    powers = [jnp.exp2(x - p).astype(BF) for x, p in zip(scores, peaks)]
    outs = [dot(p, jnp.concatenate([v, ones], 1)) for p, v in zip(powers, values)]
    peaks = [heads_to_lanes(jnp.broadcast_to(p, (p.shape[0], 128))) for p in peaks]
    lses = [p + jnp.log2(heads_to_lanes(out[:, D:])) for p, out in zip(peaks, outs)]
    return powers, peaks, lses, [out[:, :D] for out in outs]


def backward(queries, scaled, keys, values, powers, shifts):
    minus = minus_lanes()
    weights = [
        dot_nt(jnp.concatenate([g, beside(d)], 1), jnp.concatenate([v, minus], 1))
        for g, d, v in zip(scaled, shifts, values)
    ]
    scores = [(p.astype(F32) * w).astype(BF) for p, w in zip(powers, weights)]
    grad_values = [dot_tn(g, p).T for g, p in zip(scaled, powers)]
    grad_keys = [dot_tn(q, x).T * SCALE for q, x in zip(queries, scores)]
    pairs = [jnp.concatenate(pair, 1).astype(BF) for pair in zip(grad_keys, grad_values)]
    return pairs, [dot(x, k) * SCALE for x, k in zip(scores, keys)]


def whole_rows(own_ref, far_ref, j):
    lanes = slice(j * D, (j + 1) * D)
    return jnp.concatenate([own_ref[:, lanes], far_ref[:, lanes]], 0)


def level0_kernel(q_ref, k_ref, v_ref, kp_ref, vp_ref, *refs):
    power_ref, peak_ref, lse_ref, out_ref = refs[-4:]
    members = range(TOGETHER)
    queries = [by_head(q_ref[:, wide_lanes(j)]) for j in members]
    keys = [whole_rows(k_ref, kp_ref, j) for j in members]
    values = [whole_rows(v_ref, vp_ref, j) for j in members]
    for j, (power, peak, lse, out) in enumerate(zip(*forward(queries, keys, values))):
        power_ref[j], peak_ref[j], lse_ref[j], out_ref[j] = power, peak, lse, out


def attention_kernel(
    offs, q_ref, g_ref, own_ref, other_ref, peak_ref, lse_ref, out_ref,
    att_ref, part_ref, down_ref, dother_ref, factor_ref, shift_ref, level_ref, token_ref, delta_ref,
):
    members = range(TOGETHER)
    first_group = pl.program_id(0) * TOGETHER
    bounds = ((0, 256), (256, 384), (384, 448), (448, 480))
    starts = [[(offs[k, first_group + j], 128 >> k) for k in range(1, 5)] for j in members]

    def selected(ref):
        rows = [dot(selector(offs, first_group + j), ref[:, wide_lanes(j)]) for j in members]
        rows = [by_level(x).astype(BF) for x in rows]
        return [[x[a:b] for x in rows] for a, b in bounds]

    def kept(k, lanes):
        at = slice(128 * k, 128 * k + 128)
        return [jnp.concatenate([own_ref[j, at, lanes], other_ref[j, at, lanes]], 0) for j in members]

    def for_levels(ref, xs):
        for j, x in enumerate(xs):
            ref[j] = x
        return [
            [ref[j, pl.ds(starts[j][k][0], starts[j][k][1], 2 ** (k + 1)), :] for j in members]
            for k in range(4)
        ]

    def place(parts):
        rows = [jnp.concatenate(list(p) + [jnp.zeros((32, D), F32)], 0) for p in zip(*parts)]
        rows = [by_selection(x).astype(BF) for x in rows]
        return [dot(placer(offs, first_group + j), r) for j, r in enumerate(rows)]

    level_ref[...] = jnp.full(level_ref.shape, -1e30, F32)
    queries, grads = selected(q_ref), selected(g_ref)
    keys = [kept(k, slice(0, D)) for k in range(4)]
    values = [kept(k, slice(D, 2 * D)) for k in range(4)]
    results = [forward(queries[k], keys[k], values[k]) for k in range(4)]

    for k in range(4):
        for j in members:
            start, count = starts[j][k]
            level_ref[j, k, pl.ds(start, count, 2 ** (k + 1)), :] = results[k][2][j]
    firsts = [lse_ref[j] for j in members]
    tops = [functools.reduce(jnp.maximum, [level_ref[j, k] for k in range(4)], firsts[j]) for j in members]
    sums = [
        jnp.exp2(firsts[j] - tops[j]) + sum(jnp.exp2(level_ref[j, k] - tops[j]) for k in range(4))
        for j in members
    ]
    merged = [top + jnp.log2(x) for top, x in zip(tops, sums)]
    factors = [
        [jnp.exp2(p - m) for p, m in zip(results[k][1], column)]
        for k, column in enumerate(for_levels(token_ref, merged))
    ]
    spread = [[expand(f) for f in fs] for fs in factors]
    placed = place([[out * f for out, f in zip(results[k][3], spread[k])] for k in range(4)])
    deltas = []
    for j in members:
        factor = jnp.exp2(peak_ref[j] - merged[j])
        attended = (placed[j] + by_token(out_ref[j] * expand(factor))).astype(BF)
        att_ref[:, wide_lanes(j)] = attended
        product = g_ref[:, wide_lanes(j)].astype(F32) * attended.astype(F32)
        total = [
            jnp.broadcast_to(jnp.sum(product[:, h * D : (h + 1) * D], 1, keepdims=True), (TOKENS, 128))
            for h in range(HEADS)
        ]
        deltas.append(heads_to_lanes(jnp.concatenate(total, 0)))
        factor_ref[j] = factor
        shift_ref[j] = factor * deltas[j]
    shifts = [
        [f * d for f, d in zip(factors[k], column)] for k, column in enumerate(for_levels(delta_ref, deltas))
    ]
    scaled = [
        [(g.astype(F32) * f).astype(BF) for g, f in zip(grads[k], spread[k])] for k in range(4)
    ]
    parts = []
    for k in range(4):
        pairs, part = backward(queries[k], scaled[k], keys[k], values[k], results[k][0], shifts[k])
        parts.append(part)
        for j in members:
            down_ref[j, 128 * k : 128 * k + 128] = pairs[j][:128]
            dother_ref[j, 128 * k : 128 * k + 128] = pairs[j][128:]
    for j, x in enumerate(place(parts)):
        part_ref[:, wide_lanes(j)] = x


def return0_kernel(
    q_ref, g_ref, k_ref, v_ref, kp_ref, vp_ref, power_ref, factor_ref, shift_ref, part_ref, *refs
):
    dq_ref, d0_ref = refs[-2:]
    members = range(TOGETHER)
    queries = [by_head(q_ref[:, wide_lanes(j)]) for j in members]
    keys = [whole_rows(k_ref, kp_ref, j) for j in members]
    values = [whole_rows(v_ref, vp_ref, j) for j in members]
    scaled = [
        (by_head(g_ref[:, wide_lanes(j)]).astype(F32) * expand(factor_ref[j])).astype(BF) for j in members
    ]
    powers, shifts = [power_ref[j] for j in members], [shift_ref[j] for j in members]
    pairs, parts = backward(queries, scaled, keys, values, powers, shifts)
    for j in members:
        d0_ref[j] = pairs[j]
        dq_ref[:, wide_lanes(j)] = (by_token(parts[j]) + part_ref[:, wide_lanes(j)]).astype(BF)


def reduce_kernel(mine, theirs, rows_kept, rows_far, up, down, x_far, x_kept):
    zero = jnp.zeros((8, 2 * D), F32)
    for g in range(GROUPS):
        total = mine[g].astype(F32) + theirs[g].astype(F32)
        for z, ref in enumerate((rows_kept, rows_far, up, down)):
            second, third, fourth = [total[s + 32 * z : s + 32 * z + 32] for s in (128, 256, 384)]
            if z >= 2:
                ref[g] = jnp.concatenate([second, third, fourth], 0).astype(BF)
                continue
            rows = [total[64 * z : 64 * z + 64], second, third[:16], fourth[:8], zero]
            ref[g] = jnp.concatenate(rows, 0).astype(BF)
            extra = jnp.concatenate([third[16:], fourth[8:], zero], 0)
            if z == 0:
                x_kept[g] = extra
            else:
                x_far[g] = extra.astype(BF)


def place_kernel(offs, d0, rows_far, far):
    for g in range(GROUPS):
        far[g] = (d0[g, 128:256].astype(F32) + dot(placer(offs, g), rows_far[g])).astype(BF)


def cross_kernel(kept, far, up, down, one, two, three):
    zero = jnp.zeros((8, 2 * D), F32)
    for g in range(GROUPS):
        sides = up[g].astype(F32) + down[g].astype(F32)
        total = kept[g] + far[g].astype(F32)
        third = total[0:16] + sides[48:64]
        fourth = total[16:40] + sides[72:96]
        one[g] = jnp.concatenate([third, fourth[0:8], zero], 0).astype(BF)
        two[g] = jnp.concatenate([fourth[8:16], zero], 0).astype(BF)
        three[g] = jnp.concatenate([fourth[16:24], zero], 0).astype(BF)


def finish_kernel(offs, d0, rows_kept, far, up, down, one, two, three, dk_ref, dv_ref):
    for g in range(GROUPS):
        kept = rows_kept[g].astype(F32)
        sides = up[g].astype(F32) + down[g].astype(F32)
        a, b, c = one[g].astype(F32), two[g].astype(F32), three[g].astype(F32)
        rows = jnp.concatenate(
            [
                kept[0:64],
                kept[64:96] + sides[0:32],
                kept[96:112] + sides[32:48] + a[0:16],
                kept[112:120] + sides[64:72] + a[16:24] + b[0:8] + c[0:8],
                jnp.zeros((8, 2 * D), F32),
            ],
            0,
        ).astype(BF)
        whole = d0[g, 0:128].astype(F32) + far[g].astype(F32) + dot(placer(offs, g), rows)
        dk_ref[:, g * D : (g + 1) * D] = whole[:, :D].astype(BF)
        dv_ref[:, g * D : (g + 1) * D] = whole[:, D:].astype(BF)


def whole_call(body, name, outs, offs, *arrays, after=()):
    specs = [pl.BlockSpec(memory_space=pltpu.VMEM)] * len(arrays)
    specs += [pl.BlockSpec(memory_space=pl.ANY)] * len(after)
    arrays = arrays + tuple(after)
    if offs is not None:
        specs = [pl.BlockSpec(memory_space=pltpu.SMEM)] + specs
        arrays = (offs,) + arrays
    shapes = [jax.ShapeDtypeStruct(shape, dtype) for shape, dtype in outs]
    return pl.pallas_call(
        body,
        name=name,
        out_shape=shapes,
        in_specs=specs,
        out_specs=[pl.BlockSpec(memory_space=pltpu.VMEM)] * len(shapes),
        cost_estimate=pl.CostEstimate(flops=0, bytes_accessed=4 * 10**6, transcendentals=0),
        compiler_params=pltpu.CompilerParams(vmem_limit_bytes=VMEM_LIMIT),
    )(*arrays)


def grid_call(body, name, offs, inputs, outs, scratch=(), after=()):
    def spec(shape):
        if len(shape) == 2:
            return pl.BlockSpec((TOKENS, shape[1] * TOGETHER // GROUPS), lambda i: (0, i))
        return pl.BlockSpec((TOGETHER,) + shape[1:], lambda i: (i, 0, 0))

    specs = [spec(x.shape) for x in inputs] + [pl.BlockSpec(memory_space=pl.ANY)] * len(after)
    arrays = tuple(inputs) + tuple(after)
    if offs is not None:
        specs = [pl.BlockSpec(memory_space=pltpu.SMEM)] + specs
        arrays = (offs,) + arrays
    return pl.pallas_call(
        body,
        name=name,
        grid=(GROUPS // TOGETHER,),
        in_specs=specs,
        out_specs=[spec(shape) for shape, _ in outs],
        out_shape=[jax.ShapeDtypeStruct(shape, dtype) for shape, dtype in outs],
        scratch_shapes=list(scratch),
        cost_estimate=pl.CostEstimate(flops=4 * 10**9, bytes_accessed=16 * 10**6, transcendentals=10**6),
        compiler_params=pltpu.CompilerParams(vmem_limit_bytes=GRID_LIMIT),
    )(*arrays)


def routes(count):
    def along_z(i, step):
        z = ((i & 1) * 2 + (i >> 2 & 1) + step) % 4
        return (i & ~5) | (z & 1) << 2 | z >> 1

    table = {
        "head": lambda i: i ^ 1,
        "core": lambda i: i ^ 2,
        "up": lambda i: along_z(i, 1),
        "down": lambda i: along_z(i, -1),
        "x1": lambda i: i ^ 8,
        "x2": lambda i: i ^ 16,
        "x3": lambda i: i ^ 24,
    }
    return {name: [(i, to(i)) for i in range(count)] for name, to in table.items()}


def shards(count, queries, key_rows, value_rows, gradient, level_offsets):
    route = routes(count)

    def send(x, name):
        return lax.ppermute(x, AXES, route[name])

    other_offsets = send(level_offsets, "head")
    low = lax.axis_index("head") == 0
    offs = jnp.where(
        low,
        jnp.concatenate([level_offsets, other_offsets], 1),
        jnp.concatenate([other_offsets, level_offsets], 1),
    )
    key_swap, value_swap, other_offsets = lax.optimization_barrier((key_rows, value_rows, other_offsets))
    far_keys = send(key_swap, "head")
    far_values = send(value_swap, "head")

    rows = lambda n, dtype=BF: ((GROUPS, n, 2 * D), dtype)
    packed = ((GROUPS, TOKENS, 128), F32)
    wide = lambda dtype: ((TOKENS, GROUPS * WIDE), dtype)
    first, middle, tail, last = whole_call(
        select_kernel, "select", [rows(64), rows(64), rows(32), rows(16)], offs, key_rows, value_rows
    )
    lift, extra = whole_call(
        compact_kernel, "compact", [rows(96), rows(48)], None,
        middle, send(tail, "x1"), send(last, "x2"), send(last, "x3"),
    )
    lift_down = send(lift, "up")
    lift_up = send(lift, "down")
    extra_far = send(extra, "head")
    power0, peak0, lse0, out0 = grid_call(
        level0_kernel, "level0", None, [queries, key_rows, value_rows, far_keys, far_values],
        [rows(512), packed, packed, ((GROUPS, 512, 128), F32)], after=(extra,),
    )
    (own,) = whole_call(
        assemble_kernel, "assemble", [rows(512)], offs, first, lift, far_keys, far_values,
        extra_far, lift_up, lift_down, after=(lse0,),
    )
    other = send(own, "core")
    stats = pltpu.VMEM((TOGETHER, TOKENS, 128), F32)
    attended, part, down_own, down_other, factor0, shift0 = grid_call(
        attention_kernel, "attention", offs, [queries, gradient, own, other, peak0, lse0, out0],
        [wide(BF), wide(F32), rows(512), rows(512), packed, packed],
        scratch=[pltpu.VMEM((TOGETHER, 4, TOKENS, 128), F32), stats, stats],
    )
    theirs = send(down_other, "core")
    rows_kept, rows_far, up, down, x_far, x_kept = whole_call(
        reduce_kernel, "reduce", [rows(128), rows(128), rows(96), rows(96), rows(48), rows(48, F32)],
        None, down_own, theirs,
    )
    from_down = send(up, "up")
    from_up = send(down, "down")
    x_far = send(x_far, "head")
    grad_queries, d0 = grid_call(
        return0_kernel, "return0", None,
        [queries, gradient, key_rows, value_rows, far_keys, far_values, power0, factor0, shift0, part],
        [wide(BF), rows(256)], after=(x_far,),
    )
    (far,) = whole_call(place_kernel, "place", [rows(128)], offs, d0, rows_far)
    far = send(far, "head")
    one, two, three = whole_call(
        cross_kernel, "cross", [rows(32), rows(16), rows(16)], None, x_kept, x_far, from_up, from_down
    )
    one, two, three = send(one, "x1"), send(two, "x2"), send(three, "x3")
    out = ((TOKENS, GROUPS * D), BF)
    grad_keys, grad_values = whole_call(
        finish_kernel, "finish", [out, out], offs, d0, rows_kept, far, from_up, from_down, one, two, three
    )
    return (attended, grad_queries, grad_keys, grad_values)


def solution(mesh):
    rows = P(AXES, None)
    return jax.shard_map(
        functools.partial(shards, mesh.size),
        mesh=mesh,
        in_specs=(rows, rows, rows, rows, P(None, "head")),
        out_specs=(rows, rows, rows, rows),
        check_vma=False,
    )
```

```python
import functools

import jax
import jax.numpy as jnp
from jax import lax
from jax.experimental import pallas as pl
from jax.experimental.pallas import tpu as pltpu
from jax.sharding import PartitionSpec as P

D = 128
GROUPS = 8
HEADS = 4
TOKENS = 128
TOGETHER = 4
WIDE = HEADS * D
SCALE = D ** (-0.5)
LOG2E = 1.4426950408889634
AXES = ("ctx", "head")
BF = jnp.bfloat16
F32 = jnp.float32
ANY_ROWS = ((0, 64, 1), (64, 96, 2), (96, 112, 3), (112, 120, 4))
VMEM_LIMIT = 24 * 1024 * 1024
GRID_LIMIT = 32 * 1024 * 1024


def dot(a, b):
    return lax.dot_general(a, b, (((1,), (0,)), ((), ())), preferred_element_type=F32)


def dot_nt(a, b):
    return lax.dot_general(a, b, (((1,), (1,)), ((), ())), preferred_element_type=F32)


def dot_tn(a, b):
    return lax.dot_general(a, b, (((0,), (0,)), ((), ())), preferred_element_type=F32)


def one_hot(mask):
    return jnp.where(mask, 1.0, 0.0).astype(BF)


def selected_token(row, offs, group):
    token = jnp.full(row.shape, -1, jnp.int32)
    for start, stop, level in ANY_ROWS:
        inside = (row >= start) & (row < stop)
        token = jnp.where(inside, (row - start) * 2**level + offs[level, group], token)
    return token


def selector(offs, group):
    shape = (128, TOKENS)
    row = lax.broadcasted_iota(jnp.int32, shape, 0)
    return one_hot(selected_token(row, offs, group) == lax.broadcasted_iota(jnp.int32, shape, 1))


def placer(offs, group):
    shape = (TOKENS, 128)
    row = lax.broadcasted_iota(jnp.int32, shape, 1)
    return one_hot(selected_token(row, offs, group) == lax.broadcasted_iota(jnp.int32, shape, 0))


def group_rows(keys_ref, values_ref, group):
    lanes = slice(group * D, (group + 1) * D)
    return jnp.concatenate([keys_ref[:, lanes], values_ref[:, lanes]], 1)


def select_kernel(offs, keys, values, first, middle, tail, last):
    first_group = pl.program_id(0) * TOGETHER
    for j in range(TOGETHER):
        rows = dot(selector(offs, first_group + j), group_rows(keys, values, j))
        first[j] = rows[0:64].astype(BF)
        middle[j] = rows[64:128].astype(BF)
        tail[j] = rows[96:128].astype(BF)
        last[j] = rows[112:128].astype(BF)


def compact_kernel(middle, one, two, three, lift, extra):
    for g in range(GROUPS):
        mine, a, b, c = [ref[g].astype(F32) for ref in (middle, one, two, three)]
        last = [a[16:24], b[:8], c[:8]]
        lift[g] = jnp.concatenate([mine[0:48], a[0:16], mine[48:56]] + last, 0).astype(BF)
        extra[g] = jnp.concatenate([a[0:16]] + last + [jnp.zeros((8, 2 * D), F32)], 0).astype(BF)


def assemble_kernel(offs, first, lift, keys, values, x_far, lift_up, lift_down, _, held):
    for g in range(GROUPS):
        far = dot(selector(offs, g), group_rows(keys, values, g))
        extra = x_far[g].astype(F32)
        across = jnp.concatenate([far[64:112], extra[0:16], far[112:120], extra[16:40]], 0)
        lifts = [lift[g].astype(F32), across, lift_up[g].astype(F32), lift_down[g].astype(F32)]
        rows = [first[g].astype(F32), far[0:64]]
        for a, b in ((0, 32), (32, 64), (64, 96)):
            rows += [x[a:b] for x in lifts]
        held[g] = jnp.concatenate(rows, 0).astype(BF)


def by_level(rows):
    parts = []
    for start, stop in ((0, 64), (64, 96), (96, 112), (112, 120), (120, 128)):
        parts += [rows[start:stop, h * D : (h + 1) * D] for h in range(HEADS)]
    return jnp.concatenate(parts, 0)


def by_selection(rows):
    heads = []
    for h in range(HEADS):
        parts = []
        base = 0
        for count in (64, 32, 16, 8, 8):
            parts.append(rows[base + h * count : base + (h + 1) * count])
            base += HEADS * count
        heads.append(jnp.concatenate(parts, 0))
    return jnp.concatenate(heads, 1)


def heads_to_lanes(x):
    count = x.shape[0] // HEADS
    lane = lax.broadcasted_iota(jnp.int32, (count, 128), 1) & (HEADS - 1)
    out = x[(HEADS - 1) * count :]
    for h in range(HEADS - 1):
        out = jnp.where(lane == h, x[h * count : (h + 1) * count], out)
    return out


def wide_lanes(j):
    return slice(j * WIDE, (j + 1) * WIDE)


def by_head(rows):
    return jnp.concatenate([rows[:, h * D : (h + 1) * D] for h in range(HEADS)], 0)


def by_token(rows):
    count = rows.shape[0] // HEADS
    return jnp.concatenate([rows[h * count : (h + 1) * count] for h in range(HEADS)], 1)


def expand(x):
    return jnp.concatenate([jnp.broadcast_to(x[:, h : h + 1], x.shape) for h in range(HEADS)], 0)


def beside(x):
    high = x.astype(BF).astype(F32)
    lane = lax.broadcasted_iota(jnp.int32, x.shape, 1)
    both = jnp.where(lane < 64, high, x - high)
    return jnp.concatenate(
        [jnp.where((lane & (HEADS - 1)) == h, both, 0.0) for h in range(HEADS)], 0
    ).astype(BF)


def minus_lanes():
    lane = lax.broadcasted_iota(jnp.int32, (2 * D, D), 1)
    return jnp.where((lane & 63) < HEADS, -1.0, 0.0).astype(BF)


def forward(queries, keys, values):
    ones = jnp.ones((2 * D, D), BF)
    scores = [dot_nt(q, k) * (SCALE * LOG2E) for q, k in zip(queries, keys)]
    peaks = [jnp.max(x, 1, keepdims=True) for x in scores]
    powers = [jnp.exp2(x - p).astype(BF) for x, p in zip(scores, peaks)]
    outs = [dot(p, jnp.concatenate([v, ones], 1)) for p, v in zip(powers, values)]
    peaks = [heads_to_lanes(jnp.broadcast_to(p, (p.shape[0], 128))) for p in peaks]
    lses = [p + jnp.log2(heads_to_lanes(out[:, D:])) for p, out in zip(peaks, outs)]
    return powers, peaks, lses, [out[:, :D] for out in outs]


def backward(queries, scaled, keys, values, powers, shifts):
    minus = minus_lanes()
    weights = [
        dot_nt(jnp.concatenate([g, beside(d)], 1), jnp.concatenate([v, minus], 1))
        for g, d, v in zip(scaled, shifts, values)
    ]
    scores = [(p.astype(F32) * w).astype(BF) for p, w in zip(powers, weights)]
    grad_values = [dot_tn(g, p).T for g, p in zip(scaled, powers)]
    grad_keys = [dot_tn(q, x).T * SCALE for q, x in zip(queries, scores)]
    pairs = [jnp.concatenate(pair, 1).astype(BF) for pair in zip(grad_keys, grad_values)]
    return pairs, [dot(x, k) * SCALE for x, k in zip(scores, keys)]


def whole_rows(own_ref, far_ref, j):
    lanes = slice(j * D, (j + 1) * D)
    return jnp.concatenate([own_ref[:, lanes], far_ref[:, lanes]], 0)


def level0_kernel(q_ref, k_ref, v_ref, kp_ref, vp_ref, *refs):
    power_ref, peak_ref, lse_ref, out_ref = refs[-4:]
    members = range(TOGETHER)
    queries = [by_head(q_ref[:, wide_lanes(j)]) for j in members]
    keys = [whole_rows(k_ref, kp_ref, j) for j in members]
    values = [whole_rows(v_ref, vp_ref, j) for j in members]
    for j, (power, peak, lse, out) in enumerate(zip(*forward(queries, keys, values))):
        power_ref[j], peak_ref[j], lse_ref[j], out_ref[j] = power, peak, lse, out


def attention_kernel(
    offs, q_ref, g_ref, own_ref, other_ref, peak_ref, lse_ref, out_ref,
    att_ref, part_ref, down_ref, dother_ref, factor_ref, shift_ref, level_ref, token_ref, delta_ref,
):
    members = range(TOGETHER)
    first_group = pl.program_id(0) * TOGETHER
    bounds = ((0, 256), (256, 384), (384, 448), (448, 480))
    starts = [[(offs[k, first_group + j], 128 >> k) for k in range(1, 5)] for j in members]

    def selected(ref):
        rows = [dot(selector(offs, first_group + j), ref[:, wide_lanes(j)]) for j in members]
        rows = [by_level(x).astype(BF) for x in rows]
        return [[x[a:b] for x in rows] for a, b in bounds]

    def kept(k, lanes):
        at = slice(128 * k, 128 * k + 128)
        return [jnp.concatenate([own_ref[j, at, lanes], other_ref[j, at, lanes]], 0) for j in members]

    def for_levels(ref, xs):
        for j, x in enumerate(xs):
            ref[j] = x
        return [
            [ref[j, pl.ds(starts[j][k][0], starts[j][k][1], 2 ** (k + 1)), :] for j in members]
            for k in range(4)
        ]

    def place(parts):
        rows = [jnp.concatenate(list(p) + [jnp.zeros((32, D), F32)], 0) for p in zip(*parts)]
        rows = [by_selection(x).astype(BF) for x in rows]
        return [dot(placer(offs, first_group + j), r) for j, r in enumerate(rows)]

    level_ref[...] = jnp.full(level_ref.shape, -1e30, F32)
    queries, grads = selected(q_ref), selected(g_ref)
    keys = [kept(k, slice(0, D)) for k in range(4)]
    values = [kept(k, slice(D, 2 * D)) for k in range(4)]
    results = [forward(queries[k], keys[k], values[k]) for k in range(4)]

    for k in range(4):
        for j in members:
            start, count = starts[j][k]
            level_ref[j, k, pl.ds(start, count, 2 ** (k + 1)), :] = results[k][2][j]
    firsts = [lse_ref[j] for j in members]
    tops = [functools.reduce(jnp.maximum, [level_ref[j, k] for k in range(4)], firsts[j]) for j in members]
    sums = [
        jnp.exp2(firsts[j] - tops[j]) + sum(jnp.exp2(level_ref[j, k] - tops[j]) for k in range(4))
        for j in members
    ]
    merged = [top + jnp.log2(x) for top, x in zip(tops, sums)]
    factors = [
        [jnp.exp2(p - m) for p, m in zip(results[k][1], column)]
        for k, column in enumerate(for_levels(token_ref, merged))
    ]
    spread = [[expand(f) for f in fs] for fs in factors]
    placed = place([[out * f for out, f in zip(results[k][3], spread[k])] for k in range(4)])
    deltas = []
    for j in members:
        factor = jnp.exp2(peak_ref[j] - merged[j])
        attended = (placed[j] + by_token(out_ref[j] * expand(factor))).astype(BF)
        att_ref[:, wide_lanes(j)] = attended
        product = g_ref[:, wide_lanes(j)].astype(F32) * attended.astype(F32)
        total = [
            jnp.broadcast_to(jnp.sum(product[:, h * D : (h + 1) * D], 1, keepdims=True), (TOKENS, 128))
            for h in range(HEADS)
        ]
        deltas.append(heads_to_lanes(jnp.concatenate(total, 0)))
        factor_ref[j] = factor
        shift_ref[j] = factor * deltas[j]
    shifts = [
        [f * d for f, d in zip(factors[k], column)] for k, column in enumerate(for_levels(delta_ref, deltas))
    ]
    scaled = [
        [(g.astype(F32) * f).astype(BF) for g, f in zip(grads[k], spread[k])] for k in range(4)
    ]
    parts = []
    for k in range(4):
        pairs, part = backward(queries[k], scaled[k], keys[k], values[k], results[k][0], shifts[k])
        parts.append(part)
        for j in members:
            down_ref[j, 128 * k : 128 * k + 128] = pairs[j][:128]
            dother_ref[j, 128 * k : 128 * k + 128] = pairs[j][128:]
    for j, x in enumerate(place(parts)):
        part_ref[:, wide_lanes(j)] = x


def return0_kernel(
    q_ref, g_ref, k_ref, v_ref, kp_ref, vp_ref, power_ref, factor_ref, shift_ref, part_ref, *refs
):
    dq_ref, d0_ref = refs[-2:]
    members = range(TOGETHER)
    queries = [by_head(q_ref[:, wide_lanes(j)]) for j in members]
    keys = [whole_rows(k_ref, kp_ref, j) for j in members]
    values = [whole_rows(v_ref, vp_ref, j) for j in members]
    scaled = [
        (by_head(g_ref[:, wide_lanes(j)]).astype(F32) * expand(factor_ref[j])).astype(BF) for j in members
    ]
    powers, shifts = [power_ref[j] for j in members], [shift_ref[j] for j in members]
    pairs, parts = backward(queries, scaled, keys, values, powers, shifts)
    for j in members:
        d0_ref[j] = pairs[j]
        dq_ref[:, wide_lanes(j)] = (by_token(parts[j]) + part_ref[:, wide_lanes(j)]).astype(BF)


def reduce_kernel(mine, theirs, _, rows_kept, rows_far, up, down, x_far, x_kept):
    zero = jnp.zeros((8, 2 * D), F32)
    for g in range(GROUPS):
        total = mine[g].astype(F32) + theirs[g].astype(F32)
        for z, ref in enumerate((rows_kept, rows_far, up, down)):
            second, third, fourth = [total[s + 32 * z : s + 32 * z + 32] for s in (128, 256, 384)]
            if z >= 2:
                ref[g] = jnp.concatenate([second, third, fourth], 0).astype(BF)
                continue
            rows = [total[64 * z : 64 * z + 64], second, third[:16], fourth[:8], zero]
            ref[g] = jnp.concatenate(rows, 0).astype(BF)
            extra = jnp.concatenate([third[16:], fourth[8:], zero], 0)
            if z == 0:
                x_kept[g] = extra
            else:
                x_far[g] = extra.astype(BF)


def place_kernel(offs, d0, rows_far, _, far):
    for g in range(GROUPS):
        far[g] = (d0[g, 128:256].astype(F32) + dot(placer(offs, g), rows_far[g])).astype(BF)


def cross_kernel(kept, far, up, down, one, two, three):
    zero = jnp.zeros((8, 2 * D), F32)
    for g in range(GROUPS):
        sides = up[g].astype(F32) + down[g].astype(F32)
        total = kept[g] + far[g].astype(F32)
        third = total[0:16] + sides[48:64]
        fourth = total[16:40] + sides[72:96]
        one[g] = jnp.concatenate([third, fourth[0:8], zero], 0).astype(BF)
        two[g] = jnp.concatenate([fourth[8:16], zero], 0).astype(BF)
        three[g] = jnp.concatenate([fourth[16:24], zero], 0).astype(BF)


def finish_kernel(offs, d0, rows_kept, far, up, down, one, two, three, dk_ref, dv_ref):
    for g in range(GROUPS):
        kept = rows_kept[g].astype(F32)
        sides = up[g].astype(F32) + down[g].astype(F32)
        a, b, c = one[g].astype(F32), two[g].astype(F32), three[g].astype(F32)
        rows = jnp.concatenate(
            [
                kept[0:64],
                kept[64:96] + sides[0:32],
                kept[96:112] + sides[32:48] + a[0:16],
                kept[112:120] + sides[64:72] + a[16:24] + b[0:8] + c[0:8],
                jnp.zeros((8, 2 * D), F32),
            ],
            0,
        ).astype(BF)
        whole = d0[g, 0:128].astype(F32) + far[g].astype(F32) + dot(placer(offs, g), rows)
        dk_ref[:, g * D : (g + 1) * D] = whole[:, :D].astype(BF)
        dv_ref[:, g * D : (g + 1) * D] = whole[:, D:].astype(BF)


def whole_call(body, name, outs, offs, *arrays, after=()):
    specs = [pl.BlockSpec(memory_space=pltpu.VMEM)] * len(arrays)
    specs += [pl.BlockSpec(memory_space=pl.ANY)] * len(after)
    arrays = arrays + tuple(after)
    if offs is not None:
        specs = [pl.BlockSpec(memory_space=pltpu.SMEM)] + specs
        arrays = (offs,) + arrays
    shapes = [jax.ShapeDtypeStruct(shape, dtype) for shape, dtype in outs]
    return pl.pallas_call(
        body,
        name=name,
        out_shape=shapes,
        in_specs=specs,
        out_specs=[pl.BlockSpec(memory_space=pltpu.VMEM)] * len(shapes),
        cost_estimate=pl.CostEstimate(flops=0, bytes_accessed=4 * 10**6, transcendentals=0),
        compiler_params=pltpu.CompilerParams(vmem_limit_bytes=VMEM_LIMIT),
    )(*arrays)


def grid_call(body, name, offs, inputs, outs, scratch=(), after=()):
    def spec(shape, offset=0):
        if offset:
            return pl.BlockSpec((TOKENS, TOGETHER * D), lambda i: (0, i + offset - 1))
        if len(shape) == 2:
            return pl.BlockSpec((TOKENS, shape[1] * TOGETHER // GROUPS), lambda i: (0, i))
        return pl.BlockSpec((TOGETHER,) + shape[1:], lambda i: (i, 0, 0))

    specs = [spec(x[0].shape, x[1]) if isinstance(x, tuple) else spec(x.shape) for x in inputs]
    inputs = [x[0] if isinstance(x, tuple) else x for x in inputs]
    specs += [pl.BlockSpec(memory_space=pl.ANY)] * len(after)
    arrays = tuple(inputs) + tuple(after)
    if offs is not None:
        specs = [pl.BlockSpec(memory_space=pltpu.SMEM)] + specs
        arrays = (offs,) + arrays
    return pl.pallas_call(
        body,
        name=name,
        grid=(GROUPS // TOGETHER,),
        in_specs=specs,
        out_specs=[spec(shape) for shape, _ in outs],
        out_shape=[jax.ShapeDtypeStruct(shape, dtype) for shape, dtype in outs],
        scratch_shapes=list(scratch),
        cost_estimate=pl.CostEstimate(flops=4 * 10**9, bytes_accessed=16 * 10**6, transcendentals=10**6),
        compiler_params=pltpu.CompilerParams(vmem_limit_bytes=GRID_LIMIT),
    )(*arrays)


def routes(count):
    def along_z(i, step):
        z = ((i & 1) * 2 + (i >> 2 & 1) + step) % 4
        return (i & ~5) | (z & 1) << 2 | z >> 1

    table = {
        "head": lambda i: i ^ 1,
        "core": lambda i: i ^ 2,
        "up": lambda i: along_z(i, 1),
        "down": lambda i: along_z(i, -1),
        "x1": lambda i: i ^ 8,
        "x2": lambda i: i ^ 16,
        "x3": lambda i: i ^ 24,
    }
    return {name: [(i, to(i)) for i in range(count)] for name, to in table.items()}


def shards(count, queries, key_rows, value_rows, gradient, level_offsets):
    route = routes(count)

    def send(x, name):
        return lax.ppermute(x, AXES, route[name])

    other_offsets = send(level_offsets, "head")
    low = lax.axis_index("head") == 0
    offs = jnp.where(
        low,
        jnp.concatenate([level_offsets, other_offsets], 1),
        jnp.concatenate([other_offsets, level_offsets], 1),
    )
    key_swap, value_swap, other_offsets = lax.optimization_barrier((key_rows, value_rows, other_offsets))
    far_keys = send(key_swap, "head")
    far_values = send(value_swap, "head")

    rows = lambda n, dtype=BF: ((GROUPS, n, 2 * D), dtype)
    packed = ((GROUPS, TOKENS, 128), F32)
    wide = lambda dtype: ((TOKENS, GROUPS * WIDE), dtype)
    pair = jnp.concatenate([key_rows, value_rows], 1)
    first, middle, tail, last = grid_call(
        select_kernel, "select", offs, [(pair, 1), (pair, 1 + GROUPS // TOGETHER)],
        [rows(64), rows(64), rows(32), rows(16)],
    )
    lift, extra = whole_call(
        compact_kernel, "compact", [rows(96), rows(48)], None,
        middle, send(tail, "x1"), send(last, "x2"), send(last, "x3"),
    )
    lift_down = send(lift, "up")
    lift_up = send(lift, "down")
    extra_far = send(extra, "head")
    power0, peak0, lse0, out0 = grid_call(
        level0_kernel, "level0", None, [queries, key_rows, value_rows, far_keys, far_values],
        [rows(512), packed, packed, ((GROUPS, 512, 128), F32)], after=(extra,),
    )
    (own,) = whole_call(
        assemble_kernel, "assemble", [rows(512)], offs, first, lift, far_keys, far_values,
        extra_far, lift_up, lift_down, after=(lse0,),
    )
    other = send(own, "core")
    stats = pltpu.VMEM((TOGETHER, TOKENS, 128), F32)
    attended, part, down_own, down_other, factor0, shift0 = grid_call(
        attention_kernel, "attention", offs, [queries, gradient, own, other, peak0, lse0, out0],
        [wide(BF), wide(F32), rows(512), rows(512), packed, packed],
        scratch=[pltpu.VMEM((TOGETHER, 4, TOKENS, 128), F32), stats, stats],
    )
    theirs = send(down_other, "core")
    grad_queries, d0 = grid_call(
        return0_kernel, "return0", None,
        [queries, gradient, key_rows, value_rows, far_keys, far_values, power0, factor0, shift0, part],
        [wide(BF), rows(256)],
    )
    rows_kept, rows_far, up, down, x_far, x_kept = whole_call(
        reduce_kernel, "reduce", [rows(128), rows(128), rows(96), rows(96), rows(48), rows(48, F32)],
        None, down_own, theirs, after=(d0,),
    )
    from_down = send(up, "up")
    from_up = send(down, "down")
    x_far = send(x_far, "head")
    (far,) = whole_call(place_kernel, "place", [rows(128)], offs, d0, rows_far, after=(x_far,))
    far = send(far, "head")
    one, two, three = whole_call(
        cross_kernel, "cross", [rows(32), rows(16), rows(16)], None, x_kept, x_far, from_up, from_down
    )
    one, two, three = send(one, "x1"), send(two, "x2"), send(three, "x3")
    out = ((TOKENS, GROUPS * D), BF)
    grad_keys, grad_values = whole_call(
        finish_kernel, "finish", [out, out], offs, d0, rows_kept, far, from_up, from_down, one, two, three
    )
    return (attended, grad_queries, grad_keys, grad_values)


def solution(mesh):
    rows = P(AXES, None)
    return jax.shard_map(
        functools.partial(shards, mesh.size),
        mesh=mesh,
        in_specs=(rows, rows, rows, rows, P(None, "head")),
        out_specs=(rows, rows, rows, rows),
        check_vma=False,
    )
```

```python
import functools

import jax
import jax.numpy as jnp
from jax import lax
from jax.experimental import pallas as pl
from jax.experimental.pallas import tpu as pltpu
from jax.sharding import PartitionSpec as P

D = 128
GROUPS = 8
HEADS = 4
TOKENS = 128
TOGETHER = 4
WIDE = HEADS * D
SCALE = D ** (-0.5)
LOG2E = 1.4426950408889634
AXES = ("ctx", "head")
BF = jnp.bfloat16
F32 = jnp.float32
ANY_ROWS = ((0, 64, 1), (64, 96, 2), (96, 112, 3), (112, 120, 4))
VMEM_LIMIT = 24 * 1024 * 1024
GRID_LIMIT = 32 * 1024 * 1024


def dot(a, b):
    return lax.dot_general(a, b, (((1,), (0,)), ((), ())), preferred_element_type=F32)


def dot_nt(a, b):
    return lax.dot_general(a, b, (((1,), (1,)), ((), ())), preferred_element_type=F32)


def dot_tn(a, b):
    return lax.dot_general(a, b, (((0,), (0,)), ((), ())), preferred_element_type=F32)


def one_hot(mask):
    return jnp.where(mask, 1.0, 0.0).astype(BF)


def selected_token(row, offs, group):
    token = jnp.full(row.shape, -1, jnp.int32)
    for start, stop, level in ANY_ROWS:
        inside = (row >= start) & (row < stop)
        token = jnp.where(inside, (row - start) * 2**level + offs[level, group], token)
    return token


def selector(offs, group):
    shape = (128, TOKENS)
    row = lax.broadcasted_iota(jnp.int32, shape, 0)
    return one_hot(selected_token(row, offs, group) == lax.broadcasted_iota(jnp.int32, shape, 1))


def placer(offs, group):
    shape = (TOKENS, 128)
    row = lax.broadcasted_iota(jnp.int32, shape, 1)
    return one_hot(selected_token(row, offs, group) == lax.broadcasted_iota(jnp.int32, shape, 0))


def group_rows(keys_ref, values_ref, group):
    lanes = slice(group * D, (group + 1) * D)
    return jnp.concatenate([keys_ref[:, lanes], values_ref[:, lanes]], 1)


def select_kernel(offs, keys, values, first, middle, tail, last):
    first_group = pl.program_id(0) * TOGETHER
    for j in range(TOGETHER):
        rows = dot(selector(offs, first_group + j), group_rows(keys, values, j))
        first[j] = rows[0:64].astype(BF)
        middle[j] = rows[64:128].astype(BF)
        tail[j] = rows[96:128].astype(BF)
        last[j] = rows[112:128].astype(BF)


def compact_kernel(middle, one, two, three, lift, extra):
    for g in range(GROUPS):
        mine, a, b, c = [ref[g].astype(F32) for ref in (middle, one, two, three)]
        last = [a[16:24], b[:8], c[:8]]
        lift[g] = jnp.concatenate([mine[0:48], a[0:16], mine[48:56]] + last, 0).astype(BF)
        extra[g] = jnp.concatenate([a[0:16]] + last + [jnp.zeros((8, 2 * D), F32)], 0).astype(BF)


def assemble_kernel(offs, first, lift, keys, values, x_far, lift_up, lift_down, _, held):
    for g in range(GROUPS):
        far = dot(selector(offs, g), group_rows(keys, values, g))
        extra = x_far[g].astype(F32)
        across = jnp.concatenate([far[64:112], extra[0:16], far[112:120], extra[16:40]], 0)
        lifts = [lift[g].astype(F32), across, lift_up[g].astype(F32), lift_down[g].astype(F32)]
        rows = [first[g].astype(F32), far[0:64]]
        for a, b in ((0, 32), (32, 64), (64, 96)):
            rows += [x[a:b] for x in lifts]
        held[g] = jnp.concatenate(rows, 0).astype(BF)


def by_level(rows):
    parts = []
    for start, stop in ((0, 64), (64, 96), (96, 112), (112, 120), (120, 128)):
        parts += [rows[start:stop, h * D : (h + 1) * D] for h in range(HEADS)]
    return jnp.concatenate(parts, 0)


def by_selection(rows):
    heads = []
    for h in range(HEADS):
        parts = []
        base = 0
        for count in (64, 32, 16, 8, 8):
            parts.append(rows[base + h * count : base + (h + 1) * count])
            base += HEADS * count
        heads.append(jnp.concatenate(parts, 0))
    return jnp.concatenate(heads, 1)


def heads_to_lanes(x):
    count = x.shape[0] // HEADS
    lane = lax.broadcasted_iota(jnp.int32, (count, 128), 1) & (HEADS - 1)
    out = x[(HEADS - 1) * count :]
    for h in range(HEADS - 1):
        out = jnp.where(lane == h, x[h * count : (h + 1) * count], out)
    return out


def wide_lanes(j):
    return slice(j * WIDE, (j + 1) * WIDE)


def by_head(rows):
    return jnp.concatenate([rows[:, h * D : (h + 1) * D] for h in range(HEADS)], 0)


def by_token(rows):
    count = rows.shape[0] // HEADS
    return jnp.concatenate([rows[h * count : (h + 1) * count] for h in range(HEADS)], 1)


def expand(x):
    return jnp.concatenate([jnp.broadcast_to(x[:, h : h + 1], x.shape) for h in range(HEADS)], 0)


def beside(x):
    high = x.astype(BF).astype(F32)
    lane = lax.broadcasted_iota(jnp.int32, x.shape, 1)
    both = jnp.where(lane < 64, high, x - high)
    return jnp.concatenate(
        [jnp.where((lane & (HEADS - 1)) == h, both, 0.0) for h in range(HEADS)], 0
    ).astype(BF)


def minus_lanes():
    lane = lax.broadcasted_iota(jnp.int32, (2 * D, D), 1)
    return jnp.where((lane & 63) < HEADS, -1.0, 0.0).astype(BF)


def forward(queries, keys, values):
    ones = jnp.ones((2 * D, D), BF)
    scores = [dot_nt(q, k) * (SCALE * LOG2E) for q, k in zip(queries, keys)]
    peaks = [jnp.max(x, 1, keepdims=True) for x in scores]
    powers = [jnp.exp2(x - p).astype(BF) for x, p in zip(scores, peaks)]
    outs = [dot(p, jnp.concatenate([v, ones], 1)) for p, v in zip(powers, values)]
    peaks = [heads_to_lanes(jnp.broadcast_to(p, (p.shape[0], 128))) for p in peaks]
    lses = [p + jnp.log2(heads_to_lanes(out[:, D:])) for p, out in zip(peaks, outs)]
    return powers, peaks, lses, [out[:, :D] for out in outs]


def backward(queries, scaled, keys, values, powers, shifts):
    minus = minus_lanes()
    weights = [
        dot_nt(jnp.concatenate([g, beside(d)], 1), jnp.concatenate([v, minus], 1))
        for g, d, v in zip(scaled, shifts, values)
    ]
    scores = [(p.astype(F32) * w).astype(BF) for p, w in zip(powers, weights)]
    grad_values = [dot_tn(g, p).T for g, p in zip(scaled, powers)]
    grad_keys = [dot_tn(q, x).T * SCALE for q, x in zip(queries, scores)]
    pairs = [jnp.concatenate(pair, 1).astype(BF) for pair in zip(grad_keys, grad_values)]
    return pairs, [dot(x, k) * SCALE for x, k in zip(scores, keys)]


def whole_rows(own_ref, far_ref, j):
    lanes = slice(j * D, (j + 1) * D)
    return jnp.concatenate([own_ref[:, lanes], far_ref[:, lanes]], 0)


def both_rows(own_ref, other_ref, j, at, lanes):
    return jnp.concatenate([own_ref[j, at, lanes], other_ref[j, at, lanes]], 0)


K_LANES, V_LANES, LEVEL1 = slice(0, D), slice(D, 2 * D), slice(0, 128)


def early_kernel(offs, q_ref, g_ref, k_ref, v_ref, kp_ref, vp_ref, *refs):
    qs_ref, gs_ref, power0, peak0, lse0, out0 = refs[-6:]
    members = range(TOGETHER)
    first_group = pl.program_id(0) * TOGETHER
    for j in members:
        pick = selector(offs, first_group + j)
        qs_ref[j] = by_level(dot(pick, q_ref[:, wide_lanes(j)])).astype(BF)
        gs_ref[j] = by_level(dot(pick, g_ref[:, wide_lanes(j)])).astype(BF)
    queries = [by_head(q_ref[:, wide_lanes(j)]) for j in members]
    keys = [whole_rows(k_ref, kp_ref, j) for j in members]
    values = [whole_rows(v_ref, vp_ref, j) for j in members]
    for j, (power, peak, lse, out) in enumerate(zip(*forward(queries, keys, values))):
        power0[j], peak0[j], lse0[j], out0[j] = power, peak, lse, out


def place_levels(offs, first_group, rows):
    rows = [by_selection(x).astype(BF) for x in rows]
    return [dot(placer(offs, first_group + j), r) for j, r in enumerate(rows)]


def attention_kernel(
    offs, qs_ref, gs_ref, g_ref, own_ref, other_ref, peak0, lse0, out0,
    att_ref, part_ref, down_ref, dother_ref, factor0, shift0, power1, factor1, shift1,
    level_ref, token_ref, delta_ref,
):
    members = range(TOGETHER)
    first_group = pl.program_id(0) * TOGETHER
    bounds = ((0, 256), (256, 384), (384, 448), (448, 480))
    starts = [[(offs[k, first_group + j], 128 >> k) for k in range(1, 5)] for j in members]

    def kept(k, lanes):
        at = slice(128 * k, 128 * k + 128)
        return [both_rows(own_ref, other_ref, j, at, lanes) for j in members]

    def for_levels(ref, xs):
        for j, x in enumerate(xs):
            ref[j] = x
        return [
            [ref[j, pl.ds(starts[j][k][0], starts[j][k][1], 2 ** (k + 1)), :] for j in members]
            for k in range(4)
        ]

    level_ref[...] = jnp.full(level_ref.shape, -1e30, F32)
    queries = [[qs_ref[j, a:b] for j in members] for a, b in bounds]
    grads = [[gs_ref[j, a:b] for j in members] for a, b in bounds]
    keys = [kept(k, K_LANES) for k in range(4)]
    values = [kept(k, V_LANES) for k in range(4)]
    results = [forward(queries[k], keys[k], values[k]) for k in range(4)]

    for k in range(4):
        for j in members:
            start, count = starts[j][k]
            level_ref[j, k, pl.ds(start, count, 2 ** (k + 1)), :] = results[k][2][j]
    firsts = [lse0[j] for j in members]
    tops = [functools.reduce(jnp.maximum, [level_ref[j, k] for k in range(4)], firsts[j]) for j in members]
    sums = [
        jnp.exp2(firsts[j] - tops[j]) + sum(jnp.exp2(level_ref[j, k] - tops[j]) for k in range(4))
        for j in members
    ]
    merged = [top + jnp.log2(x) for top, x in zip(tops, sums)]
    factors = [
        [jnp.exp2(p - m) for p, m in zip(results[k][1], column)]
        for k, column in enumerate(for_levels(token_ref, merged))
    ]
    spread = [[expand(f) for f in fs] for fs in factors]
    pad = [jnp.zeros((32, D), F32)]
    parts = [[out * f for out, f in zip(results[k][3], spread[k])] for k in range(4)]
    placed = place_levels(offs, first_group, [jnp.concatenate(list(p) + pad, 0) for p in zip(*parts)])
    deltas = []
    for j in members:
        factor = jnp.exp2(peak0[j] - merged[j])
        attended = (placed[j] + by_token(out0[j] * expand(factor))).astype(BF)
        att_ref[:, wide_lanes(j)] = attended
        product = g_ref[:, wide_lanes(j)].astype(F32) * attended.astype(F32)
        total = [
            jnp.broadcast_to(jnp.sum(product[:, h * D : (h + 1) * D], 1, keepdims=True), (TOKENS, 128))
            for h in range(HEADS)
        ]
        deltas.append(heads_to_lanes(jnp.concatenate(total, 0)))
        factor0[j] = factor
        shift0[j] = factor * deltas[j]
    shifts = [
        [f * d for f, d in zip(factors[k], column)] for k, column in enumerate(for_levels(delta_ref, deltas))
    ]
    for j in members:
        power1[j], factor1[j], shift1[j] = results[0][0][j], factors[0][j], shifts[0][j]
    for k in range(1, 4):
        scaled = [(g.astype(F32) * f).astype(BF) for g, f in zip(grads[k], spread[k])]
        pairs, part = backward(queries[k], scaled, keys[k], values[k], results[k][0], shifts[k])
        at = slice(128 * k - 128, 128 * k)
        for j in members:
            down_ref[j, at] = pairs[j][:128]
            dother_ref[j, at] = pairs[j][128:]
            part_ref[j, bounds[k][0] - 256 : bounds[k][1] - 256] = part[j]


def return0_kernel(
    q_ref, g_ref, k_ref, v_ref, kp_ref, vp_ref, power_ref, factor_ref, shift_ref, part_ref, *refs
):
    dq_ref, d0_ref = refs[-2:]
    members = range(TOGETHER)
    queries = [by_head(q_ref[:, wide_lanes(j)]) for j in members]
    keys = [whole_rows(k_ref, kp_ref, j) for j in members]
    values = [whole_rows(v_ref, vp_ref, j) for j in members]
    scaled = [
        (by_head(g_ref[:, wide_lanes(j)]).astype(F32) * expand(factor_ref[j])).astype(BF) for j in members
    ]
    powers, shifts = [power_ref[j] for j in members], [shift_ref[j] for j in members]
    pairs, parts = backward(queries, scaled, keys, values, powers, shifts)
    for j in members:
        d0_ref[j] = pairs[j]
        dq_ref[:, wide_lanes(j)] = (by_token(parts[j]) + part_ref[:, wide_lanes(j)]).astype(BF)


def return1_kernel(
    offs, qs_ref, gs_ref, own_ref, other_ref, power_ref, factor_ref, shift_ref, part_ref,
    dq_ref, down_ref, dother_ref,
):
    members = range(TOGETHER)
    queries = [qs_ref[j, 0:256] for j in members]
    keys = [both_rows(own_ref, other_ref, j, LEVEL1, K_LANES) for j in members]
    values = [both_rows(own_ref, other_ref, j, LEVEL1, V_LANES) for j in members]
    scaled = [(gs_ref[j, 0:256].astype(F32) * expand(factor_ref[j])).astype(BF) for j in members]
    powers, shifts = [power_ref[j] for j in members], [shift_ref[j] for j in members]
    pairs, parts = backward(queries, scaled, keys, values, powers, shifts)
    pad = [jnp.zeros((32, D), F32)]
    rows = [jnp.concatenate([parts[j], part_ref[j]] + pad, 0) for j in members]
    for j, x in enumerate(place_levels(offs, pl.program_id(0) * TOGETHER, rows)):
        down_ref[j] = pairs[j][:128]
        dother_ref[j] = pairs[j][128:]
        dq_ref[:, wide_lanes(j)] = x


def reduce_kernel(mine, theirs, _, mid_kept, mid_far, up, down, x_far, x_kept):
    zero = jnp.zeros((8, 2 * D), F32)
    for g in range(GROUPS):
        total = mine[g].astype(F32) + theirs[g].astype(F32)
        for z, ref in enumerate((mid_kept, mid_far, up, down)):
            second, third, fourth = [total[s + 32 * z : s + 32 * z + 32] for s in (0, 128, 256)]
            if z >= 2:
                ref[g] = jnp.concatenate([second, third, fourth], 0).astype(BF)
                continue
            ref[g] = jnp.concatenate([second, third[:16], fourth[:8], zero], 0).astype(BF)
            extra = jnp.concatenate([third[16:], fourth[8:], zero], 0)
            if z == 0:
                x_kept[g] = extra
            else:
                x_far[g] = extra.astype(BF)


def place_kernel(offs, d0, mine, theirs, mid_far, _, *refs):
    for g in range(GROUPS):
        first = (mine[g, 64:128].astype(F32) + theirs[g, 64:128].astype(F32)).astype(BF)
        rows = jnp.concatenate([first, mid_far[g]], 0)
        whole = (d0[g, 128:256].astype(F32) + dot(placer(offs, g), rows)).astype(BF)
        refs[g // TOGETHER][g % TOGETHER] = whole


def cross_kernel(kept, far, up, down, one, two, three):
    zero = jnp.zeros((8, 2 * D), F32)
    for g in range(GROUPS):
        sides = up[g].astype(F32) + down[g].astype(F32)
        total = kept[g] + far[g].astype(F32)
        third = total[0:16] + sides[48:64]
        fourth = total[16:40] + sides[72:96]
        one[g] = jnp.concatenate([third, fourth[0:8], zero], 0).astype(BF)
        two[g] = jnp.concatenate([fourth[8:16], zero], 0).astype(BF)
        three[g] = jnp.concatenate([fourth[16:24], zero], 0).astype(BF)


def finish_kernel(offs, d0, mine, theirs, mid_kept, *refs):
    *fars, up, down, one, two, three, dk_ref, dv_ref = refs
    for g in range(GROUPS):
        kept = mid_kept[g].astype(F32)
        sides = up[g].astype(F32) + down[g].astype(F32)
        a, b, c = one[g].astype(F32), two[g].astype(F32), three[g].astype(F32)
        rows = jnp.concatenate(
            [
                mine[g, 0:64].astype(F32) + theirs[g, 0:64].astype(F32),
                kept[0:32] + sides[0:32],
                kept[32:48] + sides[32:48] + a[0:16],
                kept[48:56] + sides[64:72] + a[16:24] + b[0:8] + c[0:8],
                jnp.zeros((8, 2 * D), F32),
            ],
            0,
        ).astype(BF)
        far = fars[g // TOGETHER][g % TOGETHER].astype(F32)
        whole = d0[g, 0:128].astype(F32) + far + dot(placer(offs, g), rows)
        dk_ref[:, g * D : (g + 1) * D] = whole[:, :D].astype(BF)
        dv_ref[:, g * D : (g + 1) * D] = whole[:, D:].astype(BF)


def whole_call(body, name, outs, offs, *arrays, after=()):
    specs = [pl.BlockSpec(memory_space=pltpu.VMEM)] * len(arrays)
    specs += [pl.BlockSpec(memory_space=pl.ANY)] * len(after)
    arrays = arrays + tuple(after)
    if offs is not None:
        specs = [pl.BlockSpec(memory_space=pltpu.SMEM)] + specs
        arrays = (offs,) + arrays
    shapes = [jax.ShapeDtypeStruct(shape, dtype) for shape, dtype in outs]
    return pl.pallas_call(
        body,
        name=name,
        out_shape=shapes,
        in_specs=specs,
        out_specs=[pl.BlockSpec(memory_space=pltpu.VMEM)] * len(shapes),
        cost_estimate=pl.CostEstimate(flops=0, bytes_accessed=4 * 10**6, transcendentals=0),
        compiler_params=pltpu.CompilerParams(vmem_limit_bytes=VMEM_LIMIT),
    )(*arrays)


def grid_call(body, name, offs, inputs, outs, scratch=(), after=()):
    def spec(shape, offset=None):
        if offset == 0:
            return pl.BlockSpec((TOGETHER, 128) + shape[2:], lambda i: (i, 0, 0))
        if offset:
            return pl.BlockSpec((TOKENS, TOGETHER * D), lambda i: (0, i + offset - 1))
        if len(shape) == 2:
            return pl.BlockSpec((TOKENS, shape[1] * TOGETHER // GROUPS), lambda i: (0, i))
        return pl.BlockSpec((TOGETHER,) + shape[1:], lambda i: (i, 0, 0))

    specs = [spec(x[0].shape, x[1]) if isinstance(x, tuple) else spec(x.shape) for x in inputs]
    inputs = [x[0] if isinstance(x, tuple) else x for x in inputs]
    specs += [pl.BlockSpec(memory_space=pl.ANY)] * len(after)
    arrays = tuple(inputs) + tuple(after)
    if offs is not None:
        specs = [pl.BlockSpec(memory_space=pltpu.SMEM)] + specs
        arrays = (offs,) + arrays
    return pl.pallas_call(
        body,
        name=name,
        grid=(GROUPS // TOGETHER,),
        in_specs=specs,
        out_specs=[spec(shape) for shape, _ in outs],
        out_shape=[jax.ShapeDtypeStruct(shape, dtype) for shape, dtype in outs],
        scratch_shapes=list(scratch),
        cost_estimate=pl.CostEstimate(flops=4 * 10**9, bytes_accessed=16 * 10**6, transcendentals=10**6),
        compiler_params=pltpu.CompilerParams(vmem_limit_bytes=GRID_LIMIT),
    )(*arrays)


def routes(count):
    def along_z(i, step):
        z = ((i & 1) * 2 + (i >> 2 & 1) + step) % 4
        return (i & ~5) | (z & 1) << 2 | z >> 1

    table = {
        "head": lambda i: i ^ 1,
        "core": lambda i: i ^ 2,
        "up": lambda i: along_z(i, 1),
        "down": lambda i: along_z(i, -1),
        "x1": lambda i: i ^ 8,
        "x2": lambda i: i ^ 16,
        "x3": lambda i: i ^ 24,
    }
    return {name: [(i, to(i)) for i in range(count)] for name, to in table.items()}


def shards(count, queries, key_rows, value_rows, gradient, level_offsets):
    route = routes(count)

    def send(x, name):
        return lax.ppermute(x, AXES, route[name])

    other_offsets = send(level_offsets, "head")
    low = lax.axis_index("head") == 0
    offs = jnp.where(
        low,
        jnp.concatenate([level_offsets, other_offsets], 1),
        jnp.concatenate([other_offsets, level_offsets], 1),
    )
    pair = jnp.concatenate([key_rows, value_rows], 1)
    key_swap, value_swap, pair = lax.optimization_barrier((key_rows, value_rows, pair))
    far_keys = send(key_swap, "head")
    far_values = send(value_swap, "head")

    rows = lambda n, dtype=BF: ((GROUPS, n, 2 * D), dtype)
    packed = ((GROUPS, TOKENS, 128), F32)
    wide = lambda dtype: ((TOKENS, GROUPS * WIDE), dtype)
    first, middle, tail, last = grid_call(
        select_kernel, "select", offs, [(pair, 1), (pair, 1 + GROUPS // TOGETHER)],
        [rows(64), rows(64), rows(32), rows(16)],
    )
    lift, extra = whole_call(
        compact_kernel, "compact", [rows(96), rows(48)], None,
        middle, send(tail, "x1"), send(last, "x2"), send(last, "x3"),
    )
    lift_down = send(lift, "up")
    lift_up = send(lift, "down")
    extra_far = send(extra, "head")
    tall = lambda n, dtype=F32: ((GROUPS, n, D), dtype)
    kv = [key_rows, value_rows, far_keys, far_values]
    qs, gs, power0, peak0, lse0, out0 = grid_call(
        early_kernel, "early", offs, [queries, gradient, *kv],
        [tall(512, BF), tall(512, BF), rows(512), tall(128), tall(128), tall(512)], after=(extra,),
    )
    (own,) = whole_call(
        assemble_kernel, "assemble", [rows(512)], offs, first, lift, far_keys, far_values,
        extra_far, lift_up, lift_down, after=(lse0,),
    )
    other = send(own, "core")
    stats = pltpu.VMEM((TOGETHER, TOKENS, 128), F32)
    attended, part, down_own, down_other, factor0, shift0, power1, factor1, shift1 = grid_call(
        attention_kernel, "attention", offs,
        [qs, gs, gradient, own, other, peak0, lse0, out0],
        [wide(BF), tall(224), rows(384), rows(384), tall(128), tall(128), rows(256), tall(64), tall(64)],
        scratch=[pltpu.VMEM((TOGETHER, 4, TOKENS, 128), F32), stats, stats],
    )
    theirs = send(down_other, "core")
    placed, mine1, theirs1 = grid_call(
        return1_kernel, "return1", offs, [qs, gs, (own, 0), (other, 0), power1, factor1, shift1, part],
        [wide(F32), rows(128), rows(128)],
    )
    mid_kept, mid_far, up, down, x_far, x_kept = whole_call(
        reduce_kernel, "reduce", [rows(64), rows(64), rows(96), rows(96), rows(48), rows(48, F32)],
        None, down_own, theirs, after=(mine1,),
    )
    from_down = send(up, "up")
    from_up = send(down, "down")
    x_far = send(x_far, "head")
    grad_queries, d0 = grid_call(
        return0_kernel, "return0", None, [queries, gradient, *kv, power0, factor0, shift0, placed],
        [wide(BF), rows(256)], after=(x_far,),
    )
    theirs1 = send(theirs1, "core")
    half = ((TOGETHER, TOKENS, 2 * D), BF)
    fars = whole_call(
        place_kernel, "place", [half] * (GROUPS // TOGETHER), offs, d0, mine1, theirs1, mid_far, after=(x_far,)
    )
    fars = [send(far, "head") for far in fars]
    one, two, three = whole_call(
        cross_kernel, "cross", [rows(32), rows(16), rows(16)], None, x_kept, x_far, from_up, from_down
    )
    one, two, three = send(one, "x1"), send(two, "x2"), send(three, "x3")
    out = ((TOKENS, GROUPS * D), BF)
    grad_keys, grad_values = whole_call(
        finish_kernel, "finish", [out, out], offs, d0, mine1, theirs1, mid_kept, *fars, from_up, from_down,
        one, two, three,
    )
    return (attended, grad_queries, grad_keys, grad_values)


def solution(mesh):
    rows = P(AXES, None)
    return jax.shard_map(
        functools.partial(shards, mesh.size),
        mesh=mesh,
        in_specs=(rows, rows, rows, rows, P(None, "head")),
        out_specs=(rows, rows, rows, rows),
        check_vma=False,
    )
```

```python
import functools

import jax
import jax.numpy as jnp
from jax import lax
from jax.experimental import pallas as pl
from jax.experimental.pallas import tpu as pltpu
from jax.sharding import PartitionSpec as P

D = 128
GROUPS = 8
HEADS = 4
TOKENS = 128
TOGETHER = 4
WIDE = HEADS * D
SCALE = D ** (-0.5)
LOG2E = 1.4426950408889634
AXES = ("ctx", "head")
BF = jnp.bfloat16
F32 = jnp.float32
ANY_ROWS = ((0, 64, 1), (64, 96, 2), (96, 112, 3), (112, 120, 4))
VMEM_LIMIT = 24 * 1024 * 1024
GRID_LIMIT = 32 * 1024 * 1024


def dot(a, b):
    return lax.dot_general(a, b, (((1,), (0,)), ((), ())), preferred_element_type=F32)


def dot_nt(a, b):
    return lax.dot_general(a, b, (((1,), (1,)), ((), ())), preferred_element_type=F32)


def dot_tn(a, b):
    return lax.dot_general(a, b, (((0,), (0,)), ((), ())), preferred_element_type=F32)


def one_hot(mask):
    return jnp.where(mask, 1.0, 0.0).astype(BF)


def selected_token(row, offs, group):
    token = jnp.full(row.shape, -1, jnp.int32)
    for start, stop, level in ANY_ROWS:
        inside = (row >= start) & (row < stop)
        token = jnp.where(inside, (row - start) * 2**level + offs[level, group], token)
    return token


def selector(offs, group):
    shape = (128, TOKENS)
    row = lax.broadcasted_iota(jnp.int32, shape, 0)
    return one_hot(selected_token(row, offs, group) == lax.broadcasted_iota(jnp.int32, shape, 1))


def placer(offs, group):
    shape = (TOKENS, 128)
    row = lax.broadcasted_iota(jnp.int32, shape, 1)
    return one_hot(selected_token(row, offs, group) == lax.broadcasted_iota(jnp.int32, shape, 0))


def group_rows(keys_ref, values_ref, group):
    lanes = slice(group * D, (group + 1) * D)
    return jnp.concatenate([keys_ref[:, lanes], values_ref[:, lanes]], 1)


def select_kernel(offs, keys, values, first, middle, tail, last):
    first_group = pl.program_id(0) * TOGETHER
    for j in range(TOGETHER):
        rows = dot(selector(offs, first_group + j), group_rows(keys, values, j))
        first[j] = rows[0:64].astype(BF)
        middle[j] = rows[64:128].astype(BF)
        tail[j] = rows[96:128].astype(BF)
        last[j] = rows[112:128].astype(BF)


def extra_rows(ref, group):
    at = 40 * (group % 2)
    return ref[group // 2].astype(F32)[at : at + 40]


def compact_kernel(middle, one, two, three, lift, extra):
    whole = []
    for g in range(GROUPS):
        mine, a, b, c = [ref[g].astype(F32) for ref in (middle, one, two, three)]
        last = [a[16:24], b[:8], c[:8]]
        lift[g] = jnp.concatenate([mine[0:48], a[0:16], mine[48:56]] + last, 0).astype(BF)
        whole += [a[0:16]] + last
        if g % 2:
            extra[g // 2] = jnp.concatenate(whole, 0).astype(BF)
            whole = []


def across_kernel(offs, first, keys, values, _, held, across):
    for g in range(GROUPS):
        far = dot(selector(offs, g), group_rows(keys, values, g)).astype(BF)
        held[g] = jnp.concatenate([first[g], far[0:64]], 0)
        across[g] = far[64:128]


def assemble_kernel(held, across, lift, x_far, lift_up, lift_down, out):
    for g in range(GROUPS):
        far, extra = across[g].astype(F32), extra_rows(x_far, g)
        far = jnp.concatenate([far[0:48], extra[0:16], far[48:56], extra[16:40]], 0).astype(BF)
        lifts = [lift[g], far, lift_up[g], lift_down[g]]
        out[g, 0:128] = held[g]
        for i, (a, b) in enumerate(((0, 32), (32, 64), (64, 96))):
            out[g, 128 * i + 128 : 128 * i + 256] = jnp.concatenate([x[a:b] for x in lifts], 0)


def by_level(rows):
    parts = []
    for start, stop in ((0, 64), (64, 96), (96, 112), (112, 120), (120, 128)):
        parts += [rows[start:stop, h * D : (h + 1) * D] for h in range(HEADS)]
    return jnp.concatenate(parts, 0)


def by_selection(rows):
    heads = []
    for h in range(HEADS):
        parts = []
        base = 0
        for count in (64, 32, 16, 8, 8):
            parts.append(rows[base + h * count : base + (h + 1) * count])
            base += HEADS * count
        heads.append(jnp.concatenate(parts, 0))
    return jnp.concatenate(heads, 1)


def heads_to_lanes(x):
    count = x.shape[0] // HEADS
    lane = lax.broadcasted_iota(jnp.int32, (count, 128), 1) & (HEADS - 1)
    out = x[(HEADS - 1) * count :]
    for h in range(HEADS - 1):
        out = jnp.where(lane == h, x[h * count : (h + 1) * count], out)
    return out


def wide_lanes(j):
    return slice(j * WIDE, (j + 1) * WIDE)


def by_head(rows):
    return jnp.concatenate([rows[:, h * D : (h + 1) * D] for h in range(HEADS)], 0)


def by_token(rows):
    count = rows.shape[0] // HEADS
    return jnp.concatenate([rows[h * count : (h + 1) * count] for h in range(HEADS)], 1)


def expand(x):
    return jnp.concatenate([jnp.broadcast_to(x[:, h : h + 1], x.shape) for h in range(HEADS)], 0)


def beside(x):
    high = x.astype(BF).astype(F32)
    lane = lax.broadcasted_iota(jnp.int32, x.shape, 1)
    both = jnp.where(lane < 64, high, x - high)
    return jnp.concatenate(
        [jnp.where((lane & (HEADS - 1)) == h, both, 0.0) for h in range(HEADS)], 0
    ).astype(BF)


def minus_lanes():
    lane = lax.broadcasted_iota(jnp.int32, (2 * D, D), 1)
    return jnp.where((lane & 63) < HEADS, -1.0, 0.0).astype(BF)


def forward(queries, keys, values):
    ones = jnp.ones((2 * D, D), BF)
    scores = [dot_nt(q, k) * (SCALE * LOG2E) for q, k in zip(queries, keys)]
    peaks = [jnp.max(x, 1, keepdims=True) for x in scores]
    powers = [jnp.exp2(x - p).astype(BF) for x, p in zip(scores, peaks)]
    outs = [dot(p, jnp.concatenate([v, ones], 1)) for p, v in zip(powers, values)]
    peaks = [heads_to_lanes(jnp.broadcast_to(p, (p.shape[0], 128))) for p in peaks]
    lses = [p + jnp.log2(heads_to_lanes(out[:, D:])) for p, out in zip(peaks, outs)]
    return powers, peaks, lses, [out[:, :D] for out in outs]


def backward(queries, scaled, keys, values, powers, shifts):
    minus = minus_lanes()
    weights = [
        dot_nt(jnp.concatenate([g, beside(d)], 1), jnp.concatenate([v, minus], 1))
        for g, d, v in zip(scaled, shifts, values)
    ]
    scores = [(p.astype(F32) * w).astype(BF) for p, w in zip(powers, weights)]
    grad_values = [dot_tn(g, p).T for g, p in zip(scaled, powers)]
    grad_keys = [dot_tn(q, x).T * SCALE for q, x in zip(queries, scores)]
    pairs = [jnp.concatenate(pair, 1).astype(BF) for pair in zip(grad_keys, grad_values)]
    return pairs, [dot(x, k) * SCALE for x, k in zip(scores, keys)]


def whole_rows(own_ref, far_ref, j):
    lanes = slice(j * D, (j + 1) * D)
    return jnp.concatenate([own_ref[:, lanes], far_ref[:, lanes]], 0)


def both_rows(own_ref, other_ref, j, at, lanes):
    return jnp.concatenate([own_ref[j, at, lanes], other_ref[j, at, lanes]], 0)


K_LANES, V_LANES, LEVEL1 = slice(0, D), slice(D, 2 * D), slice(0, 128)


def early_kernel(offs, q_ref, g_ref, k_ref, v_ref, kp_ref, vp_ref, *refs):
    qs_ref, gs_ref, power0, peak0, lse0, out0 = refs[-6:]
    members = range(TOGETHER)
    first_group = pl.program_id(0) * TOGETHER
    for j in members:
        pick = selector(offs, first_group + j)
        qs_ref[j] = by_level(dot(pick, q_ref[:, wide_lanes(j)])).astype(BF)
        gs_ref[j] = by_level(dot(pick, g_ref[:, wide_lanes(j)])).astype(BF)
    queries = [by_head(q_ref[:, wide_lanes(j)]) for j in members]
    keys = [whole_rows(k_ref, kp_ref, j) for j in members]
    values = [whole_rows(v_ref, vp_ref, j) for j in members]
    for j, (power, peak, lse, out) in enumerate(zip(*forward(queries, keys, values))):
        power0[j], peak0[j], lse0[j], out0[j] = power, peak, lse, out


def place_levels(offs, first_group, rows):
    rows = [by_selection(x).astype(BF) for x in rows]
    return [dot(placer(offs, first_group + j), r) for j, r in enumerate(rows)]


def attention_kernel(
    offs, qs_ref, gs_ref, g_ref, own_ref, other_ref, peak0, lse0, out0,
    att_ref, part_ref, down_ref, dother_ref, factor0, shift0, power1, factor1, shift1,
    level_ref, token_ref, delta_ref,
):
    members = range(TOGETHER)
    first_group = pl.program_id(0) * TOGETHER
    bounds = ((0, 256), (256, 384), (384, 448), (448, 480))
    starts = [[(offs[k, first_group + j], 128 >> k) for k in range(1, 5)] for j in members]

    def kept(k, lanes):
        at = slice(128 * k, 128 * k + 128)
        return [both_rows(own_ref, other_ref, j, at, lanes) for j in members]

    def for_levels(ref, xs):
        for j, x in enumerate(xs):
            ref[j] = x
        return [
            [ref[j, pl.ds(starts[j][k][0], starts[j][k][1], 2 ** (k + 1)), :] for j in members]
            for k in range(4)
        ]

    level_ref[...] = jnp.full(level_ref.shape, -1e30, F32)
    queries = [[qs_ref[j, a:b] for j in members] for a, b in bounds]
    grads = [[gs_ref[j, a:b] for j in members] for a, b in bounds]
    keys = [kept(k, K_LANES) for k in range(4)]
    values = [kept(k, V_LANES) for k in range(4)]
    results = [forward(queries[k], keys[k], values[k]) for k in range(4)]

    for k in range(4):
        for j in members:
            start, count = starts[j][k]
            level_ref[j, k, pl.ds(start, count, 2 ** (k + 1)), :] = results[k][2][j]
    firsts = [lse0[j] for j in members]
    tops = [functools.reduce(jnp.maximum, [level_ref[j, k] for k in range(4)], firsts[j]) for j in members]
    sums = [
        jnp.exp2(firsts[j] - tops[j]) + sum(jnp.exp2(level_ref[j, k] - tops[j]) for k in range(4))
        for j in members
    ]
    merged = [top + jnp.log2(x) for top, x in zip(tops, sums)]
    factors = [
        [jnp.exp2(p - m) for p, m in zip(results[k][1], column)]
        for k, column in enumerate(for_levels(token_ref, merged))
    ]
    spread = [[expand(f) for f in fs] for fs in factors]
    pad = [jnp.zeros((32, D), F32)]
    parts = [[out * f for out, f in zip(results[k][3], spread[k])] for k in range(4)]
    placed = place_levels(offs, first_group, [jnp.concatenate(list(p) + pad, 0) for p in zip(*parts)])
    deltas = []
    for j in members:
        factor = jnp.exp2(peak0[j] - merged[j])
        attended = (placed[j] + by_token(out0[j] * expand(factor))).astype(BF)
        att_ref[:, wide_lanes(j)] = attended
        product = g_ref[:, wide_lanes(j)].astype(F32) * attended.astype(F32)
        total = [
            jnp.broadcast_to(jnp.sum(product[:, h * D : (h + 1) * D], 1, keepdims=True), (TOKENS, 128))
            for h in range(HEADS)
        ]
        deltas.append(heads_to_lanes(jnp.concatenate(total, 0)))
        factor0[j] = factor
        shift0[j] = factor * deltas[j]
    shifts = [
        [f * d for f, d in zip(factors[k], column)] for k, column in enumerate(for_levels(delta_ref, deltas))
    ]
    for j in members:
        power1[j], factor1[j], shift1[j] = results[0][0][j], factors[0][j], shifts[0][j]
    for k in range(1, 4):
        scaled = [(g.astype(F32) * f).astype(BF) for g, f in zip(grads[k], spread[k])]
        pairs, part = backward(queries[k], scaled, keys[k], values[k], results[k][0], shifts[k])
        at = slice(128 * k - 128, 128 * k)
        for j in members:
            down_ref[j, at] = pairs[j][:128]
            dother_ref[j, at] = pairs[j][128:]
            part_ref[j, bounds[k][0] - 256 : bounds[k][1] - 256] = part[j]


def return0_kernel(
    q_ref, g_ref, k_ref, v_ref, kp_ref, vp_ref, power_ref, factor_ref, shift_ref, part_ref, *refs
):
    dq_ref, d0_ref = refs[-2:]
    members = range(TOGETHER)
    queries = [by_head(q_ref[:, wide_lanes(j)]) for j in members]
    keys = [whole_rows(k_ref, kp_ref, j) for j in members]
    values = [whole_rows(v_ref, vp_ref, j) for j in members]
    scaled = [
        (by_head(g_ref[:, wide_lanes(j)]).astype(F32) * expand(factor_ref[j])).astype(BF) for j in members
    ]
    powers, shifts = [power_ref[j] for j in members], [shift_ref[j] for j in members]
    pairs, parts = backward(queries, scaled, keys, values, powers, shifts)
    for j in members:
        d0_ref[j] = pairs[j]
        dq_ref[:, wide_lanes(j)] = (by_token(parts[j]) + part_ref[:, wide_lanes(j)]).astype(BF)


def return1_kernel(
    offs, qs_ref, gs_ref, own_ref, other_ref, power_ref, factor_ref, shift_ref, part_ref,
    dq_ref, down_ref, dother_ref,
):
    members = range(TOGETHER)
    queries = [qs_ref[j, 0:256] for j in members]
    keys = [both_rows(own_ref, other_ref, j, LEVEL1, K_LANES) for j in members]
    values = [both_rows(own_ref, other_ref, j, LEVEL1, V_LANES) for j in members]
    scaled = [(gs_ref[j, 0:256].astype(F32) * expand(factor_ref[j])).astype(BF) for j in members]
    powers, shifts = [power_ref[j] for j in members], [shift_ref[j] for j in members]
    pairs, parts = backward(queries, scaled, keys, values, powers, shifts)
    pad = [jnp.zeros((32, D), F32)]
    rows = [jnp.concatenate([parts[j], part_ref[j]] + pad, 0) for j in members]
    for j, x in enumerate(place_levels(offs, pl.program_id(0) * TOGETHER, rows)):
        down_ref[j] = pairs[j][:128]
        dother_ref[j] = pairs[j][128:]
        dq_ref[:, wide_lanes(j)] = x


def reduce_kernel(mine, theirs, _, mid_kept, mid_far, up, down, x_far, x_kept):
    zero = jnp.zeros((8, 2 * D), F32)
    whole = [[], []]
    for g in range(GROUPS):
        total = mine[g].astype(F32) + theirs[g].astype(F32)
        for z, ref in enumerate((mid_kept, mid_far, up, down)):
            second, third, fourth = [total[s + 32 * z : s + 32 * z + 32] for s in (0, 128, 256)]
            if z >= 2:
                ref[g] = jnp.concatenate([second, third, fourth], 0).astype(BF)
                continue
            ref[g] = jnp.concatenate([second, third[:16], fourth[:8], zero], 0).astype(BF)
            whole[z] += [third[16:], fourth[8:]]
        if g % 2:
            x_kept[g // 2] = jnp.concatenate(whole[0], 0)
            x_far[g // 2] = jnp.concatenate(whole[1], 0).astype(BF)
            whole = [[], []]


def place_kernel(offs, d0, mine, theirs, mid_far, _, *refs):
    for g in range(GROUPS):
        first = (mine[g, 64:128].astype(F32) + theirs[g, 64:128].astype(F32)).astype(BF)
        rows = jnp.concatenate([first, mid_far[g]], 0)
        whole = (d0[g, 128:256].astype(F32) + dot(placer(offs, g), rows)).astype(BF)
        refs[0][g] = whole


def cross_kernel(kept, far, down, up, one, two, three):
    zero = jnp.zeros((8, 2 * D), F32)
    for g in range(GROUPS):
        sides = up[g].astype(F32) + down[g].astype(F32)
        total = extra_rows(kept, g) + extra_rows(far, g)
        third = total[0:16] + sides[48:64]
        fourth = total[16:40] + sides[72:96]
        one[g] = jnp.concatenate([third, fourth[0:8], zero], 0).astype(BF)
        two[g] = jnp.concatenate([fourth[8:16], zero], 0).astype(BF)
        three[g] = jnp.concatenate([fourth[16:24], zero], 0).astype(BF)


def keep_kernel(offs, d0, mine, theirs, mid_kept, down, up, one, two, three, kept):
    for g in range(GROUPS):
        mid = mid_kept[g].astype(F32)
        sides = up[g].astype(F32) + down[g].astype(F32)
        a, b, c = one[g].astype(F32), two[g].astype(F32), three[g].astype(F32)
        rows = jnp.concatenate(
            [
                mine[g, 0:64].astype(F32) + theirs[g, 0:64].astype(F32),
                mid[0:32] + sides[0:32],
                mid[32:48] + sides[32:48] + a[0:16],
                mid[48:56] + sides[64:72] + a[16:24] + b[0:8] + c[0:8],
                jnp.zeros((8, 2 * D), F32),
            ],
            0,
        ).astype(BF)
        kept[g] = d0[g, 0:128].astype(F32) + dot(placer(offs, g), rows)


def finish_kernel(kept, *refs):
    *fars, dk_ref, dv_ref = refs
    for g in range(GROUPS):
        whole = kept[g] + fars[0][g].astype(F32)
        dk_ref[:, g * D : (g + 1) * D] = whole[:, :D].astype(BF)
        dv_ref[:, g * D : (g + 1) * D] = whole[:, D:].astype(BF)


def whole_call(body, name, outs, offs, *arrays, after=()):
    specs = [pl.BlockSpec(memory_space=pltpu.VMEM)] * len(arrays)
    specs += [pl.BlockSpec(memory_space=pl.ANY)] * len(after)
    arrays = arrays + tuple(after)
    if offs is not None:
        specs = [pl.BlockSpec(memory_space=pltpu.SMEM)] + specs
        arrays = (offs,) + arrays
    shapes = [jax.ShapeDtypeStruct(shape, dtype) for shape, dtype in outs]
    return pl.pallas_call(
        body,
        name=name,
        out_shape=shapes,
        in_specs=specs,
        out_specs=[pl.BlockSpec(memory_space=pltpu.VMEM)] * len(shapes),
        cost_estimate=pl.CostEstimate(flops=0, bytes_accessed=4 * 10**6, transcendentals=0),
        compiler_params=pltpu.CompilerParams(vmem_limit_bytes=VMEM_LIMIT),
    )(*arrays)


def grid_call(body, name, offs, inputs, outs, scratch=(), after=()):
    def spec(shape, offset=None):
        if offset == 0:
            return pl.BlockSpec((TOGETHER, 128) + shape[2:], lambda i: (i, 0, 0))
        if offset:
            return pl.BlockSpec((TOKENS, TOGETHER * D), lambda i: (0, i + offset - 1))
        if len(shape) == 2:
            return pl.BlockSpec((TOKENS, shape[1] * TOGETHER // GROUPS), lambda i: (0, i))
        return pl.BlockSpec((TOGETHER,) + shape[1:], lambda i: (i, 0, 0))

    specs = [spec(x[0].shape, x[1]) if isinstance(x, tuple) else spec(x.shape) for x in inputs]
    inputs = [x[0] if isinstance(x, tuple) else x for x in inputs]
    specs += [pl.BlockSpec(memory_space=pl.ANY)] * len(after)
    arrays = tuple(inputs) + tuple(after)
    if offs is not None:
        specs = [pl.BlockSpec(memory_space=pltpu.SMEM)] + specs
        arrays = (offs,) + arrays
    return pl.pallas_call(
        body,
        name=name,
        grid=(GROUPS // TOGETHER,),
        in_specs=specs,
        out_specs=[spec(shape) for shape, _ in outs],
        out_shape=[jax.ShapeDtypeStruct(shape, dtype) for shape, dtype in outs],
        scratch_shapes=list(scratch),
        cost_estimate=pl.CostEstimate(flops=4 * 10**9, bytes_accessed=16 * 10**6, transcendentals=10**6),
        compiler_params=pltpu.CompilerParams(vmem_limit_bytes=GRID_LIMIT),
    )(*arrays)


def routes(count):
    def along_z(i, step):
        z = ((i & 1) * 2 + (i >> 2 & 1) + step) % 4
        return (i & ~5) | (z & 1) << 2 | z >> 1

    table = {
        "head": lambda i: i ^ 1,
        "near": lambda i: along_z(i, 1 if i & 4 else -1),
        "core": lambda i: i ^ 2,
        "up": lambda i: along_z(i, 1),
        "down": lambda i: along_z(i, -1),
        "x1": lambda i: i ^ 8,
        "x2": lambda i: i ^ 16,
        "x3": lambda i: i ^ 24,
    }
    return {name: [(i, to(i)) for i in range(count)] for name, to in table.items()}


def shards(count, queries, key_rows, value_rows, gradient, level_offsets):
    route = routes(count)

    def send(x, name):
        return lax.ppermute(x, AXES, route[name])

    other_offsets = send(level_offsets, "near")
    low = lax.axis_index("head") == 0
    offs = jnp.where(
        low,
        jnp.concatenate([level_offsets, other_offsets], 1),
        jnp.concatenate([other_offsets, level_offsets], 1),
    )
    pair = jnp.concatenate([key_rows, value_rows], 1)
    far_keys = send(key_rows, "head")
    far_values = send(value_rows, "head")

    rows = lambda n, dtype=BF: ((GROUPS, n, 2 * D), dtype)
    extras = lambda dtype: ((GROUPS // 2, 80, 2 * D), dtype)
    wide = lambda dtype: ((TOKENS, GROUPS * WIDE), dtype)
    first, middle, tail, last = grid_call(
        select_kernel, "select", offs, [(pair, 1), (pair, 1 + GROUPS // TOGETHER)],
        [rows(64), rows(64), rows(32), rows(16)],
    )
    lift, extra = whole_call(
        compact_kernel, "compact", [rows(96), extras(BF)], None,
        middle, send(tail, "x1"), send(last, "x2"), send(last, "x3"),
    )
    lift_down = send(lift, "up")
    lift_up = send(lift, "down")
    extra_far = send(extra, "head")
    tall = lambda n, dtype=F32: ((GROUPS, n, D), dtype)
    kv = [key_rows, value_rows, far_keys, far_values]
    qs, gs, power0, peak0, lse0, out0 = grid_call(
        early_kernel, "early", offs, [queries, gradient, *kv],
        [tall(512, BF), tall(512, BF), rows(512), tall(128), tall(128), tall(512)], after=(extra,),
    )
    held, across = whole_call(
        across_kernel, "across", [rows(128), rows(64)], offs, first, far_keys, far_values, after=(lse0,)
    )
    (own,) = whole_call(
        assemble_kernel, "assemble", [rows(512)], None, held, across, lift, extra_far, lift_up, lift_down
    )
    other = send(own, "core")
    stats = pltpu.VMEM((TOGETHER, TOKENS, 128), F32)
    attended, part, down_own, down_other, factor0, shift0, power1, factor1, shift1 = grid_call(
        attention_kernel, "attention", offs,
        [qs, gs, gradient, own, other, peak0, lse0, out0],
        [wide(BF), tall(224), rows(384), rows(384), tall(128), tall(128), rows(256), tall(64), tall(64)],
        scratch=[pltpu.VMEM((TOGETHER, 4, TOKENS, 128), F32), stats, stats],
    )
    theirs = send(down_other, "core")
    placed, mine1, theirs1 = grid_call(
        return1_kernel, "return1", offs, [qs, gs, (own, 0), (other, 0), power1, factor1, shift1, part],
        [wide(F32), rows(128), rows(128)],
    )
    mid_kept, mid_far, up, down, x_far, x_kept = whole_call(
        reduce_kernel, "reduce", [rows(64), rows(64), rows(96), rows(96), extras(BF), extras(F32)],
        None, down_own, theirs, after=(mine1,),
    )
    from_down = send(up, "up")
    from_up = send(down, "down")
    x_far = send(x_far, "head")
    theirs1 = send(theirs1, "core")
    grad_queries, d0 = grid_call(
        return0_kernel, "return0", None, [queries, gradient, *kv, power0, factor0, shift0, placed],
        [wide(BF), rows(256)], after=(theirs1,),
    )
    half = ((TOGETHER, TOKENS, 2 * D), BF)
    fars = whole_call(
        place_kernel, "place", [rows(128)], offs, d0, mine1, theirs1, mid_far, after=(x_far,)
    )
    fars = [send(far, "head") for far in fars]
    one, two, three = whole_call(
        cross_kernel, "cross", [rows(32), rows(16), rows(16)], None, x_kept, x_far, from_down, from_up
    )
    one, two, three = send(one, "x1"), send(two, "x2"), send(three, "x3")
    out = ((TOKENS, GROUPS * D), BF)
    (kept,) = whole_call(
        keep_kernel, "keep", [rows(128, F32)], offs, d0, mine1, theirs1, mid_kept, from_down, from_up,
        one, two, three,
    )
    grad_keys, grad_values = whole_call(finish_kernel, "finish", [out, out], None, kept, *fars)
    return (attended, grad_queries, grad_keys, grad_values)


def solution(mesh):
    rows = P(AXES, None)
    return jax.shard_map(
        functools.partial(shards, mesh.size),
        mesh=mesh,
        in_specs=(rows, rows, rows, rows, P(None, "head")),
        out_specs=(rows, rows, rows, rows),
        check_vma=False,
    )
```

```python
import functools

import jax
import jax.numpy as jnp
from jax import lax
from jax.experimental import pallas as pl
from jax.experimental.pallas import tpu as pltpu
from jax.sharding import PartitionSpec as P

D = 128
GROUPS = 8
HEADS = 4
TOKENS = 128
TOGETHER = 4
WIDE = HEADS * D
SCALE = D ** (-0.5)
LOG2E = 1.4426950408889634
AXES = ("ctx", "head")
BF = jnp.bfloat16
F32 = jnp.float32
ANY_ROWS = ((0, 64, 1), (64, 96, 2), (96, 112, 3), (112, 120, 4))
VMEM_LIMIT = 24 * 1024 * 1024
GRID_LIMIT = 32 * 1024 * 1024


def dot(a, b):
    return lax.dot_general(a, b, (((1,), (0,)), ((), ())), preferred_element_type=F32)


def dot_nt(a, b):
    return lax.dot_general(a, b, (((1,), (1,)), ((), ())), preferred_element_type=F32)


def dot_tn(a, b):
    return lax.dot_general(a, b, (((0,), (0,)), ((), ())), preferred_element_type=F32)


def one_hot(mask):
    return jnp.where(mask, 1.0, 0.0).astype(BF)


def selected_token(row, offs, group):
    token = jnp.full(row.shape, -1, jnp.int32)
    for start, stop, level in ANY_ROWS:
        inside = (row >= start) & (row < stop)
        token = jnp.where(inside, (row - start) * 2**level + offs[level, group], token)
    return token


def selector(offs, group):
    shape = (128, TOKENS)
    row = lax.broadcasted_iota(jnp.int32, shape, 0)
    return one_hot(selected_token(row, offs, group) == lax.broadcasted_iota(jnp.int32, shape, 1))


def placer(offs, group):
    shape = (TOKENS, 128)
    row = lax.broadcasted_iota(jnp.int32, shape, 1)
    return one_hot(selected_token(row, offs, group) == lax.broadcasted_iota(jnp.int32, shape, 0))


def group_rows(keys_ref, values_ref, group):
    lanes = slice(group * D, (group + 1) * D)
    return jnp.concatenate([keys_ref[:, lanes], values_ref[:, lanes]], 1)


def select_kernel(offs, keys, values, first, middle, tail, last):
    first_group = pl.program_id(0) * TOGETHER
    for j in range(TOGETHER):
        rows = dot(selector(offs, first_group + j), group_rows(keys, values, j))
        first[j] = rows[0:64].astype(BF)
        middle[j] = rows[64:128].astype(BF)
        tail[j] = rows[96:128].astype(BF)
        last[j] = rows[112:128].astype(BF)


def extra_rows(ref, group):
    at = 40 * (group % 2)
    return ref[group // 2].astype(F32)[at : at + 40]


def compact_kernel(middle, one, two, three, lift, extra):
    whole = []
    for g in range(GROUPS):
        mine, a, b, c = [ref[g].astype(F32) for ref in (middle, one, two, three)]
        last = [a[16:24], b[:8], c[:8]]
        lift[g] = jnp.concatenate([mine[0:48], a[0:16], mine[48:56]] + last, 0).astype(BF)
        whole += [a[0:16]] + last
        if g % 2:
            extra[g // 2] = jnp.concatenate(whole, 0).astype(BF)
            whole = []


def across_kernel(offs, keys, values, _, across):
    for g in range(GROUPS):
        across[g] = dot(selector(offs, g), group_rows(keys, values, g)).astype(BF)


def assemble_kernel(across, x_far, lift_up, lift_down, _, __, out):
    for g in range(GROUPS):
        far, extra = across[g].astype(F32), extra_rows(x_far, g)
        far = jnp.concatenate([far[0:112], extra[0:16], far[112:120], extra[16:40]], 0).astype(BF)
        out[g, 0:64] = far[0:64]
        for i, at in enumerate((0, 32, 64)):
            rows = [far[64 + at : 96 + at], lift_up[g, at : at + 32], lift_down[g, at : at + 32]]
            out[g, 96 * i + 64 : 96 * i + 160] = jnp.concatenate(rows, 0)


def by_level(rows):
    parts = []
    for start, stop in ((0, 64), (64, 96), (96, 112), (112, 120), (120, 128)):
        parts += [rows[start:stop, h * D : (h + 1) * D] for h in range(HEADS)]
    return jnp.concatenate(parts, 0)


def by_selection(rows):
    heads = []
    for h in range(HEADS):
        parts = []
        base = 0
        for count in (64, 32, 16, 8, 8):
            parts.append(rows[base + h * count : base + (h + 1) * count])
            base += HEADS * count
        heads.append(jnp.concatenate(parts, 0))
    return jnp.concatenate(heads, 1)


def heads_to_lanes(x):
    count = x.shape[0] // HEADS
    lane = lax.broadcasted_iota(jnp.int32, (count, 128), 1) & (HEADS - 1)
    out = x[(HEADS - 1) * count :]
    for h in range(HEADS - 1):
        out = jnp.where(lane == h, x[h * count : (h + 1) * count], out)
    return out


def wide_lanes(j):
    return slice(j * WIDE, (j + 1) * WIDE)


def by_head(rows):
    return jnp.concatenate([rows[:, h * D : (h + 1) * D] for h in range(HEADS)], 0)


def by_token(rows):
    count = rows.shape[0] // HEADS
    return jnp.concatenate([rows[h * count : (h + 1) * count] for h in range(HEADS)], 1)


def expand(x):
    return jnp.concatenate([jnp.broadcast_to(x[:, h : h + 1], x.shape) for h in range(HEADS)], 0)


def beside(x):
    high = x.astype(BF).astype(F32)
    lane = lax.broadcasted_iota(jnp.int32, x.shape, 1)
    both = jnp.where(lane < 64, high, x - high)
    return jnp.concatenate(
        [jnp.where((lane & (HEADS - 1)) == h, both, 0.0) for h in range(HEADS)], 0
    ).astype(BF)


def minus_lanes():
    lane = lax.broadcasted_iota(jnp.int32, (2 * D, D), 1)
    return jnp.where((lane & 63) < HEADS, -1.0, 0.0).astype(BF)


def forward(queries, keys, values):
    ones = jnp.ones((2 * D, D), BF)
    scores = [dot_nt(q, k) * (SCALE * LOG2E) for q, k in zip(queries, keys)]
    peaks = [jnp.max(x, 1, keepdims=True) for x in scores]
    powers = [jnp.exp2(x - p).astype(BF) for x, p in zip(scores, peaks)]
    outs = [dot(p, jnp.concatenate([v, ones], 1)) for p, v in zip(powers, values)]
    peaks = [heads_to_lanes(jnp.broadcast_to(p, (p.shape[0], 128))) for p in peaks]
    lses = [p + jnp.log2(heads_to_lanes(out[:, D:])) for p, out in zip(peaks, outs)]
    return powers, peaks, lses, [out[:, :D] for out in outs]


def backward(queries, scaled, keys, values, powers, shifts):
    minus = minus_lanes()
    weights = [
        dot_nt(jnp.concatenate([g, beside(d)], 1), jnp.concatenate([v, minus], 1))
        for g, d, v in zip(scaled, shifts, values)
    ]
    scores = [(p.astype(F32) * w).astype(BF) for p, w in zip(powers, weights)]
    grad_values = [dot_tn(g, p).T for g, p in zip(scaled, powers)]
    grad_keys = [dot_tn(q, x).T * SCALE for q, x in zip(queries, scores)]
    pairs = [jnp.concatenate(pair, 1).astype(BF) for pair in zip(grad_keys, grad_values)]
    return pairs, [dot(x, k) * SCALE for x, k in zip(scores, keys)]


def whole_rows(own_ref, far_ref, j):
    lanes = slice(j * D, (j + 1) * D)
    return jnp.concatenate([own_ref[:, lanes], far_ref[:, lanes]], 0)


def level1_rows(refs, j, lanes):
    return jnp.concatenate([ref[j, 0:64, lanes] for ref in refs], 0)


K_LANES, V_LANES = slice(0, D), slice(D, 2 * D)


def early_kernel(offs, q_ref, g_ref, k_ref, v_ref, kp_ref, vp_ref, *refs):
    qs_ref, gs_ref, power0, peak0, lse0, out0 = refs[-6:]
    members = range(TOGETHER)
    first_group = pl.program_id(0) * TOGETHER
    for j in members:
        pick = selector(offs, first_group + j)
        qs_ref[j] = by_level(dot(pick, q_ref[:, wide_lanes(j)])).astype(BF)
        gs_ref[j] = by_level(dot(pick, g_ref[:, wide_lanes(j)])).astype(BF)
    queries = [by_head(q_ref[:, wide_lanes(j)]) for j in members]
    keys = [whole_rows(k_ref, kp_ref, j) for j in members]
    values = [whole_rows(v_ref, vp_ref, j) for j in members]
    for j, (power, peak, lse, out) in enumerate(zip(*forward(queries, keys, values))):
        power0[j], peak0[j], lse0[j], out0[j] = power, peak, lse, out


def place_levels(offs, first_group, rows):
    rows = [by_selection(x).astype(BF) for x in rows]
    return [dot(placer(offs, first_group + j), r) for j, r in enumerate(rows)]


def attention_kernel(
    offs, qs_ref, gs_ref, g_ref, first, lift, late, other_first, other_lift, other_late, peak0, lse0, out0,
    att_ref, part_ref, down_ref, dother_ref, factor0, shift0, power1, factor1, shift1,
    level_ref, token_ref, delta_ref,
):
    members = range(TOGETHER)
    first_group = pl.program_id(0) * TOGETHER
    bounds = ((0, 256), (256, 384), (384, 448), (448, 480))
    starts = [[(offs[k, first_group + j], 128 >> k) for k in range(1, 5)] for j in members]

    def kept(k, lanes):
        if k == 0:
            return [level1_rows((first, late, other_first, other_late), j, lanes) for j in members]
        mine, rest = slice(32 * k - 32, 32 * k), slice(96 * k - 32, 96 * k + 64)
        parts = ((lift, mine), (late, rest), (other_lift, mine), (other_late, rest))
        return [jnp.concatenate([ref[j, at, lanes] for ref, at in parts], 0) for j in members]

    def for_levels(ref, xs):
        for j, x in enumerate(xs):
            ref[j] = x
        return [
            [ref[j, pl.ds(starts[j][k][0], starts[j][k][1], 2 ** (k + 1)), :] for j in members]
            for k in range(4)
        ]

    level_ref[...] = jnp.full(level_ref.shape, -1e30, F32)
    queries = [[qs_ref[j, a:b] for j in members] for a, b in bounds]
    grads = [[gs_ref[j, a:b] for j in members] for a, b in bounds]
    keys = [kept(k, K_LANES) for k in range(4)]
    values = [kept(k, V_LANES) for k in range(4)]
    results = [forward(queries[k], keys[k], values[k]) for k in range(4)]

    for k in range(4):
        for j in members:
            start, count = starts[j][k]
            level_ref[j, k, pl.ds(start, count, 2 ** (k + 1)), :] = results[k][2][j]
    firsts = [lse0[j] for j in members]
    tops = [functools.reduce(jnp.maximum, [level_ref[j, k] for k in range(4)], firsts[j]) for j in members]
    sums = [
        jnp.exp2(firsts[j] - tops[j]) + sum(jnp.exp2(level_ref[j, k] - tops[j]) for k in range(4))
        for j in members
    ]
    merged = [top + jnp.log2(x) for top, x in zip(tops, sums)]
    factors = [
        [jnp.exp2(p - m) for p, m in zip(results[k][1], column)]
        for k, column in enumerate(for_levels(token_ref, merged))
    ]
    spread = [[expand(f) for f in fs] for fs in factors]
    pad = [jnp.zeros((32, D), F32)]
    parts = [[out * f for out, f in zip(results[k][3], spread[k])] for k in range(4)]
    placed = place_levels(offs, first_group, [jnp.concatenate(list(p) + pad, 0) for p in zip(*parts)])
    deltas = []
    for j in members:
        factor = jnp.exp2(peak0[j] - merged[j])
        attended = (placed[j] + by_token(out0[j] * expand(factor))).astype(BF)
        att_ref[:, wide_lanes(j)] = attended
        product = g_ref[:, wide_lanes(j)].astype(F32) * attended.astype(F32)
        total = [
            jnp.broadcast_to(jnp.sum(product[:, h * D : (h + 1) * D], 1, keepdims=True), (TOKENS, 128))
            for h in range(HEADS)
        ]
        deltas.append(heads_to_lanes(jnp.concatenate(total, 0)))
        factor0[j] = factor
        shift0[j] = factor * deltas[j]
    shifts = [
        [f * d for f, d in zip(factors[k], column)] for k, column in enumerate(for_levels(delta_ref, deltas))
    ]
    for j in members:
        power1[j], factor1[j], shift1[j] = results[0][0][j], factors[0][j], shifts[0][j]
    for k in range(1, 4):
        scaled = [(g.astype(F32) * f).astype(BF) for g, f in zip(grads[k], spread[k])]
        pairs, part = backward(queries[k], scaled, keys[k], values[k], results[k][0], shifts[k])
        at = slice(128 * k - 128, 128 * k)
        for j in members:
            down_ref[j, at] = pairs[j][:128]
            dother_ref[j, at] = pairs[j][128:]
            part_ref[j, bounds[k][0] - 256 : bounds[k][1] - 256] = part[j]


def return0_kernel(
    q_ref, g_ref, k_ref, v_ref, kp_ref, vp_ref, power_ref, factor_ref, shift_ref, part_ref, *refs
):
    dq_ref, d0_ref = refs[-2:]
    members = range(TOGETHER)
    queries = [by_head(q_ref[:, wide_lanes(j)]) for j in members]
    keys = [whole_rows(k_ref, kp_ref, j) for j in members]
    values = [whole_rows(v_ref, vp_ref, j) for j in members]
    scaled = [
        (by_head(g_ref[:, wide_lanes(j)]).astype(F32) * expand(factor_ref[j])).astype(BF) for j in members
    ]
    powers, shifts = [power_ref[j] for j in members], [shift_ref[j] for j in members]
    pairs, parts = backward(queries, scaled, keys, values, powers, shifts)
    for j in members:
        d0_ref[j] = pairs[j]
        dq_ref[:, wide_lanes(j)] = (by_token(parts[j]) + part_ref[:, wide_lanes(j)]).astype(BF)


def return1_kernel(
    offs, qs_ref, gs_ref, first, late, other_first, other_late, power_ref, factor_ref, shift_ref, part_ref,
    dq_ref, down_ref, dother_ref,
):
    level1 = (first, late, other_first, other_late)
    members = range(TOGETHER)
    queries = [qs_ref[j, 0:256] for j in members]
    keys = [level1_rows(level1, j, K_LANES) for j in members]
    values = [level1_rows(level1, j, V_LANES) for j in members]
    scaled = [(gs_ref[j, 0:256].astype(F32) * expand(factor_ref[j])).astype(BF) for j in members]
    powers, shifts = [power_ref[j] for j in members], [shift_ref[j] for j in members]
    pairs, parts = backward(queries, scaled, keys, values, powers, shifts)
    pad = [jnp.zeros((32, D), F32)]
    rows = [jnp.concatenate([parts[j], part_ref[j]] + pad, 0) for j in members]
    for j, x in enumerate(place_levels(offs, pl.program_id(0) * TOGETHER, rows)):
        down_ref[j] = pairs[j][:128]
        dother_ref[j] = pairs[j][128:]
        dq_ref[:, wide_lanes(j)] = x


def reduce_kernel(mine, theirs, _, mid_kept, mid_far, up, down, x_far, x_kept):
    zero = jnp.zeros((8, 2 * D), F32)
    whole = [[], []]
    for g in range(GROUPS):
        total = mine[g].astype(F32) + theirs[g].astype(F32)
        for z, ref in enumerate((mid_kept, mid_far, up, down)):
            second, third, fourth = [total[s + 32 * z : s + 32 * z + 32] for s in (0, 128, 256)]
            if z >= 2:
                ref[g] = jnp.concatenate([second, third, fourth], 0).astype(BF)
                continue
            ref[g] = jnp.concatenate([second, third[:16], fourth[:8], zero], 0).astype(BF)
            whole[z] += [third[16:], fourth[8:]]
        if g % 2:
            x_kept[g // 2] = jnp.concatenate(whole[0], 0)
            x_far[g // 2] = jnp.concatenate(whole[1], 0).astype(BF)
            whole = [[], []]


def place_kernel(offs, d0, mine, theirs, mid_far, _, *refs):
    for g in range(GROUPS):
        first = (mine[g, 64:128].astype(F32) + theirs[g, 64:128].astype(F32)).astype(BF)
        rows = jnp.concatenate([first, mid_far[g]], 0)
        whole = (d0[g, 128:256].astype(F32) + dot(placer(offs, g), rows)).astype(BF)
        refs[0][g] = whole


def cross_kernel(kept, far, down, up, one, two, three):
    zero = jnp.zeros((8, 2 * D), F32)
    for g in range(GROUPS):
        sides = up[g].astype(F32) + down[g].astype(F32)
        total = extra_rows(kept, g) + extra_rows(far, g)
        third = total[0:16] + sides[48:64]
        fourth = total[16:40] + sides[72:96]
        one[g] = jnp.concatenate([third, fourth[0:8], zero], 0).astype(BF)
        two[g] = jnp.concatenate([fourth[8:16], zero], 0).astype(BF)
        three[g] = jnp.concatenate([fourth[16:24], zero], 0).astype(BF)


def keep_kernel(offs, d0, mine, theirs, mid_kept, down, up, one, two, three, kept):
    for g in range(GROUPS):
        mid = mid_kept[g].astype(F32)
        sides = up[g].astype(F32) + down[g].astype(F32)
        a, b, c = one[g].astype(F32), two[g].astype(F32), three[g].astype(F32)
        rows = jnp.concatenate(
            [
                mine[g, 0:64].astype(F32) + theirs[g, 0:64].astype(F32),
                mid[0:32] + sides[0:32],
                mid[32:48] + sides[32:48] + a[0:16],
                mid[48:56] + sides[64:72] + a[16:24] + b[0:8] + c[0:8],
                jnp.zeros((8, 2 * D), F32),
            ],
            0,
        ).astype(BF)
        kept[g] = d0[g, 0:128].astype(F32) + dot(placer(offs, g), rows)


def finish_kernel(kept, *refs):
    *fars, dk_ref, dv_ref = refs
    for g in range(GROUPS):
        whole = kept[g] + fars[0][g].astype(F32)
        dk_ref[:, g * D : (g + 1) * D] = whole[:, :D].astype(BF)
        dv_ref[:, g * D : (g + 1) * D] = whole[:, D:].astype(BF)


def whole_call(body, name, outs, offs, *arrays, after=()):
    specs = [pl.BlockSpec(memory_space=pltpu.VMEM)] * len(arrays)
    specs += [pl.BlockSpec(memory_space=pl.ANY)] * len(after)
    arrays = arrays + tuple(after)
    if offs is not None:
        specs = [pl.BlockSpec(memory_space=pltpu.SMEM)] + specs
        arrays = (offs,) + arrays
    shapes = [jax.ShapeDtypeStruct(shape, dtype) for shape, dtype in outs]
    return pl.pallas_call(
        body,
        name=name,
        out_shape=shapes,
        in_specs=specs,
        out_specs=[pl.BlockSpec(memory_space=pltpu.VMEM)] * len(shapes),
        cost_estimate=pl.CostEstimate(flops=0, bytes_accessed=4 * 10**6, transcendentals=0),
        compiler_params=pltpu.CompilerParams(vmem_limit_bytes=VMEM_LIMIT),
    )(*arrays)


def grid_call(body, name, offs, inputs, outs, scratch=(), after=()):
    def spec(shape, offset=None):
        if offset == 0:
            return pl.BlockSpec((TOGETHER, 64) + shape[2:], lambda i: (i, 0, 0))
        if offset:
            return pl.BlockSpec((TOKENS, TOGETHER * D), lambda i: (0, i + offset - 1))
        if len(shape) == 2:
            return pl.BlockSpec((TOKENS, shape[1] * TOGETHER // GROUPS), lambda i: (0, i))
        return pl.BlockSpec((TOGETHER,) + shape[1:], lambda i: (i, 0, 0))

    specs = [spec(x[0].shape, x[1]) if isinstance(x, tuple) else spec(x.shape) for x in inputs]
    inputs = [x[0] if isinstance(x, tuple) else x for x in inputs]
    specs += [pl.BlockSpec(memory_space=pl.ANY)] * len(after)
    arrays = tuple(inputs) + tuple(after)
    if offs is not None:
        specs = [pl.BlockSpec(memory_space=pltpu.SMEM)] + specs
        arrays = (offs,) + arrays
    return pl.pallas_call(
        body,
        name=name,
        grid=(GROUPS // TOGETHER,),
        in_specs=specs,
        out_specs=[spec(shape) for shape, _ in outs],
        out_shape=[jax.ShapeDtypeStruct(shape, dtype) for shape, dtype in outs],
        scratch_shapes=list(scratch),
        cost_estimate=pl.CostEstimate(flops=4 * 10**9, bytes_accessed=16 * 10**6, transcendentals=10**6),
        compiler_params=pltpu.CompilerParams(vmem_limit_bytes=GRID_LIMIT),
    )(*arrays)


def routes(count):
    def along_z(i, step):
        z = ((i & 1) * 2 + (i >> 2 & 1) + step) % 4
        return (i & ~5) | (z & 1) << 2 | z >> 1

    table = {
        "head": lambda i: i ^ 1,
        "near": lambda i: along_z(i, 1 if i & 4 else -1),
        "core": lambda i: i ^ 2,
        "up": lambda i: along_z(i, 1),
        "down": lambda i: along_z(i, -1),
        "x1": lambda i: i ^ 8,
        "x2": lambda i: i ^ 16,
        "x3": lambda i: i ^ 24,
    }
    return {name: [(i, to(i)) for i in range(count)] for name, to in table.items()}


def shards(count, queries, key_rows, value_rows, gradient, level_offsets):
    route = routes(count)

    def send(x, name):
        return lax.ppermute(x, AXES, route[name])

    other_offsets = send(level_offsets, "near")
    low = lax.axis_index("head") == 0
    offs = jnp.where(
        low,
        jnp.concatenate([level_offsets, other_offsets], 1),
        jnp.concatenate([other_offsets, level_offsets], 1),
    )
    pair = jnp.concatenate([key_rows, value_rows], 1)
    far_keys = send(key_rows, "head")
    far_values = send(value_rows, "head")

    rows = lambda n, dtype=BF: ((GROUPS, n, 2 * D), dtype)
    extras = lambda dtype: ((GROUPS // 2, 80, 2 * D), dtype)
    wide = lambda dtype: ((TOKENS, GROUPS * WIDE), dtype)
    first, middle, tail, last = grid_call(
        select_kernel, "select", offs, [(pair, 1), (pair, 1 + GROUPS // TOGETHER)],
        [rows(64), rows(64), rows(32), rows(16)],
    )
    lift, extra = whole_call(
        compact_kernel, "compact", [rows(96), extras(BF)], None,
        middle, send(tail, "x1"), send(last, "x2"), send(last, "x3"),
    )
    lift_down = send(lift, "up")
    lift_up = send(lift, "down")
    extra_far = send(extra, "head")
    tall = lambda n, dtype=F32: ((GROUPS, n, D), dtype)
    kv = [key_rows, value_rows, far_keys, far_values]
    qs, gs, power0, peak0, lse0, out0 = grid_call(
        early_kernel, "early", offs, [queries, gradient, *kv],
        [tall(512, BF), tall(512, BF), rows(512), tall(128), tall(128), tall(512)], after=(extra,),
    )
    (across,) = whole_call(
        across_kernel, "across", [rows(128)], offs, far_keys, far_values, after=(lse0,)
    )
    first_sent, lift_sent, _ = lax.optimization_barrier((first, lift, (far_keys, far_values)))
    other_first, other_lift = send(first_sent, "core"), send(lift_sent, "core")
    (late,) = whole_call(
        assemble_kernel, "assemble", [rows(352)], None, across, extra_far, lift_up, lift_down,
        after=(other_first, other_lift),
    )
    other_late = send(late, "core")
    near = [first, lift, late, other_first, other_lift, other_late]
    stats = pltpu.VMEM((TOGETHER, TOKENS, 128), F32)
    attended, part, down_own, down_other, factor0, shift0, power1, factor1, shift1 = grid_call(
        attention_kernel, "attention", offs,
        [qs, gs, gradient, *near, peak0, lse0, out0],
        [wide(BF), tall(224), rows(384), rows(384), tall(128), tall(128), rows(256), tall(64), tall(64)],
        scratch=[pltpu.VMEM((TOGETHER, 4, TOKENS, 128), F32), stats, stats],
    )
    theirs = send(down_other, "core")
    placed, mine1, theirs1 = grid_call(
        return1_kernel, "return1", offs, [qs, gs, first, (late, 0), other_first, (other_late, 0), power1, factor1, shift1, part],
        [wide(F32), rows(128), rows(128)],
    )
    mid_kept, mid_far, up, down, x_far, x_kept = whole_call(
        reduce_kernel, "reduce", [rows(64), rows(64), rows(96), rows(96), extras(BF), extras(F32)],
        None, down_own, theirs, after=(mine1,),
    )
    from_down = send(up, "up")
    from_up = send(down, "down")
    x_far = send(x_far, "head")
    theirs1 = send(theirs1, "core")
    grad_queries, d0 = grid_call(
        return0_kernel, "return0", None, [queries, gradient, *kv, power0, factor0, shift0, placed],
        [wide(BF), rows(256)], after=(theirs1,),
    )
    half = ((TOGETHER, TOKENS, 2 * D), BF)
    fars = whole_call(
        place_kernel, "place", [rows(128)], offs, d0, mine1, theirs1, mid_far, after=(x_far,)
    )
    fars = [send(far, "head") for far in fars]
    one, two, three = whole_call(
        cross_kernel, "cross", [rows(32), rows(16), rows(16)], None, x_kept, x_far, from_down, from_up
    )
    one, two, three = send(one, "x1"), send(two, "x2"), send(three, "x3")
    out = ((TOKENS, GROUPS * D), BF)
    (kept,) = whole_call(
        keep_kernel, "keep", [rows(128, F32)], offs, d0, mine1, theirs1, mid_kept, from_down, from_up,
        one, two, three,
    )
    grad_keys, grad_values = whole_call(finish_kernel, "finish", [out, out], None, kept, *fars)
    return (attended, grad_queries, grad_keys, grad_values)


def solution(mesh):
    rows = P(AXES, None)
    return jax.shard_map(
        functools.partial(shards, mesh.size),
        mesh=mesh,
        in_specs=(rows, rows, rows, rows, P(None, "head")),
        out_specs=(rows, rows, rows, rows),
        check_vma=False,
    )
```

```python
import functools

import jax
import jax.numpy as jnp
from jax import lax
from jax.experimental import pallas as pl
from jax.experimental.pallas import tpu as pltpu
from jax.sharding import PartitionSpec as P

D = 128
GROUPS = 8
HEADS = 4
TOKENS = 128
TOGETHER = 4
WIDE = HEADS * D
SCALE = D ** (-0.5)
LOG2E = 1.4426950408889634
AXES = ("ctx", "head")
BF = jnp.bfloat16
F32 = jnp.float32
ANY_ROWS = ((0, 64, 1), (64, 96, 2), (96, 112, 3), (112, 120, 4))
VMEM_LIMIT = 24 * 1024 * 1024
GRID_LIMIT = 32 * 1024 * 1024


def dot(a, b):
    return lax.dot_general(a, b, (((1,), (0,)), ((), ())), preferred_element_type=F32)


def dot_nt(a, b):
    return lax.dot_general(a, b, (((1,), (1,)), ((), ())), preferred_element_type=F32)


def dot_tn(a, b):
    return lax.dot_general(a, b, (((0,), (0,)), ((), ())), preferred_element_type=F32)


def one_hot(mask):
    return jnp.where(mask, 1.0, 0.0).astype(BF)


def selected_token(row, offs, group):
    token = jnp.full(row.shape, -1, jnp.int32)
    for start, stop, level in ANY_ROWS:
        inside = (row >= start) & (row < stop)
        token = jnp.where(inside, (row - start) * 2**level + offs[level, group], token)
    return token


def selector(offs, group):
    shape = (128, TOKENS)
    row = lax.broadcasted_iota(jnp.int32, shape, 0)
    return one_hot(selected_token(row, offs, group) == lax.broadcasted_iota(jnp.int32, shape, 1))


def placer(offs, group):
    shape = (TOKENS, 128)
    row = lax.broadcasted_iota(jnp.int32, shape, 1)
    return one_hot(selected_token(row, offs, group) == lax.broadcasted_iota(jnp.int32, shape, 0))


def group_rows(keys_ref, values_ref, group):
    lanes = slice(group * D, (group + 1) * D)
    return jnp.concatenate([keys_ref[:, lanes], values_ref[:, lanes]], 1)


def select_kernel(offs, keys, values, first, middle, tail, last):
    first_group = pl.program_id(0) * TOGETHER
    for j in range(TOGETHER):
        rows = dot(selector(offs, first_group + j), group_rows(keys, values, j))
        first[j] = rows[0:64].astype(BF)
        middle[j] = rows[64:128].astype(BF)
        tail[j] = rows[96:128].astype(BF)
        last[j] = rows[112:128].astype(BF)


def extra_rows(ref, group):
    at = 40 * (group % 2)
    return ref[group // 2].astype(F32)[at : at + 40]


def compact_kernel(middle, two, one, three, lift, extra):
    whole = []
    for g in range(GROUPS):
        mine, a, b, c = [ref[g].astype(F32) for ref in (middle, one, two, three)]
        last = [a[16:24], b[:8], c[:8]]
        lift[g] = jnp.concatenate([mine[0:48], a[0:16], mine[48:56]] + last, 0).astype(BF)
        whole += [a[0:16]] + last
        if g % 2:
            extra[g // 2] = jnp.concatenate(whole, 0).astype(BF)
            whole = []


def across_kernel(offs, keys, values, _, across):
    for g in range(GROUPS):
        across[g] = dot(selector(offs, g), group_rows(keys, values, g)).astype(BF)


def assemble_kernel(across, x_far, lift_up, lift_down, _, __, out):
    for g in range(GROUPS):
        far, extra = across[g].astype(F32), extra_rows(x_far, g)
        far = jnp.concatenate([far[0:112], extra[0:16], far[112:120], extra[16:40]], 0).astype(BF)
        out[g, 0:64] = far[0:64]
        for i, at in enumerate((0, 32, 64)):
            rows = [far[64 + at : 96 + at], lift_up[g, at : at + 32], lift_down[g, at : at + 32]]
            out[g, 96 * i + 64 : 96 * i + 160] = jnp.concatenate(rows, 0)


def by_level(rows):
    parts = []
    for start, stop in ((0, 64), (64, 96), (96, 112), (112, 120), (120, 128)):
        parts += [rows[start:stop, h * D : (h + 1) * D] for h in range(HEADS)]
    return jnp.concatenate(parts, 0)


def by_selection(rows):
    heads = []
    for h in range(HEADS):
        parts = []
        base = 0
        for count in (64, 32, 16, 8, 8):
            parts.append(rows[base + h * count : base + (h + 1) * count])
            base += HEADS * count
        heads.append(jnp.concatenate(parts, 0))
    return jnp.concatenate(heads, 1)


def heads_to_lanes(x):
    count = x.shape[0] // HEADS
    lane = lax.broadcasted_iota(jnp.int32, (count, 128), 1) & (HEADS - 1)
    out = x[(HEADS - 1) * count :]
    for h in range(HEADS - 1):
        out = jnp.where(lane == h, x[h * count : (h + 1) * count], out)
    return out


def wide_lanes(j):
    return slice(j * WIDE, (j + 1) * WIDE)


def by_head(rows):
    return jnp.concatenate([rows[:, h * D : (h + 1) * D] for h in range(HEADS)], 0)


def by_token(rows):
    count = rows.shape[0] // HEADS
    return jnp.concatenate([rows[h * count : (h + 1) * count] for h in range(HEADS)], 1)


def expand(x):
    return jnp.concatenate([jnp.broadcast_to(x[:, h : h + 1], x.shape) for h in range(HEADS)], 0)


def beside(x):
    high = x.astype(BF).astype(F32)
    lane = lax.broadcasted_iota(jnp.int32, x.shape, 1)
    both = jnp.where(lane < 64, high, x - high)
    return jnp.concatenate(
        [jnp.where((lane & (HEADS - 1)) == h, both, 0.0) for h in range(HEADS)], 0
    ).astype(BF)


def minus_lanes():
    lane = lax.broadcasted_iota(jnp.int32, (2 * D, D), 1)
    return jnp.where((lane & 63) < HEADS, -1.0, 0.0).astype(BF)


def forward(queries, keys, values):
    ones = jnp.ones((2 * D, D), BF)
    scores = [dot_nt(q, k) * (SCALE * LOG2E) for q, k in zip(queries, keys)]
    peaks = [jnp.max(x, 1, keepdims=True) for x in scores]
    powers = [jnp.exp2(x - p).astype(BF) for x, p in zip(scores, peaks)]
    outs = [dot(p, jnp.concatenate([v, ones], 1)) for p, v in zip(powers, values)]
    peaks = [heads_to_lanes(jnp.broadcast_to(p, (p.shape[0], 128))) for p in peaks]
    lses = [p + jnp.log2(heads_to_lanes(out[:, D:])) for p, out in zip(peaks, outs)]
    return powers, peaks, lses, [out[:, :D] for out in outs]


def backward(queries, scaled, keys, values, powers, shifts):
    minus = minus_lanes()
    weights = [
        dot_nt(jnp.concatenate([g, beside(d)], 1), jnp.concatenate([v, minus], 1))
        for g, d, v in zip(scaled, shifts, values)
    ]
    scores = [(p.astype(F32) * w).astype(BF) for p, w in zip(powers, weights)]
    grad_values = [dot_tn(g, p).T for g, p in zip(scaled, powers)]
    grad_keys = [dot_tn(q, x).T * SCALE for q, x in zip(queries, scores)]
    pairs = [jnp.concatenate(pair, 1).astype(BF) for pair in zip(grad_keys, grad_values)]
    return pairs, [dot(x, k) * SCALE for x, k in zip(scores, keys)]


def whole_rows(own_ref, far_ref, j):
    lanes = slice(j * D, (j + 1) * D)
    return jnp.concatenate([own_ref[:, lanes], far_ref[:, lanes]], 0)


def level1_rows(refs, j, lanes):
    return jnp.concatenate([ref[j, 0:64, lanes] for ref in refs], 0)


K_LANES, V_LANES = slice(0, D), slice(D, 2 * D)


def early_kernel(offs, q_ref, g_ref, k_ref, v_ref, kp_ref, vp_ref, *refs):
    qs_ref, gs_ref, power0, peak0, lse0, out0 = refs[-6:]
    members = range(TOGETHER)
    first_group = pl.program_id(0) * TOGETHER
    for j in members:
        pick = selector(offs, first_group + j)
        qs_ref[j] = by_level(dot(pick, q_ref[:, wide_lanes(j)])).astype(BF)
        gs_ref[j] = by_level(dot(pick, g_ref[:, wide_lanes(j)])).astype(BF)
    queries = [by_head(q_ref[:, wide_lanes(j)]) for j in members]
    keys = [whole_rows(k_ref, kp_ref, j) for j in members]
    values = [whole_rows(v_ref, vp_ref, j) for j in members]
    for j, (power, peak, lse, out) in enumerate(zip(*forward(queries, keys, values))):
        power0[j], peak0[j], lse0[j], out0[j] = power, peak, lse, out


def place_levels(offs, first_group, rows):
    rows = [by_selection(x).astype(BF) for x in rows]
    return [dot(placer(offs, first_group + j), r) for j, r in enumerate(rows)]


def attention_kernel(
    offs, qs_ref, gs_ref, g_ref, first, lift, late, other_first, other_lift, other_late, peak0, lse0, out0,
    att_ref, part_ref, down_ref, dother_ref, factor0, shift0, power1, factor1, shift1,
    level_ref, token_ref, delta_ref,
):
    members = range(TOGETHER)
    first_group = pl.program_id(0) * TOGETHER
    bounds = ((0, 256), (256, 384), (384, 448), (448, 480))
    starts = [[(offs[k, first_group + j], 128 >> k) for k in range(1, 5)] for j in members]

    def kept(k, lanes):
        if k == 0:
            return [level1_rows((first, late, other_first, other_late), j, lanes) for j in members]
        mine, rest = slice(32 * k - 32, 32 * k), slice(96 * k - 32, 96 * k + 64)
        parts = ((lift, mine), (late, rest), (other_lift, mine), (other_late, rest))
        return [jnp.concatenate([ref[j, at, lanes] for ref, at in parts], 0) for j in members]

    def for_levels(ref, xs):
        for j, x in enumerate(xs):
            ref[j] = x
        return [
            [ref[j, pl.ds(starts[j][k][0], starts[j][k][1], 2 ** (k + 1)), :] for j in members]
            for k in range(4)
        ]

    level_ref[...] = jnp.full(level_ref.shape, -1e30, F32)
    queries = [[qs_ref[j, a:b] for j in members] for a, b in bounds]
    grads = [[gs_ref[j, a:b] for j in members] for a, b in bounds]
    keys = [kept(k, K_LANES) for k in range(4)]
    values = [kept(k, V_LANES) for k in range(4)]
    results = [forward(queries[k], keys[k], values[k]) for k in range(4)]

    for k in range(4):
        for j in members:
            start, count = starts[j][k]
            level_ref[j, k, pl.ds(start, count, 2 ** (k + 1)), :] = results[k][2][j]
    firsts = [lse0[j] for j in members]
    tops = [functools.reduce(jnp.maximum, [level_ref[j, k] for k in range(4)], firsts[j]) for j in members]
    sums = [
        jnp.exp2(firsts[j] - tops[j]) + sum(jnp.exp2(level_ref[j, k] - tops[j]) for k in range(4))
        for j in members
    ]
    merged = [top + jnp.log2(x) for top, x in zip(tops, sums)]
    factors = [
        [jnp.exp2(p - m) for p, m in zip(results[k][1], column)]
        for k, column in enumerate(for_levels(token_ref, merged))
    ]
    spread = [[expand(f) for f in fs] for fs in factors]
    pad = [jnp.zeros((32, D), F32)]
    parts = [[out * f for out, f in zip(results[k][3], spread[k])] for k in range(4)]
    placed = place_levels(offs, first_group, [jnp.concatenate(list(p) + pad, 0) for p in zip(*parts)])
    deltas = []
    for j in members:
        factor = jnp.exp2(peak0[j] - merged[j])
        attended = (placed[j] + by_token(out0[j] * expand(factor))).astype(BF)
        att_ref[:, wide_lanes(j)] = attended
        product = g_ref[:, wide_lanes(j)].astype(F32) * attended.astype(F32)
        total = [
            jnp.broadcast_to(jnp.sum(product[:, h * D : (h + 1) * D], 1, keepdims=True), (TOKENS, 128))
            for h in range(HEADS)
        ]
        deltas.append(heads_to_lanes(jnp.concatenate(total, 0)))
        factor0[j] = factor
        shift0[j] = factor * deltas[j]
    shifts = [
        [f * d for f, d in zip(factors[k], column)] for k, column in enumerate(for_levels(delta_ref, deltas))
    ]
    for j in members:
        power1[j], factor1[j], shift1[j] = results[0][0][j], factors[0][j], shifts[0][j]
    for k in range(1, 4):
        scaled = [(g.astype(F32) * f).astype(BF) for g, f in zip(grads[k], spread[k])]
        pairs, part = backward(queries[k], scaled, keys[k], values[k], results[k][0], shifts[k])
        at = slice(128 * k - 128, 128 * k)
        for j in members:
            down_ref[j, at] = pairs[j][:128]
            dother_ref[j, at] = pairs[j][128:]
            part_ref[j, bounds[k][0] - 256 : bounds[k][1] - 256] = part[j]


def return0_kernel(
    q_ref, g_ref, k_ref, v_ref, kp_ref, vp_ref, power_ref, factor_ref, shift_ref, part_ref, *refs
):
    dq_ref, d0_ref = refs[-2:]
    members = range(TOGETHER)
    queries = [by_head(q_ref[:, wide_lanes(j)]) for j in members]
    keys = [whole_rows(k_ref, kp_ref, j) for j in members]
    values = [whole_rows(v_ref, vp_ref, j) for j in members]
    scaled = [
        (by_head(g_ref[:, wide_lanes(j)]).astype(F32) * expand(factor_ref[j])).astype(BF) for j in members
    ]
    powers, shifts = [power_ref[j] for j in members], [shift_ref[j] for j in members]
    pairs, parts = backward(queries, scaled, keys, values, powers, shifts)
    for j in members:
        d0_ref[j] = pairs[j]
        dq_ref[:, wide_lanes(j)] = (by_token(parts[j]) + part_ref[:, wide_lanes(j)]).astype(BF)


def return1_kernel(
    offs, qs_ref, gs_ref, first, late, other_first, other_late, power_ref, factor_ref, shift_ref, part_ref,
    dq_ref, down_ref, dother_ref,
):
    level1 = (first, late, other_first, other_late)
    members = range(TOGETHER)
    queries = [qs_ref[j, 0:256] for j in members]
    keys = [level1_rows(level1, j, K_LANES) for j in members]
    values = [level1_rows(level1, j, V_LANES) for j in members]
    scaled = [(gs_ref[j, 0:256].astype(F32) * expand(factor_ref[j])).astype(BF) for j in members]
    powers, shifts = [power_ref[j] for j in members], [shift_ref[j] for j in members]
    pairs, parts = backward(queries, scaled, keys, values, powers, shifts)
    pad = [jnp.zeros((32, D), F32)]
    rows = [jnp.concatenate([parts[j], part_ref[j]] + pad, 0) for j in members]
    for j, x in enumerate(place_levels(offs, pl.program_id(0) * TOGETHER, rows)):
        down_ref[j] = pairs[j][:128]
        dother_ref[j] = pairs[j][128:]
        dq_ref[:, wide_lanes(j)] = x


def reduce_kernel(mine, theirs, _, mid_kept, mid_far, up, down, x_far, x_kept):
    zero = jnp.zeros((8, 2 * D), F32)
    whole = [[], []]
    for g in range(GROUPS):
        total = mine[g].astype(F32) + theirs[g].astype(F32)
        for z, ref in enumerate((mid_kept, mid_far, up, down)):
            second, third, fourth = [total[s + 32 * z : s + 32 * z + 32] for s in (0, 128, 256)]
            if z >= 2:
                ref[g] = jnp.concatenate([second, third, fourth], 0).astype(BF)
                continue
            ref[g] = jnp.concatenate([second, third[:16], fourth[:8], zero], 0).astype(BF)
            whole[z] += [third[16:], fourth[8:]]
        if g % 2:
            x_kept[g // 2] = jnp.concatenate(whole[0], 0)
            x_far[g // 2] = jnp.concatenate(whole[1], 0).astype(BF)
            whole = [[], []]


def place_kernel(offs, d0, mine, theirs, mid_far, _, *refs):
    for g in range(GROUPS):
        first = (mine[g, 64:128].astype(F32) + theirs[g, 64:128].astype(F32)).astype(BF)
        rows = jnp.concatenate([first, mid_far[g]], 0)
        whole = (d0[g, 128:256].astype(F32) + dot(placer(offs, g), rows)).astype(BF)
        refs[0][g] = whole


def cross_kernel(kept, far, down, up, one, two, three):
    zero = jnp.zeros((8, 2 * D), F32)
    for g in range(GROUPS):
        sides = up[g].astype(F32) + down[g].astype(F32)
        total = extra_rows(kept, g) + extra_rows(far, g)
        third = total[0:16] + sides[48:64]
        fourth = total[16:40] + sides[72:96]
        one[g] = jnp.concatenate([third, fourth[0:8], zero], 0).astype(BF)
        two[g] = jnp.concatenate([fourth[8:16], zero], 0).astype(BF)
        three[g] = jnp.concatenate([fourth[16:24], zero], 0).astype(BF)


def keep_kernel(offs, d0, mine, theirs, mid_kept, down, up, one, two, three, kept):
    for g in range(GROUPS):
        mid = mid_kept[g].astype(F32)
        sides = up[g].astype(F32) + down[g].astype(F32)
        a, b, c = one[g].astype(F32), two[g].astype(F32), three[g].astype(F32)
        rows = jnp.concatenate(
            [
                mine[g, 0:64].astype(F32) + theirs[g, 0:64].astype(F32),
                mid[0:32] + sides[0:32],
                mid[32:48] + sides[32:48] + a[0:16],
                mid[48:56] + sides[64:72] + a[16:24] + b[0:8] + c[0:8],
                jnp.zeros((8, 2 * D), F32),
            ],
            0,
        ).astype(BF)
        kept[g] = d0[g, 0:128].astype(F32) + dot(placer(offs, g), rows)


def finish_kernel(kept, *refs):
    *fars, dk_ref, dv_ref = refs
    for g in range(GROUPS):
        whole = kept[g] + fars[0][g].astype(F32)
        dk_ref[:, g * D : (g + 1) * D] = whole[:, :D].astype(BF)
        dv_ref[:, g * D : (g + 1) * D] = whole[:, D:].astype(BF)


def whole_call(body, name, outs, offs, *arrays, after=()):
    specs = [pl.BlockSpec(memory_space=pltpu.VMEM)] * len(arrays)
    specs += [pl.BlockSpec(memory_space=pl.ANY)] * len(after)
    arrays = arrays + tuple(after)
    if offs is not None:
        specs = [pl.BlockSpec(memory_space=pltpu.SMEM)] + specs
        arrays = (offs,) + arrays
    shapes = [jax.ShapeDtypeStruct(shape, dtype) for shape, dtype in outs]
    return pl.pallas_call(
        body,
        name=name,
        out_shape=shapes,
        in_specs=specs,
        out_specs=[pl.BlockSpec(memory_space=pltpu.VMEM)] * len(shapes),
        cost_estimate=pl.CostEstimate(flops=0, bytes_accessed=4 * 10**6, transcendentals=0),
        compiler_params=pltpu.CompilerParams(vmem_limit_bytes=VMEM_LIMIT),
    )(*arrays)


def grid_call(body, name, offs, inputs, outs, scratch=(), after=()):
    def spec(shape, offset=None):
        if offset == 0:
            return pl.BlockSpec((TOGETHER, 64) + shape[2:], lambda i: (i, 0, 0))
        if offset:
            return pl.BlockSpec((TOKENS, TOGETHER * D), lambda i: (0, i + offset - 1))
        if len(shape) == 2:
            return pl.BlockSpec((TOKENS, shape[1] * TOGETHER // GROUPS), lambda i: (0, i))
        return pl.BlockSpec((TOGETHER,) + shape[1:], lambda i: (i, 0, 0))

    specs = [spec(x[0].shape, x[1]) if isinstance(x, tuple) else spec(x.shape) for x in inputs]
    inputs = [x[0] if isinstance(x, tuple) else x for x in inputs]
    specs += [pl.BlockSpec(memory_space=pl.ANY)] * len(after)
    arrays = tuple(inputs) + tuple(after)
    if offs is not None:
        specs = [pl.BlockSpec(memory_space=pltpu.SMEM)] + specs
        arrays = (offs,) + arrays
    return pl.pallas_call(
        body,
        name=name,
        grid=(GROUPS // TOGETHER,),
        in_specs=specs,
        out_specs=[spec(shape) for shape, _ in outs],
        out_shape=[jax.ShapeDtypeStruct(shape, dtype) for shape, dtype in outs],
        scratch_shapes=list(scratch),
        cost_estimate=pl.CostEstimate(flops=4 * 10**9, bytes_accessed=16 * 10**6, transcendentals=10**6),
        compiler_params=pltpu.CompilerParams(vmem_limit_bytes=GRID_LIMIT),
    )(*arrays)


def routes(count):
    def along_z(i, step):
        z = ((i & 1) * 2 + (i >> 2 & 1) + step) % 4
        return (i & ~5) | (z & 1) << 2 | z >> 1

    table = {
        "head": lambda i: i ^ 1,
        "near": lambda i: along_z(i, 1 if i & 4 else -1),
        "core": lambda i: i ^ 2,
        "up": lambda i: along_z(i, 1),
        "down": lambda i: along_z(i, -1),
        "x1": lambda i: i ^ 8,
        "x2": lambda i: i ^ 16,
        "x3": lambda i: i ^ 24,
    }
    return {name: [(i, to(i)) for i in range(count)] for name, to in table.items()}


def shards(count, queries, key_rows, value_rows, gradient, level_offsets):
    route = routes(count)

    def send(x, name):
        return lax.ppermute(x, AXES, route[name])

    other_offsets = send(level_offsets, "near")
    low = lax.axis_index("head") == 0
    offs = jnp.where(
        low,
        jnp.concatenate([level_offsets, other_offsets], 1),
        jnp.concatenate([other_offsets, level_offsets], 1),
    )
    pair = jnp.concatenate([key_rows, value_rows], 1)
    far_keys = send(key_rows, "head")
    far_values = send(value_rows, "head")

    rows = lambda n, dtype=BF: ((GROUPS, n, 2 * D), dtype)
    extras = lambda dtype: ((GROUPS // 2, 80, 2 * D), dtype)
    wide = lambda dtype: ((TOKENS, GROUPS * WIDE), dtype)
    first, middle, tail, last = grid_call(
        select_kernel, "select", offs, [(pair, 1), (pair, 1 + GROUPS // TOGETHER)],
        [rows(64), rows(64), rows(32), rows(16)],
    )
    lift, extra = whole_call(
        compact_kernel, "compact", [rows(96), extras(BF)], None,
        middle, send(last, "x2"), send(tail, "x1"), send(last, "x3"),
    )
    lift_down = send(lift, "up")
    lift_up = send(lift, "down")
    extra_far = send(extra, "head")
    tall = lambda n, dtype=F32: ((GROUPS, n, D), dtype)
    kv = [key_rows, value_rows, far_keys, far_values]
    qs, gs, power0, peak0, lse0, out0 = grid_call(
        early_kernel, "early", offs, [queries, gradient, *kv],
        [tall(512, BF), tall(512, BF), rows(512), tall(128), tall(128), tall(512)], after=(extra,),
    )
    (across,) = whole_call(
        across_kernel, "across", [rows(128)], offs, far_keys, far_values, after=(lse0,)
    )
    first_sent, lift_sent, _ = lax.optimization_barrier((first, lift, (far_keys, far_values)))
    other_first, other_lift = send(first_sent, "core"), send(lift_sent, "core")
    (late,) = whole_call(
        assemble_kernel, "assemble", [rows(352)], None, across, extra_far, lift_up, lift_down,
        after=(other_first, other_lift),
    )
    other_late = send(late, "core")
    near = [first, lift, late, other_first, other_lift, other_late]
    stats = pltpu.VMEM((TOGETHER, TOKENS, 128), F32)
    attended, part, down_own, down_other, factor0, shift0, power1, factor1, shift1 = grid_call(
        attention_kernel, "attention", offs,
        [qs, gs, gradient, *near, peak0, lse0, out0],
        [wide(BF), tall(224), rows(384), rows(384), tall(128), tall(128), rows(256), tall(64), tall(64)],
        scratch=[pltpu.VMEM((TOGETHER, 4, TOKENS, 128), F32), stats, stats],
    )
    theirs = send(down_other, "core")
    placed, mine1, theirs1 = grid_call(
        return1_kernel, "return1", offs, [qs, gs, first, (late, 0), other_first, (other_late, 0), power1, factor1, shift1, part],
        [wide(F32), rows(128), rows(128)],
    )
    mid_kept, mid_far, up, down, x_far, x_kept = whole_call(
        reduce_kernel, "reduce", [rows(64), rows(64), rows(96), rows(96), extras(BF), extras(F32)],
        None, down_own, theirs, after=(mine1,),
    )
    from_down = send(up, "up")
    from_up = send(down, "down")
    x_far = send(x_far, "head")
    theirs1 = send(theirs1, "core")
    grad_queries, d0 = grid_call(
        return0_kernel, "return0", None, [queries, gradient, *kv, power0, factor0, shift0, placed],
        [wide(BF), rows(256)], after=(theirs1,),
    )
    half = ((TOGETHER, TOKENS, 2 * D), BF)
    fars = whole_call(
        place_kernel, "place", [rows(128)], offs, d0, mine1, theirs1, mid_far, after=(x_far,)
    )
    fars = [send(far, "head") for far in fars]
    one, two, three = whole_call(
        cross_kernel, "cross", [rows(32), rows(16), rows(16)], None, x_kept, x_far, from_down, from_up
    )
    one, two, three = send(one, "x1"), send(two, "x2"), send(three, "x3")
    out = ((TOKENS, GROUPS * D), BF)
    (kept,) = whole_call(
        keep_kernel, "keep", [rows(128, F32)], offs, d0, mine1, theirs1, mid_kept, from_down, from_up,
        one, two, three,
    )
    grad_keys, grad_values = whole_call(finish_kernel, "finish", [out, out], None, kept, *fars)
    return (attended, grad_queries, grad_keys, grad_values)


def solution(mesh):
    rows = P(AXES, None)
    return jax.shard_map(
        functools.partial(shards, mesh.size),
        mesh=mesh,
        in_specs=(rows, rows, rows, rows, P(None, "head")),
        out_specs=(rows, rows, rows, rows),
        check_vma=False,
    )
```
